256 devices in a mesh: ax: 4 (over y), az: 64 (over x, z, core).
Axes of the slice: x: 4, y: 4, z: 8, core: 2. Of those that a mesh axis runs over, the one named last changes fastest.
Arguments:
- fraction: float32 [2048, 32, 512], P('az', 'ax'), may hold values from 0 to 1
- courant_axial: float32 [2048, 32, 512], P('az', 'ax'), may hold values from -0.45 to 0.45
- courant_azimuth: float32 [2048, 32, 512], P('az', 'ax'), may hold values from -0.45 to 0.45
- courant_radial: float32 [2048, 32, 512], P('az', 'ax'), may hold values from -0.45 to 0.45
- plane_code: int32 [2048, 512], P('az', 'ax'), may hold values from 0 to 4095
- strip_width: float32 [2048, 512], P('az', 'ax'), may hold values from 0.25 to 0.75
- tile_reader: int32 [2048, 32], P('az', 'ax'), may hold values from 0 to 63, as said below
- landing_column: int32 [2048, 32], P('az', 'ax'), may hold values from 0 to 31
Outputs:
- fraction_new: float32 [2048, 32, 512], P('az', 'ax')
The draws below stay inside these ranges and needn't reach their ends.
Inputs may be any that keep to these rules, and one draw needn't show every extreme that they name: `tile_reader`: among the 32 x 8 rows (column, plane) of one device's block at most 8 name the same reader, and in every such block exactly 8 name some reader.
All inputs are finite; a program needn't handle non-finite values.
Results may differ from the reference program's by a relative error of at most 0.000057.
Values sent between devices are 32-bit elements; how exact they have to be, the bound alone decides.
No kernel may reach another device: no remote copies, remote signals or barrier semaphores. Data moves between devices by JAX's collectives and lax.ppermute only.
A program may use at most 64 MiB of HBM per device.

```python
import math
import jax
import jax.numpy as jnp

NR = 512
NTH = 2048
Z_DEV = 8
R_AX = 64
XR = 16
SECTOR = 32
NZ = 32
CAP = 8


def draw_tile_reader(key, part):
    row_count = SECTOR * Z_DEV
    readers = NTH // SECTOR
    axial_blocks = NZ // Z_DEV
    slot_count = readers * CAP

    def one_block(block_key):
        score_key, label_key = jax.random.split(block_key)
        slot_index = jnp.arange(slot_count).astype(jnp.int32)
        score = jax.random.randint(score_key, (slot_count,), 0, 65536).astype(jnp.int32) * slot_count + slot_index
        score = jnp.where(slot_index < CAP, slot_index - CAP, score)
        chosen = jnp.argsort(score, stable=True)[:row_count].astype(jnp.int32)
        relabel = jax.random.permutation(label_key, readers).astype(jnp.int32)
        return relabel[chosen // CAP]
    block_keys = jax.random.split(jax.random.fold_in(key, 17), readers * axial_blocks)
    blocks = jax.vmap(one_block)(block_keys)
    arranged = blocks.reshape(readers, axial_blocks, SECTOR, Z_DEV).transpose(0, 2, 1, 3)
    return arranged.reshape(NTH, NZ).astype(jnp.int32)


def with_ends(entries, stream_key, least, top_value):
    dims = entries.shape
    place = [jax.random.randint(jax.random.fold_in(stream_key, axis), (), 0, dims[axis]) for axis in range(len(dims))]
    entries = entries.at[tuple(place)].set(least)
    longest = dims.index(max(dims))
    place[longest] = (place[longest] + 1) % dims[longest]
    return entries.at[tuple(place)].set(top_value)


def block_levels(stream_key, shape, pieces, low, top_value):
    level, own = 1.0, jax.random.fold_in(stream_key, 6)
    for position, parts in pieces:
        heights = jnp.exp(jax.random.uniform(jax.random.fold_in(own, position), (parts,), jnp.float32, low / len(pieces), top_value / len(pieces)))
        level = level * jnp.repeat(heights, shape[position] // parts).reshape([-1 if axis == position else 1 for axis in range(len(shape))])
    return level


def setup_inputs(seed: int = 0) -> dict:
    seeds = jax.random.split(jax.random.key(seed), 9)
    fraction = jnp.clip(1.0 * jax.random.uniform(seeds[0], (NTH, NZ, NR), jnp.float32) ** block_levels(seeds[0], (NTH, NZ, NR), ((0, 64), (1, 4)), -0.2, 0.2), 0.0, 1.0)
    courant_axial = jnp.clip(jax.random.uniform(seeds[1], (NTH, NZ, NR), jnp.float32, -0.45, 0.45) * block_levels(seeds[1], (NTH, NZ, NR), ((0, 64), (1, 4)), -0.4, 0.0), -0.45, 0.45)
    courant_azimuth = jnp.clip(jax.random.uniform(seeds[2], (NTH, NZ, NR), jnp.float32, -0.45, 0.45) * block_levels(seeds[2], (NTH, NZ, NR), ((0, 64), (1, 4)), -0.4, 0.0), -0.45, 0.45)
    courant_radial = jnp.clip(jax.random.uniform(seeds[3], (NTH, NZ, NR), jnp.float32, -0.45, 0.45) * block_levels(seeds[3], (NTH, NZ, NR), ((0, 64), (1, 4)), -0.4, 0.0), -0.45, 0.45)
    plane_code = with_ends(jax.random.randint(seeds[4], (NTH, NZ * XR), 0, 4096), jax.random.fold_in(seeds[4], 1), 0, 4095).astype(jnp.int32)
    strip_width = jnp.clip(0.25 + 0.5 * jax.random.uniform(seeds[5], (NTH, NZ * XR), jnp.float32) ** block_levels(seeds[5], (NTH, NZ * XR), ((0, 64), (1, 4)), -0.2, 0.2), 0.25, 0.75)
    tile_reader = draw_tile_reader(jax.random.fold_in(seeds[8], 71), 0)
    landing_column = with_ends(jax.random.randint(seeds[7], (NTH, NZ), 0, SECTOR), jax.random.fold_in(seeds[7], 1), 0, SECTOR - 1).astype(jnp.int32)
    return dict(fraction=fraction, courant_axial=courant_axial, courant_azimuth=courant_azimuth, courant_radial=courant_radial, plane_code=plane_code, strip_width=strip_width, tile_reader=tile_reader, landing_column=landing_column)


def upwind(courant, below_cell, above_cell):
    return jnp.maximum(courant, 0.0) * below_cell + jnp.minimum(courant, 0.0) * above_cell


def periodic_sweep(values, courant, sweep_axis):
    face_flux = upwind(courant, values, jnp.roll(values, -1, sweep_axis))
    return values - (face_flux - jnp.roll(face_flux, 1, sweep_axis))


def radial_sweep(values, courant):
    above_cell = jnp.concatenate([values[:, :, 1:], jnp.zeros_like(values[:, :, :1])], axis=2)
    face_flux = upwind(courant, values, above_cell)
    radius = jnp.arange(values.shape[2]).astype(jnp.float32)
    outer_flux = (radius + 1.0) * face_flux
    inner_flux = jnp.concatenate([jnp.zeros_like(outer_flux[:, :, :1]), outer_flux[:, :, :-1]], axis=2)
    return values - (outer_flux - inner_flux) / (radius + 0.5)


def cycle_filter(swept_field):
    near_cycles = swept_field[:, :, :R_AX]
    spectrum = jnp.fft.rfft(near_cycles, axis=0)
    mode_index = jnp.arange(NTH // 2 + 1).astype(jnp.float32)[:, None, None]
    cycle_index = jnp.arange(R_AX).astype(jnp.float32)[None, None, :]
    cutoff = (cycle_index + 1.0) * (NTH / 1024.0)
    damped = spectrum * jnp.exp(-(mode_index / cutoff) ** 2)
    restored = jnp.fft.irfft(damped, n=NTH, axis=0).astype(jnp.float32)
    return jnp.concatenate([restored, swept_field[:, :, R_AX:]], axis=2)


def plic_volume(plane_code, strip_width):
    normal = (plane_code // 64).astype(jnp.float32)
    offset = (plane_code % 64).astype(jnp.float32)
    plane_angle = math.pi / 16 + (normal + 0.5) * (3 * math.pi / 512)
    normal_along = jnp.cos(plane_angle)
    across = jnp.sin(plane_angle)
    plane_level = (offset + 0.5) * (normal_along + across) / 64.0
    strip_span = strip_width * normal_along

    def square(shift_value):
        return jnp.maximum(shift_value, 0.0) ** 2

    strip_area = (square(plane_level) - square(plane_level - strip_span) - square(plane_level - across)
                  + square(plane_level - strip_span - across)) / (2.0 * strip_span * across)
    return strip_width * strip_area


def reference(fraction, courant_axial, courant_azimuth, courant_radial, plane_code, strip_width, tile_reader, landing_column):
    swept_field = periodic_sweep(fraction, courant_axial, 1)
    swept_field = periodic_sweep(swept_field, courant_azimuth, 0)
    swept_field = radial_sweep(swept_field, courant_radial)
    swept_field = periodic_sweep(swept_field, courant_azimuth, 0)
    swept_field = periodic_sweep(swept_field, courant_axial, 1)
    filtered = cycle_filter(swept_field)
    volume = plic_volume(plane_code, strip_width)
    volume_rows = volume.reshape(NTH * NZ, XR)
    plane_index = jnp.arange(NZ).astype(jnp.int32)
    target = ((tile_reader * SECTOR + landing_column) * NZ + plane_index[None, :]).reshape(-1).astype(jnp.int32)
    arrived = jax.ops.segment_sum(volume_rows, target, num_segments=NTH * NZ).reshape(NTH, NZ * XR)
    inner_cycles = filtered[:, :, :XR].reshape(NTH, NZ * XR) - volume + arrived
    return jnp.concatenate([inner_cycles.reshape(NTH, NZ, XR), filtered[:, :, XR:]], axis=2)
```

```python
import functools
import math

import jax
import jax.numpy as jnp
import ml_dtypes
import numpy as np
from jax import lax
from jax.experimental import pallas as pl
from jax.experimental.pallas import tpu as pltpu
from jax.sharding import PartitionSpec as P

R_AX = 64
XR = 16
COLS = 32
PLANES = 8
ROWS = COLS * PLANES
NR = 512
SLOTS = 8
KD = 40

F32 = jnp.float32
BF16 = jnp.bfloat16

BELOW = ((0, -2), (0, -1), (1, -2), (1, -1), (2, -1), (3, -1))
ABOVE = ((0, 8), (0, 9), (1, 8), (2, 8), (3, 8))
LEFT = ((0, -2), (0, -1), (1, -2), (1, -1), (2, -2), (2, -1), (3, -1))
RIGHT = ((0, 32), (0, 33), (1, 32), (1, 33), (2, 32), (3, 32))
HALO_PLANES = ((-2, -1, 8, 9), (-2, -1, 8), (-1, 8), (-1, 8))


def corner_list(columns):
    return [(f, c, p) for f, c in columns for p in HALO_PLANES[f]]


LEFT_ROWS = 80
RIGHT_ROWS = 72


def plane_slot(plane):
    return plane % 16 - 8


def pack_planes(f, ca, ct, cr, up, down):
    fields = (f, ca, ct, cr)
    for k, (field, plane) in enumerate(BELOW):
        up[k * COLS : (k + 1) * COLS, :] = fields[field][pl.ds(plane + PLANES, COLS, stride=PLANES), :]
    for k, (field, plane) in enumerate(ABOVE):
        down[k * COLS : (k + 1) * COLS, :] = fields[field][pl.ds(plane - PLANES, COLS, stride=PLANES), :]


def pack_columns(f0, c0, t0, r0, f1, c1, t1, r1, below, above, right, left):
    low = (f0, c0, t0, r0)
    high = (f1, c1, t1, r1)

    def corner(field, column, plane):
        if plane < 0:
            return below, BELOW.index((field, plane)) * COLS + column
        return above, ABOVE.index((field, plane)) * COLS + column

    for k, (field, column) in enumerate(LEFT):
        right[k * 8 : k * 8 + 8, :] = high[field][(column + 2) * 8 : (column + 2) * 8 + 8, :]
    for k, (field, column, plane) in enumerate(corner_list(LEFT)):
        source, row = corner(field, column + COLS, plane)
        at = len(LEFT) * 8 + k
        right[at : at + 1, :] = source[row : row + 1, :]
    for k, (field, column) in enumerate(RIGHT):
        left[k * 8 : k * 8 + 8, :] = low[field][(column - 32) * 8 : (column - 32) * 8 + 8, :]
    for k, (field, column, plane) in enumerate(corner_list(RIGHT)):
        source, row = corner(field, column - COLS, plane)
        at = len(RIGHT) * 8 + k
        left[at : at + 1, :] = source[row : row + 1, :]


def upwind(courant, below_cell, above_cell):
    return courant * jnp.where(courant > 0.0, below_cell, above_cell)


def sweep(fields, below, above, left, right, halos, store, lanes, unrolled):
    for tile in range(lanes // 128):
        at_lanes = pl.ds(tile * 128, 128)
        for planes, source in ((BELOW, below), (ABOVE, above)):
            for k, (field, plane) in enumerate(planes):
                at_rows = pl.ds(16 + plane_slot(plane), COLS, stride=8)
                halos[field].at[tile][at_rows, :] = source[k * COLS : (k + 1) * COLS, at_lanes]
        for columns, source in ((LEFT, left), (RIGHT, right)):
            for k, (field, column, plane) in enumerate(corner_list(columns)):
                at = (column + 2) * 8 + plane_slot(plane)
                row = len(columns) * 8 + k
                halos[field].at[tile][at : at + 1, :] = source[row : row + 1, at_lanes]

    plane = lax.broadcasted_iota(jnp.int32, (8, lanes), 0)
    cycle = lax.broadcasted_iota(jnp.int32, (8, lanes), 1)
    first, last = plane == 0, plane == 7
    radius = cycle.astype(F32)
    outer_radius = radius + 1.0
    inverse = 1.0 / (radius + 0.5)
    axis_cell, rim_cell = cycle == 0, cycle == NR - 1

    def load(field, column):
        if isinstance(column, int) and (column, field) in [(c, f) for f, c in LEFT]:
            at = LEFT.index((field, column)) * 8
            own = left[at : at + 8, :]
        elif isinstance(column, int) and (column, field) in [(c, f) for f, c in RIGHT]:
            at = RIGHT.index((field, column)) * 8
            own = right[at : at + 8, :]
        elif isinstance(column, int):
            own = fields[field][column * 8 : column * 8 + 8, :]
        else:
            own = fields[field][pl.ds(pl.multiple_of(column * 8, 8), 8), :]
        if isinstance(column, int):
            at_rows = pl.ds((column + 2) * 8, 8)
        else:
            at_rows = pl.ds(pl.multiple_of(column * 8 + 16, 8), 8)
        tiles = [halos[field].at[tile][at_rows, :] for tile in range(lanes // 128)]
        return own, jnp.concatenate(tiles, axis=1) if len(tiles) > 1 else tiles[0]

    def next_plane(pair):
        own, halo = (pltpu.roll(a, 7, 0) for a in pair)
        return jnp.where(last, halo, own), jnp.where(last, own, halo)

    def previous_plane(pair):
        own, halo = (pltpu.roll(a, 1, 0) for a in pair)
        return jnp.where(first, halo, own), jnp.where(first, own, halo)

    def flux(courant, low, high):
        return tuple(upwind(c, a, b) for c, a, b in zip(courant, low, high))

    def update(values, upper, lower):
        return tuple(v - (a - b) for v, a, b in zip(values, upper, lower))

    def axial(values, courant):
        face = flux(courant, values, next_plane(values))
        return update(values, face, previous_plane(face))

    def axial_own(values, courant):
        own, halo = flux(courant, values, next_plane(values))
        lower = jnp.where(first, pltpu.roll(halo, 1, 0), pltpu.roll(own, 1, 0))
        return values[0] - (own - lower)

    def radial_one(values, courant):
        above_cell = jnp.where(rim_cell, 0.0, pltpu.roll(values, lanes - 1, 1))
        outer = outer_radius * upwind(courant, values, above_cell)
        inner = jnp.where(axis_cell, 0.0, pltpu.roll(outer, 1, 1))
        return values - (outer - inner) * inverse

    def radial(values, courant):
        return tuple(radial_one(v, c) for v, c in zip(values, courant))

    def step(column, state, stage):
        v1_old, face_a_old, v3_old, face_b_old = state
        v1 = axial(load(0, column), load(1, column)) if stage < 6 else None
        face_a = v3 = face_b = None
        if stage >= 1:
            face_a = flux(load(2, column - 1), v1_old, v1)
        if stage >= 2:
            v2 = update(v1_old, face_a, face_a_old)
            v3 = radial(v2, load(3, column - 1))
        if stage >= 3:
            face_b = flux(load(2, column - 2), v3_old, v3)
        if stage >= 4:
            v4 = update(v3_old, face_b, face_b_old)
            store(column - 2, axial_own(v4, load(1, column - 2)))
        return v1, face_a, v3, face_b

    state = (None, None, None, None)
    for stage, column in enumerate(range(-2, 4)):
        state = step(column, state, stage if stage < 4 else 4)
    if unrolled:
        for column in range(4, 32):
            state = step(column, state, 4)
    else:
        state = lax.fori_loop(4, 32, lambda column, s: step(column, s, 4), state)
    for column in (32, 33):
        state = step(column, state, 4)


def near_kernel(f, ca, ct, cr, below, above, left, right, crossing, out, h0, h1, h2, h3, swept):
    def store(column, values):
        swept[column * 8 : column * 8 + 8, :] = values

    sweep((f, ca, ct, cr), below, above, left, right, (h0, h1, h2, h3), store, 128, True)
    turned = swept[...].T
    out[pl.ds(0, R_AX, stride=4), :] = turned[:R_AX, :128]
    out[pl.ds(1, R_AX, stride=4), :] = turned[:R_AX, 128:]
    out[pl.ds(2, R_AX, stride=4), :] = crossing[:R_AX, :]
    out[pl.ds(3, R_AX, stride=4), :] = crossing[R_AX:, :]


def far_kernel(f, ca, ct, cr, below, above, left, right, out, h0, h1, h2, h3):
    def store(column, values):
        if isinstance(column, int):
            out[column * 8 : column * 8 + 8, :] = values
        else:
            out[pl.ds(pl.multiple_of(column * 8, 8), 8), :] = values

    sweep((f, ca, ct, cr), below, above, left, right, (h0, h1, h2, h3), store, NR, False)


def pieces(values, count):
    out = []
    for _ in range(count):
        piece = values.astype(BF16)
        out.append(piece)
        values = values - piece.astype(F32)
    return out


def mm(a, b, dims=((1,), (0,))):
    return lax.dot_general(a, b, (dims, ((), ())), preferred_element_type=F32)


def plic_volume(plane_code, strip_width):
    normal = lax.shift_right_logical(plane_code, 6).astype(F32)
    offset = lax.bitwise_and(plane_code, 63).astype(F32)
    plane_angle = math.pi / 16 + (normal + 0.5) * (3 * math.pi / 512)
    normal_along = jnp.cos(plane_angle)
    across = jnp.sin(plane_angle)
    plane_level = (offset + 0.5) * (normal_along + across) / 64.0
    strip_span = strip_width * normal_along

    def square(shift_value):
        positive = jnp.maximum(shift_value, 0.0)
        return positive * positive

    strip_area = (
        square(plane_level)
        - square(plane_level - strip_span)
        - square(plane_level - across)
        + square(plane_level - strip_span - across)
    ) / (2.0 * strip_span * across)
    return strip_width * strip_area


def crossing_kernel(code, width, reader, landing, out, volume_out):
    iota = functools.partial(lax.broadcasted_iota, jnp.int32)
    volume = plic_volume(code[...], width[...])
    both = jnp.concatenate([reader[...].astype(F32), landing[...].astype(F32)], axis=0).astype(BF16)
    column_of_row = (iota((ROWS, COLS), 0) // 8 == iota((ROWS, COLS), 1)).astype(F32).astype(BF16)
    spread = mm(column_of_row, both, ((1,), (1,)))
    row16, lane16 = iota((ROWS, 16), 0), iota((ROWS, 16), 1)
    reader_rows = jnp.sum(jnp.where(lane16 == row16 % 8, spread, 0.0), axis=1, keepdims=True)
    landing_rows = jnp.sum(jnp.where(lane16 == row16 % 8 + 8, spread, 0.0), axis=1, keepdims=True)
    across = mm(both, column_of_row, ((1,), (1,)))
    reader_lanes = jnp.sum(
        jnp.where(iota((16, ROWS), 0) == iota((16, ROWS), 1) % 8, across, 0.0), axis=0, keepdims=True
    )
    same = (reader_rows == reader_lanes) & (iota((ROWS, ROWS), 1) < iota((ROWS, ROWS), 0))
    rank = jnp.sum(jnp.where(same, 1.0, 0.0), axis=1, keepdims=True)

    row, lane = iota((ROWS, 128), 0), iota((ROWS, 128), 1)
    wide = jnp.broadcast_to(volume[:, None, :], (COLS, PLANES, 128)).reshape(ROWS, 128)
    own = jnp.where(lane // 16 == row % 8, wide, 0.0)
    repeat = (iota((128, 128), 0) % 16 == iota((128, 128), 1) % 16).astype(F32).astype(BF16)
    rows_of_volume = sum(mm(piece, repeat) for piece in pieces(own, 3))
    volume_out[...] = rows_of_volume.T[:XR, :]
    chosen = (reader_lanes == iota((R_AX, ROWS), 0).astype(F32)).astype(F32).astype(BF16)
    slotted = jnp.where((lane // 16).astype(F32) == rank, rows_of_volume, 0.0)
    out[:R_AX, :] = sum(mm(chosen, piece) for piece in pieces(slotted, 3))
    target = landing_rows * 8.0 + (row % 8).astype(F32) + 1.0
    marked = jnp.where(lane.astype(F32) == rank, target, 0.0)
    out[R_AX:, :] = mm(chosen, marked.astype(BF16))


def arrival_kernel(received, volume, out):
    values = received[pl.ds(2, R_AX, stride=4), :]
    targets = received[pl.ds(3, R_AX, stride=4), :]
    turned = values.T
    row = lax.broadcasted_iota(jnp.int32, (R_AX, ROWS), 1).astype(F32) + 1.0
    total = -volume[...]
    for slot in range(SLOTS):
        chosen = (targets[:, slot : slot + 1] == row).astype(F32).astype(BF16)
        for piece in pieces(turned[slot * XR : (slot + 1) * XR, :], 3):
            total += mm(piece, chosen)
    out[...] = total


def halves(table):
    high = table.astype(ml_dtypes.bfloat16)
    low = (table - high.astype(np.float64)).astype(ml_dtypes.bfloat16)
    return high, low


def filter_tables():
    outer, sector = np.arange(33)[:, None], np.arange(64)[None, :]
    phase = 2 * np.pi * (outer * sector % 64) / 64
    first = np.zeros((2 * KD, 64))
    first[:33], first[KD : KD + 33] = np.cos(phase), -np.sin(phase)
    weight = np.where((outer == 0) | (outer == 32), 1.0, 2.0) / 2048
    last = np.zeros((64, 2 * KD))
    last[:, :33], last[:, KD : KD + 33] = (weight * np.cos(phase)).T, (-weight * np.sin(phase)).T
    column, plane = np.arange(ROWS) // PLANES, np.arange(ROWS) % PLANES
    inner = 2 * np.pi * (column[:, None] * column[None, :] % 32) / 32
    same = plane[:, None] == plane[None, :]
    block = np.concatenate([np.where(same, np.cos(inner), 0.0), np.where(same, -np.sin(inner), 0.0)], axis=1)
    turn = 2 * np.pi * np.arange(KD)[:, None] * column[None, :] / 2048
    twiddle = np.concatenate([np.cos(turn), -np.sin(turn)], axis=0).astype(np.float32)
    return (*halves(first), *halves(block), twiddle, *halves(last))


def dot3(a, b):
    (ah, al), (bh, bl) = a, b
    return mm(ah, bh) + (mm(al, bh) + mm(ah, bl))


def filter_kernel(received, first_h, first_l, block_h, block_l, twiddle, last_h, last_l, out):
    sectors = jnp.concatenate(
        [received[pl.ds(0, R_AX, stride=4), :], received[pl.ds(1, R_AX, stride=4), :]], axis=1
    )
    outer = dot3((first_h[...], first_l[...]), pieces(sectors, 2))
    re, im = outer[:KD], outer[KD:]
    t_re, t_im = twiddle[:KD, :], twiddle[KD:, :]
    turned = jnp.concatenate([re * t_re - im * t_im, re * t_im + im * t_re], axis=0)
    block = (block_h[...], block_l[...])
    inner = dot3(pieces(turned, 2), block)
    re = inner[:KD, :ROWS] - inner[KD:, ROWS:]
    im = inner[:KD, ROWS:] + inner[KD:, :ROWS]
    mode = lax.broadcasted_iota(jnp.int32, (KD, ROWS), 0) + 64 * (
        lax.broadcasted_iota(jnp.int32, (KD, ROWS), 1) // PLANES
    )
    folded = jnp.minimum(mode, 2048 - mode).astype(F32)
    cutoff = (lax.axis_index("az") + 1).astype(F32) * 2.0
    scaled = folded / cutoff
    damped = jnp.exp(-(scaled * scaled))
    back = dot3(pieces(jnp.concatenate([re * damped, im * damped], axis=0), 2), block)
    re = back[:KD, :ROWS] + back[KD:, ROWS:]
    im = back[KD:, :ROWS] - back[:KD, ROWS:]
    turned = jnp.concatenate([re * t_re + im * t_im, im * t_re - re * t_im], axis=0)
    result = dot3((last_h[...], last_l[...]), pieces(turned, 2))
    out[pl.ds(0, R_AX, stride=2), :] = result[:, :128]
    out[pl.ds(1, R_AX, stride=2), :] = result[:, 128:]


def final_kernel(received, delta, swept, out):
    near = jnp.concatenate(
        [received[pl.ds(0, R_AX, stride=2), :], received[pl.ds(1, R_AX, stride=2), :]], axis=1
    )
    near = jnp.concatenate([near[:XR] + delta[...], near[XR:], jnp.zeros((R_AX, ROWS), F32)], axis=0)
    cycle = lax.broadcasted_iota(jnp.int32, (ROWS, 128), 1)
    out[...] = jnp.where(cycle < R_AX, near.T, swept[...])


def block(rows, lanes, row=0):
    return pl.BlockSpec((rows, lanes), lambda i: (row, 0))


def lane_tile(rows):
    return pl.BlockSpec((rows, 128), lambda i: (0, i))


def call(kernel, inputs, specs, out_shapes, out_specs, scratch=(), cost=1.0, steps=1, **options):
    return pl.pallas_call(
        kernel,
        grid=(steps,),
        in_specs=list(specs),
        out_specs=out_specs,
        out_shape=out_shapes,
        scratch_shapes=list(scratch),
        cost_estimate=pl.CostEstimate(flops=int(cost * 1e6), bytes_accessed=int(cost * 3e6), transcendentals=0),
        compiler_params=pltpu.CompilerParams(vmem_limit_bytes=32 * 1024 * 1024),
        **options,
    )(*inputs)


def shape(*dims):
    return jax.ShapeDtypeStruct(dims, F32)


def local(
    fraction,
    courant_axial,
    courant_azimuth,
    courant_radial,
    plane_code,
    strip_width,
    tile_reader,
    landing_column,
):
    ax_count, az_count = lax.axis_size("ax"), lax.axis_size("az")
    fields = [a.reshape(ROWS, NR) for a in (fraction, courant_axial, courant_azimuth, courant_radial)]
    n_below, n_above = len(BELOW) * COLS, len(ABOVE) * COLS

    up, down = call(
        pack_planes,
        fields,
        [lane_tile(ROWS)] * 4,
        (shape(n_below, NR), shape(n_above, NR)),
        (lane_tile(n_below), lane_tile(n_above)),
        steps=NR // 128,
    )
    below = lax.ppermute(up, "ax", [(i, (i + 1) % ax_count) for i in range(ax_count)])
    above = lax.ppermute(down, "ax", [((i + 1) % ax_count, i) for i in range(ax_count)])

    crossing, volume = call(
        crossing_kernel,
        (plane_code, strip_width, tile_reader.T, landing_column.T),
        [block(COLS, 128), block(COLS, 128), block(PLANES, COLS), block(PLANES, COLS)],
        (shape(2 * R_AX, 128), shape(XR, ROWS)),
        (block(2 * R_AX, 128), block(XR, ROWS)),
    )

    to_right, to_left = call(
        pack_columns,
        (*fields, *fields, below, above),
        [block(16, NR)] * 4 + [block(16, NR, 15)] * 4 + [block(n_below, NR), block(n_above, NR)],
        (shape(LEFT_ROWS, NR), shape(RIGHT_ROWS, NR)),
        (block(LEFT_ROWS, NR), block(RIGHT_ROWS, NR)),
    )
    left = lax.ppermute(to_right, "az", [(i, (i + 1) % az_count) for i in range(az_count)])
    right = lax.ppermute(to_left, "az", [((i + 1) % az_count, i) for i in range(az_count)])

    parts = (*fields, below, above, left, right)

    def part_specs(lanes):
        return [block(ROWS, lanes)] * 4 + [block(a.shape[0], lanes) for a in (below, above, left, right)]

    def halo_scratch(lanes):
        return [pltpu.VMEM((lanes // 128, (COLS + 4) * 8, 128), F32)] * 4

    send = call(
        near_kernel,
        (*parts, crossing),
        part_specs(128) + [block(2 * R_AX, 128)],
        shape(4 * R_AX, 128),
        block(4 * R_AX, 128),
        halo_scratch(128) + [pltpu.VMEM((ROWS, 128), F32)],
    )
    got = lax.all_to_all(send.reshape(R_AX, 4, 128), "az", 0, 0, tiled=True).reshape(4 * R_AX, 128)
    swept = call(far_kernel, parts, part_specs(NR), shape(ROWS, NR), block(ROWS, NR), halo_scratch(NR), cost=4.0)

    tables = filter_tables()
    back = call(
        filter_kernel,
        (got, *tables),
        [block(4 * R_AX, 128)] + [block(*t.shape) for t in tables],
        shape(2 * R_AX, 128),
        block(2 * R_AX, 128),
    )
    returned = lax.all_to_all(back.reshape(R_AX, 2, 128), "az", 0, 0, tiled=True).reshape(2 * R_AX, 128)
    delta = call(
        arrival_kernel,
        (got, volume),
        [block(4 * R_AX, 128), block(XR, ROWS)],
        shape(XR, ROWS),
        block(XR, ROWS),
    )
    out = call(
        final_kernel,
        (returned, delta, swept),
        [block(2 * R_AX, 128), block(XR, ROWS), block(ROWS, 128)],
        shape(ROWS, NR),
        block(ROWS, 128),
        input_output_aliases={2: 0},
    )
    return out.reshape(COLS, PLANES, NR)


def solution(mesh):
    return jax.shard_map(
        local,
        mesh=mesh,
        in_specs=(
            P("az", "ax", None),
            P("az", "ax", None),
            P("az", "ax", None),
            P("az", "ax", None),
            P("az", "ax"),
            P("az", "ax"),
            P("az", "ax"),
            P("az", "ax"),
        ),
        out_specs=P("az", "ax", None),
        check_vma=False,
    )
```

```python
import functools
import math

import jax
import jax.numpy as jnp
import ml_dtypes
import numpy as np
from jax import lax
from jax.experimental import pallas as pl
from jax.experimental.pallas import tpu as pltpu
from jax.sharding import PartitionSpec as P

R_AX = 64
XR = 16
COLS = 32
PLANES = 8
ROWS = COLS * PLANES
NR = 512
SLOTS = 8
KD = 40

F32 = jnp.float32
BF16 = jnp.bfloat16

BELOW = ((0, -2), (0, -1), (1, -2), (1, -1), (2, -1), (3, -1))
ABOVE = ((0, 8), (0, 9), (1, 8), (2, 8), (3, 8))
HALO_PLANES = ((-2, -1, 8, 9), (-2, -1, 8), (-1, 8), (-1, 8))

NEAR_LEFT = tuple((f, c) for f in range(3) for c in range(-4, 0)) + tuple((3, c) for c in range(-3, 0))
NEAR_CORNERS = tuple((f, c, p) for f, c in NEAR_LEFT for p in HALO_PLANES[f])
NEAR_ROWS = 8 * len(NEAR_LEFT) + 48
LEFT = ((0, -2), (0, -1), (1, -2), (1, -1), (2, -2), (2, -1), (3, -1))
RIGHT = ((0, 32), (0, 33), (1, 32), (1, 33), (2, 32), (3, 32))
TILES = NR // 128


def far_layout(planes):
    entries, row = [], 0
    for tile in range(TILES):
        for field, plane in planes:
            left = sum(f == field for f, _ in LEFT)
            right = sum(f == field for f, _ in RIGHT)
            if tile:
                runs = ((-left, left + COLS + right),)
            else:
                runs = ((-left, left), (COLS, right))
            for column, count in runs:
                entries.append((tile, field, plane, column, count, row))
                row += count
    return entries, -(-row // 8) * 8


FAR_BELOW, FAR_BELOW_ROWS = far_layout(BELOW)
FAR_ABOVE, FAR_ABOVE_ROWS = far_layout(ABOVE)


def plane_slot(plane):
    return plane % 16 - 8


def pack_first(*refs):
    near, low, high, (up, down, right, left) = refs[:4], refs[4:8], refs[8:12], refs[12:]
    for k, (field, plane) in enumerate(BELOW):
        up[k * COLS : (k + 1) * COLS, :] = near[field][pl.ds(plane + PLANES, COLS, stride=PLANES), :]
    for k, (field, plane) in enumerate(ABOVE):
        down[k * COLS : (k + 1) * COLS, :] = near[field][pl.ds(plane - PLANES, COLS, stride=PLANES), :]
    for k, (field, column) in enumerate(LEFT):
        right[k * 8 : k * 8 + 8, :] = high[field][(column + 2) * 8 : (column + 3) * 8, :]
    for k, (field, column) in enumerate(RIGHT):
        left[k * 8 : k * 8 + 8, :] = low[field][(column - COLS) * 8 : (column - COLS + 1) * 8, :]


def pack_near_columns(*refs):
    high, (below, above, right) = refs[:4], refs[4:]
    for k, (field, column) in enumerate(NEAR_LEFT):
        right[k * 8 : k * 8 + 8, :] = high[field][(column + 4) * 8 : (column + 5) * 8, :]
    right[len(NEAR_LEFT) * 8 :, :] = jnp.zeros((48, 128), F32)
    for k, (field, column, plane) in enumerate(NEAR_CORNERS):
        planes, source = (BELOW, below) if plane < 0 else (ABOVE, above)
        row = planes.index((field, plane)) * COLS + column + COLS
        at = len(NEAR_LEFT) * 8 + k
        right[at : at + 1, :] = source[row : row + 1, :]


def pack_far_planes(*refs):
    own, (left, right, up, down) = refs[: 4 * (TILES - 1)], refs[4 * (TILES - 1) :]
    for entries, out, shift in ((FAR_BELOW, up, PLANES), (FAR_ABOVE, down, -PLANES)):
        for tile, field, plane, column, count, row in entries:
            lanes = pl.ds(tile * 128, 128)
            for at in range(count):
                for columns, source in ((LEFT, left), (RIGHT, right)):
                    if (field, column + at) in columns:
                        origin = columns.index((field, column + at)) * 8 + plane + shift
                        out[row + at : row + at + 1, :] = source[origin : origin + 1, lanes]
            if tile:
                source = own[field * (TILES - 1) + tile - 1]
                out[row - column : row - column + COLS, :] = source[pl.ds(plane + shift, COLS, stride=PLANES), :]


def upwind(courant, below_cell, above_cell):
    return courant * jnp.where(courant > 0.0, below_cell, above_cell)


def sweep(lowest, load_own, load_halo, store, lanes, unrolled):
    plane = lax.broadcasted_iota(jnp.int32, (8, lanes), 0)
    cycle = lax.broadcasted_iota(jnp.int32, (8, lanes), 1)
    first, last = plane == 0, plane == 7
    radius = cycle.astype(F32)
    outer_radius = radius + 1.0
    inverse = 1.0 / (radius + 0.5)
    axis_cell, rim_cell = cycle == 0, cycle == NR - 1

    def load(field, column):
        return load_own(field, column), load_halo(field, column)

    def next_plane(pair):
        own, halo = (pltpu.roll(a, 7, 0) for a in pair)
        return jnp.where(last, halo, own), jnp.where(last, own, halo)

    def previous_plane(pair):
        own, halo = (pltpu.roll(a, 1, 0) for a in pair)
        return jnp.where(first, halo, own), jnp.where(first, own, halo)

    def flux(courant, low, high):
        return tuple(upwind(c, a, b) for c, a, b in zip(courant, low, high))

    def update(values, upper, lower):
        return tuple(v - (a - b) for v, a, b in zip(values, upper, lower))

    def axial(values, courant):
        face = flux(courant, values, next_plane(values))
        return update(values, face, previous_plane(face))

    def axial_own(values, courant):
        own, halo = flux(courant, values, next_plane(values))
        lower = jnp.where(first, pltpu.roll(halo, 1, 0), pltpu.roll(own, 1, 0))
        return values[0] - (own - lower)

    def radial_one(values, courant):
        above_cell = jnp.where(rim_cell, 0.0, pltpu.roll(values, lanes - 1, 1))
        outer = outer_radius * upwind(courant, values, above_cell)
        inner = jnp.where(axis_cell, 0.0, pltpu.roll(outer, 1, 1))
        return values - (outer - inner) * inverse

    def radial(values, courant):
        return tuple(radial_one(v, c) for v, c in zip(values, courant))

    def step(column, state, stage):
        v1_old, face_a_old, v3_old, face_b_old = state
        v1 = axial(load(0, column), load(1, column))
        face_a = v3 = face_b = None
        if stage >= 1:
            face_a = flux(load(2, column - 1), v1_old, v1)
        if stage >= 2:
            v2 = update(v1_old, face_a, face_a_old)
            v3 = radial(v2, load(3, column - 1))
        if stage >= 3:
            face_b = flux(load(2, column - 2), v3_old, v3)
        if stage >= 4:
            v4 = update(v3_old, face_b, face_b_old)
            store(column - 2, axial_own(v4, load(1, column - 2)))
        return v1, face_a, v3, face_b

    state = (None, None, None, None)
    for stage in range(6):
        state = step(lowest + stage, state, stage)
    if unrolled:
        for stage in range(6, 34):
            state = step(lowest + stage, state, stage)
    else:
        state = lax.fori_loop(lowest + 6, lowest + 34, lambda column, s: step(column, s, 6), state, unroll=4)
    for stage in (34, 35):
        state = step(lowest + stage, state, stage)


def near_kernel(*refs):
    fields, (below, above, left, crossing, out), halos, swept = refs[:4], refs[4:9], refs[9:13], refs[13]
    lowest = -4
    for planes, source in ((BELOW, below), (ABOVE, above)):
        for k, (field, plane) in enumerate(planes):
            rows = pl.ds(-lowest * 8 + plane_slot(plane), COLS, stride=8)
            halos[field][rows, :] = source[k * COLS : (k + 1) * COLS, :]
    for k, (field, column, plane) in enumerate(NEAR_CORNERS):
        at = (column - lowest) * 8 + plane_slot(plane)
        row = len(NEAR_LEFT) * 8 + k
        halos[field][at : at + 1, :] = left[row : row + 1, :]

    def load_own(field, column):
        if column < 0:
            at = NEAR_LEFT.index((field, column)) * 8
            return left[at : at + 8, :]
        return fields[field][column * 8 : column * 8 + 8, :]

    def load_halo(field, column):
        return halos[field][(column - lowest) * 8 : (column - lowest + 1) * 8, :]

    def store(column, values):
        swept[(column + 2) * 8 : (column + 3) * 8, :] = values

    sweep(lowest, load_own, load_halo, store, 128, True)
    turned = swept[...].T
    out[pl.ds(0, R_AX, stride=4), :] = turned[:R_AX, :128]
    out[pl.ds(1, R_AX, stride=4), :] = turned[:R_AX, 128:]
    out[pl.ds(2, R_AX, stride=4), :] = crossing[:R_AX, :]
    out[pl.ds(3, R_AX, stride=4), :] = crossing[R_AX:, :]


def far_kernel(*refs):
    fields, (near_below, near_above, below, above, left, right, out, first_tile) = refs[:4], refs[4:12]
    halos = refs[12:]
    lowest = -2
    for planes, near, entries, far in ((BELOW, near_below, FAR_BELOW, below), (ABOVE, near_above, FAR_ABOVE, above)):
        for k, (field, plane) in enumerate(planes):
            rows = pl.ds(-lowest * 8 + plane_slot(plane), COLS, stride=8)
            halos[field].at[0][rows, :] = near[k * COLS : (k + 1) * COLS, :]
        for tile, field, plane, column, count, row in entries:
            rows = pl.ds((column - lowest) * 8 + plane_slot(plane), count, stride=8)
            halos[field].at[tile][rows, :] = far[row : row + count, :]

    def load_own(field, column):
        if not isinstance(column, int):
            return fields[field][pl.ds(pl.multiple_of(column * 8, 8), 8), :]
        for columns, source in ((LEFT, left), (RIGHT, right)):
            if (field, column) in columns:
                at = columns.index((field, column)) * 8
                return source[at : at + 8, :]
        return fields[field][column * 8 : column * 8 + 8, :]

    def load_halo(field, column):
        at = (column - lowest) * 8
        rows = pl.ds(at if isinstance(at, int) else pl.multiple_of(at, 8), 8)
        return jnp.concatenate([halos[field].at[tile][rows, :] for tile in range(TILES)], axis=1)

    def store(column, values):
        rows = pl.ds(column * 8 if isinstance(column, int) else pl.multiple_of(column * 8, 8), 8)
        out[rows, :] = values
        first_tile[rows, :] = values[:, :128]

    sweep(lowest, load_own, load_halo, store, NR, False)


def pieces(values, count):
    out = []
    for _ in range(count):
        piece = values.astype(BF16)
        out.append(piece)
        values = values - piece.astype(F32)
    return out


def mm(a, b, dims=((1,), (0,))):
    return lax.dot_general(a, b, (dims, ((), ())), preferred_element_type=F32)


def plic_volume(plane_code, strip_width):
    normal = lax.shift_right_logical(plane_code, 6).astype(F32)
    offset = lax.bitwise_and(plane_code, 63).astype(F32)
    plane_angle = math.pi / 16 + (normal + 0.5) * (3 * math.pi / 512)
    normal_along = jnp.cos(plane_angle)
    across = jnp.sin(plane_angle)
    plane_level = (offset + 0.5) * (normal_along + across) / 64.0
    strip_span = strip_width * normal_along

    def square(shift_value):
        positive = jnp.maximum(shift_value, 0.0)
        return positive * positive

    strip_area = (
        square(plane_level)
        - square(plane_level - strip_span)
        - square(plane_level - across)
        + square(plane_level - strip_span - across)
    ) / (2.0 * strip_span * across)
    return strip_width * strip_area


def crossing_kernel(code, width, reader, landing, out, volume_out):
    iota = functools.partial(lax.broadcasted_iota, jnp.int32)
    volume = plic_volume(code[...], width[...])
    both = jnp.concatenate([reader[...].astype(F32), landing[...].astype(F32)], axis=0).astype(BF16)
    column_of_row = (iota((ROWS, COLS), 0) // 8 == iota((ROWS, COLS), 1)).astype(F32).astype(BF16)
    spread = mm(column_of_row, both, ((1,), (1,)))
    row16, lane16 = iota((ROWS, 16), 0), iota((ROWS, 16), 1)
    reader_rows = jnp.sum(jnp.where(lane16 == row16 % 8, spread, 0.0), axis=1, keepdims=True)
    landing_rows = jnp.sum(jnp.where(lane16 == row16 % 8 + 8, spread, 0.0), axis=1, keepdims=True)
    across = mm(both, column_of_row, ((1,), (1,)))
    reader_lanes = jnp.sum(
        jnp.where(iota((16, ROWS), 0) == iota((16, ROWS), 1) % 8, across, 0.0), axis=0, keepdims=True
    )
    same = (reader_rows == reader_lanes) & (iota((ROWS, ROWS), 1) < iota((ROWS, ROWS), 0))
    rank = jnp.sum(jnp.where(same, 1.0, 0.0), axis=1, keepdims=True)

    row, lane = iota((ROWS, 128), 0), iota((ROWS, 128), 1)
    wide = jnp.broadcast_to(volume[:, None, :], (COLS, PLANES, 128)).reshape(ROWS, 128)
    own = jnp.where(lane // 16 == row % 8, wide, 0.0)
    repeat = (iota((128, 128), 0) % 16 == iota((128, 128), 1) % 16).astype(F32).astype(BF16)
    rows_of_volume = sum(mm(piece, repeat) for piece in pieces(own, 3))
    volume_out[...] = rows_of_volume.T[:XR, :]
    chosen = (reader_lanes == iota((R_AX, ROWS), 0).astype(F32)).astype(F32).astype(BF16)
    slotted = jnp.where((lane // 16).astype(F32) == rank, rows_of_volume, 0.0)
    out[:R_AX, :] = sum(mm(chosen, piece) for piece in pieces(slotted, 3))
    target = landing_rows * 8.0 + (row % 8).astype(F32) + 1.0
    marked = jnp.where(lane.astype(F32) == rank, target, 0.0)
    out[R_AX:, :] = mm(chosen, marked.astype(BF16))


def arrival_kernel(received, volume, out):
    values = received[pl.ds(2, R_AX, stride=4), :]
    targets = received[pl.ds(3, R_AX, stride=4), :]
    turned = values.T
    row = lax.broadcasted_iota(jnp.int32, (R_AX, ROWS), 1).astype(F32) + 1.0
    total = -volume[...]
    for slot in range(SLOTS):
        chosen = (targets[:, slot : slot + 1] == row).astype(F32).astype(BF16)
        for piece in pieces(turned[slot * XR : (slot + 1) * XR, :], 3):
            total += mm(piece, chosen)
    out[...] = total


def halves(table):
    high = table.astype(ml_dtypes.bfloat16)
    low = (table - high.astype(np.float64)).astype(ml_dtypes.bfloat16)
    return high, low


def filter_tables():
    outer, sector = np.arange(33)[:, None], np.arange(64)[None, :]
    phase = 2 * np.pi * (outer * sector % 64) / 64
    first = np.zeros((2 * KD, 64))
    first[:33], first[KD : KD + 33] = np.cos(phase), -np.sin(phase)
    weight = np.where((outer == 0) | (outer == 32), 1.0, 2.0) / 2048
    last = np.zeros((64, 2 * KD))
    last[:, :33], last[:, KD : KD + 33] = (weight * np.cos(phase)).T, (-weight * np.sin(phase)).T
    column, plane = np.arange(ROWS) // PLANES, np.arange(ROWS) % PLANES
    inner = 2 * np.pi * (column[:, None] * column[None, :] % 32) / 32
    same = plane[:, None] == plane[None, :]
    block = np.concatenate([np.where(same, np.cos(inner), 0.0), np.where(same, -np.sin(inner), 0.0)], axis=1)
    turn = 2 * np.pi * np.arange(KD)[:, None] * column[None, :] / 2048
    mode = np.arange(KD)[:, None] + 64 * column[None, :]
    shift = 2 * np.pi * (2 * mode % 2048) / 2048
    turns = [np.cos(turn), -np.sin(turn), np.cos(shift), np.sin(shift)]
    twiddle = np.concatenate(turns, axis=0).astype(np.float32)
    return (*halves(first), *halves(block), twiddle, *halves(last))


def dot3(a, b):
    (ah, al), (bh, bl) = a, b
    return mm(ah, bh) + (mm(al, bh) + mm(ah, bl))


def filter_kernel(received, first_h, first_l, block_h, block_l, twiddle, last_h, last_l, out):
    sectors = jnp.concatenate(
        [received[pl.ds(0, R_AX, stride=4), :], received[pl.ds(1, R_AX, stride=4), :]], axis=1
    )
    outer = dot3((first_h[...], first_l[...]), pieces(sectors, 2))
    re, im = outer[:KD], outer[KD:]
    t_re, t_im, s_re, s_im = (twiddle[k * KD : (k + 1) * KD, :] for k in range(4))
    turned = jnp.concatenate([re * t_re - im * t_im, re * t_im + im * t_re], axis=0)
    block = (block_h[...], block_l[...])
    inner = dot3(pieces(turned, 2), block)
    re = inner[:KD, :ROWS] - inner[KD:, ROWS:]
    im = inner[:KD, ROWS:] + inner[KD:, :ROWS]
    re, im = re * s_re - im * s_im, re * s_im + im * s_re
    mode = lax.broadcasted_iota(jnp.int32, (KD, ROWS), 0) + 64 * (
        lax.broadcasted_iota(jnp.int32, (KD, ROWS), 1) // PLANES
    )
    folded = jnp.minimum(mode, 2048 - mode).astype(F32)
    cutoff = (lax.axis_index("az") + 1).astype(F32) * 2.0
    scaled = folded / cutoff
    damped = jnp.exp(-(scaled * scaled))
    back = dot3(pieces(jnp.concatenate([re * damped, im * damped], axis=0), 2), block)
    re = back[:KD, :ROWS] + back[KD:, ROWS:]
    im = back[KD:, :ROWS] - back[:KD, ROWS:]
    turned = jnp.concatenate([re * t_re + im * t_im, im * t_re - re * t_im], axis=0)
    result = dot3((last_h[...], last_l[...]), pieces(turned, 2))
    out[pl.ds(0, R_AX, stride=2), :] = result[:, :128]
    out[pl.ds(1, R_AX, stride=2), :] = result[:, 128:]


def final_kernel(received, delta, swept, _, out):
    near = jnp.concatenate(
        [received[pl.ds(0, R_AX, stride=2), :], received[pl.ds(1, R_AX, stride=2), :]], axis=1
    )
    near = jnp.concatenate([near[:XR] + delta[...], near[XR:], jnp.zeros((R_AX, ROWS), F32)], axis=0)
    cycle = lax.broadcasted_iota(jnp.int32, (ROWS, 128), 1)
    out[...] = jnp.where(cycle < R_AX, near.T, swept[...])


def block(rows, lanes, row=0, lane=0):
    return pl.BlockSpec((rows, lanes), lambda i: (row, lane))


def whole(array):
    return block(*array.shape)


def call(kernel, inputs, specs, out_shapes, out_specs=None, scratch=(), cost=1.0, vmem=32, **options):
    if out_specs is None:
        out_specs = jax.tree.map(whole, out_shapes)
    return pl.pallas_call(
        kernel,
        grid=(1,),
        in_specs=list(specs),
        out_specs=out_specs,
        out_shape=out_shapes,
        scratch_shapes=list(scratch),
        cost_estimate=pl.CostEstimate(flops=int(cost * 1e6), bytes_accessed=int(cost * 3e6), transcendentals=0),
        compiler_params=pltpu.CompilerParams(vmem_limit_bytes=vmem * 1024 * 1024),
        **options,
    )(*inputs)


def shape(*dims):
    return jax.ShapeDtypeStruct(dims, F32)


def local(
    fraction,
    courant_axial,
    courant_azimuth,
    courant_radial,
    plane_code,
    strip_width,
    tile_reader,
    landing_column,
):
    ax_count, az_count = lax.axis_size("ax"), lax.axis_size("az")
    higher_ax, higher_az = ([(i, (i + 1) % n) for i in range(n)] for n in (ax_count, az_count))
    lower_ax, lower_az = ([(j, i) for i, j in pairs] for pairs in (higher_ax, higher_az))
    fields = [a.reshape(ROWS, NR) for a in (fraction, courant_axial, courant_azimuth, courant_radial)]

    near_up, near_down, far_right, far_left = call(
        pack_first,
        fields * 3,
        [block(ROWS, 128)] * 4 + [block(16, NR)] * 4 + [block(16, NR, 15)] * 4,
        (
            shape(len(BELOW) * COLS, 128),
            shape(len(ABOVE) * COLS, 128),
            shape(len(LEFT) * 8, NR),
            shape(len(RIGHT) * 8, NR),
        ),
        vmem=60,
    )
    near_below = lax.ppermute(near_up, "ax", higher_ax)
    near_above = lax.ppermute(near_down, "ax", lower_ax)
    left = lax.ppermute(far_right, "az", higher_az)
    right = lax.ppermute(far_left, "az", lower_az)

    crossing, volume = call(
        crossing_kernel,
        (plane_code, strip_width, tile_reader.T, landing_column.T),
        [block(COLS, 128), block(COLS, 128), block(PLANES, COLS), block(PLANES, COLS)],
        (shape(2 * R_AX, 128), shape(XR, ROWS)),
    )

    near_right = call(
        pack_near_columns,
        (*fields, near_below, near_above),
        [block(32, 128, 7)] * 4 + [whole(near_below), whole(near_above)],
        shape(NEAR_ROWS, 128),
    )
    near_left = lax.ppermute(near_right, "az", higher_az)

    far_up, far_down = call(
        pack_far_planes,
        (*(f for f in fields for _ in range(TILES - 1)), left, right),
        [block(ROWS, 128, 0, tile) for _ in fields for tile in range(1, TILES)] + [whole(left), whole(right)],
        (shape(FAR_BELOW_ROWS, 128), shape(FAR_ABOVE_ROWS, 128)),
    )
    far_below = lax.ppermute(far_up, "ax", higher_ax)
    far_above = lax.ppermute(far_down, "ax", lower_ax)

    send = call(
        near_kernel,
        (*fields, near_below, near_above, near_left, crossing),
        [block(ROWS, 128)] * 4 + [whole(a) for a in (near_below, near_above, near_left, crossing)],
        shape(4 * R_AX, 128),
        scratch=[pltpu.VMEM((36 * 8, 128), F32)] * 4 + [pltpu.VMEM((ROWS, 128), F32)],
    )
    got = lax.all_to_all(send.reshape(R_AX, 4, 128), "az", 0, 0, tiled=True).reshape(4 * R_AX, 128)

    halos = (near_below, near_above, far_below, far_above, left, right)
    swept, first_tile = call(
        far_kernel,
        (*fields, *halos),
        [whole(a) for a in (*fields, *halos)],
        (shape(ROWS, NR), shape(ROWS, 128)),
        scratch=[pltpu.VMEM((TILES, 36 * 8, 128), F32)] * 4,
        cost=4.0,
    )

    tables = filter_tables()
    back = call(filter_kernel, (got, *tables), [whole(a) for a in (got, *tables)], shape(2 * R_AX, 128))
    returned = lax.all_to_all(back.reshape(R_AX, 2, 128), "az", 0, 0, tiled=True).reshape(2 * R_AX, 128)
    delta = call(arrival_kernel, (got, volume), [whole(got), whole(volume)], shape(XR, ROWS))
    out = call(
        final_kernel,
        (returned, delta, first_tile, swept),
        [whole(returned), whole(delta), whole(first_tile), pl.BlockSpec(memory_space=pl.ANY)],
        shape(ROWS, NR),
        block(ROWS, 128),
        input_output_aliases={3: 0},
    )
    return out.reshape(COLS, PLANES, NR)


def solution(mesh):
    return jax.shard_map(
        local,
        mesh=mesh,
        in_specs=(
            P("az", "ax", None),
            P("az", "ax", None),
            P("az", "ax", None),
            P("az", "ax", None),
            P("az", "ax"),
            P("az", "ax"),
            P("az", "ax"),
            P("az", "ax"),
        ),
        out_specs=P("az", "ax", None),
        check_vma=False,
    )
```

```python
import functools
import math

import jax
import jax.numpy as jnp
import ml_dtypes
import numpy as np
from jax import lax
from jax.experimental import pallas as pl
from jax.experimental.pallas import tpu as pltpu
from jax.sharding import PartitionSpec as P

R_AX = 64
XR = 16
COLS = 32
PLANES = 8
ROWS = COLS * PLANES
NR = 512
SLOTS = 8
KD = 40

F32 = jnp.float32
BF16 = jnp.bfloat16

BELOW = ((0, -2), (0, -1), (1, -2), (1, -1), (2, -1), (3, -1))
ABOVE = ((0, 8), (0, 9), (1, 8), (2, 8), (3, 8))
HALO_PLANES = ((-2, -1, 8, 9), (-2, -1, 8), (-1, 8), (-1, 8))

NEAR_LEFT = tuple((f, c) for f in range(3) for c in range(-4, 0)) + tuple((3, c) for c in range(-3, 0))
NEAR_CORNERS = tuple((f, c, p) for f, c in NEAR_LEFT for p in HALO_PLANES[f])
NEAR_ROWS = 8 * len(NEAR_LEFT) + 48
LEFT = ((0, -2), (0, -1), (1, -2), (1, -1), (2, -2), (2, -1), (3, -1))
RIGHT = ((0, 32), (0, 33), (1, 32), (1, 33), (2, 32), (3, 32))
TILES = NR // 128


def far_layout(planes):
    entries, row = [], 0
    for tile in range(TILES):
        for field, plane in planes:
            left = sum(f == field for f, _ in LEFT)
            right = sum(f == field for f, _ in RIGHT)
            if tile:
                runs = ((-left, left + COLS + right),)
            else:
                runs = ((-left, left), (COLS, right))
            for column, count in runs:
                entries.append((tile, field, plane, column, count, row))
                row += count
    return entries, -(-row // 8) * 8


FAR_BELOW, FAR_BELOW_ROWS = far_layout(BELOW)
FAR_ABOVE, FAR_ABOVE_ROWS = far_layout(ABOVE)


def plane_slot(plane):
    return plane % 16 - 8


def copy_all(pairs, semaphores, first=0):
    copies = [pltpu.make_async_copy(a, b, semaphores.at[first + k]) for k, (a, b) in enumerate(pairs)]
    for copy in copies:
        copy.start()
    return copies


def copy_out(source, target, semaphore):
    copy = pltpu.make_async_copy(source, target, semaphore)
    copy.start()
    copy.wait()


def pack_first(*refs):
    fields, tiles, (up, down, semaphores) = refs[:4], refs[4:8], refs[8:]
    copies = copy_all([(f.at[:, pl.ds(0, 128)], tile) for f, tile in zip(fields, tiles)], semaphores)
    for field, copy in enumerate(copies):
        copy.wait()
        for planes, out, shift in ((BELOW, up, PLANES), (ABOVE, down, -PLANES)):
            for k, (of, plane) in enumerate(planes):
                if of == field:
                    out[k * COLS : (k + 1) * COLS, :] = tiles[field][pl.ds(plane + shift, COLS, stride=PLANES), :]


def pack_near_columns(*refs):
    tiles, (below, above, right) = refs[:4], refs[4:]
    for k, (field, column) in enumerate(NEAR_LEFT):
        right[k * 8 : k * 8 + 8, :] = tiles[field][(column + COLS) * 8 : (column + COLS + 1) * 8, :]
    right[len(NEAR_LEFT) * 8 :, :] = jnp.zeros((48, 128), F32)
    for k, (field, column, plane) in enumerate(NEAR_CORNERS):
        planes, source = (BELOW, below) if plane < 0 else (ABOVE, above)
        row = planes.index((field, plane)) * COLS + column + COLS
        at = len(NEAR_LEFT) * 8 + k
        right[at : at + 1, :] = source[row : row + 1, :]


def pack_far_columns(*refs):
    fields, (_, right, left, semaphores) = refs[:4], refs[4:]
    pairs = []
    for columns, out, shift in ((LEFT, right, COLS), (RIGHT, left, -COLS)):
        for field in range(4):
            at = [k for k, (f, _) in enumerate(columns) if f == field]
            source = fields[field].at[pl.ds((columns[at[0]][1] + shift) * 8, len(at) * 8), :]
            pairs.append((source, out.at[pl.ds(at[0] * 8, len(at) * 8), :]))
    for copy in copy_all(pairs, semaphores):
        copy.wait()


def pack_far_planes(*refs):
    tiles, (left, right, up, down) = refs[:4], refs[4:]
    for entries, out, shift in ((FAR_BELOW, up, PLANES), (FAR_ABOVE, down, -PLANES)):
        for tile, field, plane, column, count, row in entries:
            lanes = pl.ds(tile * 128, 128)
            for at in range(count):
                for columns, source in ((LEFT, left), (RIGHT, right)):
                    if (field, column + at) in columns:
                        origin = columns.index((field, column + at)) * 8 + plane + shift
                        out[row + at : row + at + 1, :] = source[origin : origin + 1, lanes]
            if tile:
                rows = pl.ds((tile - 1) * ROWS + plane + shift, COLS, stride=PLANES)
                out[row - column : row - column + COLS, :] = tiles[field][rows, :]
        used = sum(e[4] for e in entries)
        if used < out.shape[0]:
            out[used:, :] = jnp.zeros((out.shape[0] - used, 128), F32)


def upwind(courant, below_cell, above_cell):
    return courant * jnp.where(courant > 0.0, below_cell, above_cell)


def sweep(lowest, load_own, load_halo, store, lanes, unrolled):
    plane = lax.broadcasted_iota(jnp.int32, (8, lanes), 0)
    cycle = lax.broadcasted_iota(jnp.int32, (8, lanes), 1)
    first, last = plane == 0, plane == 7
    radius = cycle.astype(F32)
    outer_radius = radius + 1.0
    inverse = 1.0 / (radius + 0.5)
    axis_cell, rim_cell = cycle == 0, cycle == NR - 1

    def load(field, column):
        return load_own(field, column), load_halo(field, column)

    def next_plane(pair):
        own, halo = (pltpu.roll(a, 7, 0) for a in pair)
        return jnp.where(last, halo, own), jnp.where(last, own, halo)

    def previous_plane(pair):
        own, halo = (pltpu.roll(a, 1, 0) for a in pair)
        return jnp.where(first, halo, own), jnp.where(first, own, halo)

    def flux(courant, low, high):
        return tuple(upwind(c, a, b) for c, a, b in zip(courant, low, high))

    def update(values, upper, lower):
        return tuple(v - (a - b) for v, a, b in zip(values, upper, lower))

    def axial(values, courant):
        face = flux(courant, values, next_plane(values))
        return update(values, face, previous_plane(face))

    def axial_own(values, courant):
        own, halo = flux(courant, values, next_plane(values))
        lower = jnp.where(first, pltpu.roll(halo, 1, 0), pltpu.roll(own, 1, 0))
        return values[0] - (own - lower)

    def radial_one(values, courant):
        above_cell = jnp.where(rim_cell, 0.0, pltpu.roll(values, lanes - 1, 1))
        outer = outer_radius * upwind(courant, values, above_cell)
        inner = jnp.where(axis_cell, 0.0, pltpu.roll(outer, 1, 1))
        return values - (outer - inner) * inverse

    def radial(values, courant):
        return tuple(radial_one(v, c) for v, c in zip(values, courant))

    def step(column, state, stage):
        v1_old, face_a_old, v3_old, face_b_old = state
        v1 = axial(load(0, column), load(1, column))
        face_a = v3 = face_b = None
        if stage >= 1:
            face_a = flux(load(2, column - 1), v1_old, v1)
        if stage >= 2:
            v2 = update(v1_old, face_a, face_a_old)
            v3 = radial(v2, load(3, column - 1))
        if stage >= 3:
            face_b = flux(load(2, column - 2), v3_old, v3)
        if stage >= 4:
            v4 = update(v3_old, face_b, face_b_old)
            store(column - 2, axial_own(v4, load(1, column - 2)))
        return v1, face_a, v3, face_b

    state = (None, None, None, None)
    for stage in range(6):
        state = step(lowest + stage, state, stage)
    if unrolled:
        for stage in range(6, 34):
            state = step(lowest + stage, state, stage)
    else:
        state = lax.fori_loop(lowest + 6, lowest + 34, lambda column, s: step(column, s, 6), state, unroll=4)
    for stage in (34, 35):
        state = step(lowest + stage, state, stage)


def near_kernel(*refs):
    fields, (below, above, left, crossing, send) = refs[:4], refs[4:9]
    halos, (swept, out, semaphore) = refs[9:13], refs[13:]
    lowest = -4
    for planes, source in ((BELOW, below), (ABOVE, above)):
        for k, (field, plane) in enumerate(planes):
            rows = pl.ds(-lowest * 8 + plane_slot(plane), COLS, stride=8)
            halos[field][rows, :] = source[k * COLS : (k + 1) * COLS, :]
    for k, (field, column, plane) in enumerate(NEAR_CORNERS):
        at = (column - lowest) * 8 + plane_slot(plane)
        row = len(NEAR_LEFT) * 8 + k
        halos[field][at : at + 1, :] = left[row : row + 1, :]

    def load_own(field, column):
        if column < 0:
            at = NEAR_LEFT.index((field, column)) * 8
            return left[at : at + 8, :]
        return fields[field][column * 8 : column * 8 + 8, :]

    def load_halo(field, column):
        return halos[field][(column - lowest) * 8 : (column - lowest + 1) * 8, :]

    def store(column, values):
        swept[(column + 2) * 8 : (column + 3) * 8, :] = values

    sweep(lowest, load_own, load_halo, store, 128, True)
    turned = swept[...].T
    out[pl.ds(0, R_AX, stride=4), :] = turned[:R_AX, :128]
    out[pl.ds(1, R_AX, stride=4), :] = turned[:R_AX, 128:]
    out[pl.ds(2, R_AX, stride=4), :] = crossing[:R_AX, :]
    out[pl.ds(3, R_AX, stride=4), :] = crossing[R_AX:, :]
    copy_out(out, send, semaphore)


def far_kernel(*refs):
    near_tiles, tiles, (near_below, near_above, below, above, left, right) = refs[:4], refs[4:8], refs[8:14]
    result, first_tile, *halos, out, semaphore = refs[14:]
    lowest = -2
    for planes, near, entries, far in ((BELOW, near_below, FAR_BELOW, below), (ABOVE, near_above, FAR_ABOVE, above)):
        for k, (field, plane) in enumerate(planes):
            rows = pl.ds(-lowest * 8 + plane_slot(plane), COLS, stride=8)
            halos[field].at[0][rows, :] = near[k * COLS : (k + 1) * COLS, :]
        for tile, field, plane, column, count, row in entries:
            rows = pl.ds((column - lowest) * 8 + plane_slot(plane), count, stride=8)
            halos[field].at[tile][rows, :] = far[row : row + count, :]

    def load_own(field, column):
        for columns, source in ((LEFT, left), (RIGHT, right)):
            if isinstance(column, int) and (field, column) in columns:
                at = columns.index((field, column)) * 8
                return source[at : at + 8, :]
        at = column * 8 if isinstance(column, int) else pl.multiple_of(column * 8, 8)
        parts = [near_tiles[field][pl.ds(at, 8), :]]
        parts += [tiles[field][pl.ds(tile * ROWS + at, 8), :] for tile in range(TILES - 1)]
        return jnp.concatenate(parts, axis=1)

    def load_halo(field, column):
        at = (column - lowest) * 8
        rows = pl.ds(at if isinstance(at, int) else pl.multiple_of(at, 8), 8)
        return jnp.concatenate([halos[field].at[tile][rows, :] for tile in range(TILES)], axis=1)

    def store(column, values):
        rows = pl.ds(column * 8 if isinstance(column, int) else pl.multiple_of(column * 8, 8), 8)
        out[rows, :] = values
        first_tile[rows, :] = values[:, :128]

    sweep(lowest, load_own, load_halo, store, NR, False)
    copy_out(out, result, semaphore)


def pieces(values, count):
    out = []
    for _ in range(count):
        piece = values.astype(BF16)
        out.append(piece)
        values = values - piece.astype(F32)
    return out


def mm(a, b, dims=((1,), (0,))):
    return lax.dot_general(a, b, (dims, ((), ())), preferred_element_type=F32)


def plic_volume(plane_code, strip_width):
    normal = lax.shift_right_logical(plane_code, 6).astype(F32)
    offset = lax.bitwise_and(plane_code, 63).astype(F32)
    plane_angle = math.pi / 16 + (normal + 0.5) * (3 * math.pi / 512)
    normal_along = jnp.cos(plane_angle)
    across = jnp.sin(plane_angle)
    plane_level = (offset + 0.5) * (normal_along + across) / 64.0
    strip_span = strip_width * normal_along

    def square(shift_value):
        positive = jnp.maximum(shift_value, 0.0)
        return positive * positive

    strip_area = (
        square(plane_level)
        - square(plane_level - strip_span)
        - square(plane_level - across)
        + square(plane_level - strip_span - across)
    ) / (2.0 * strip_span * across)
    return strip_width * strip_area


def crossing_kernel(*refs):
    (code, width, reader, landing), fields, tables = refs[:4], refs[4:8], refs[8:15]
    (out, volume_out), tiles, held, semaphores = refs[15:17], refs[17:21], refs[21:28], refs[28]
    pairs = list(zip(tables, held))
    for field, tile in zip(fields, tiles):
        for k in range(1, TILES):
            pairs.append((field.at[:, pl.ds(k * 128, 128)], tile.at[pl.ds((k - 1) * ROWS, ROWS), :]))
    copies = copy_all(pairs, semaphores)
    iota = functools.partial(lax.broadcasted_iota, jnp.int32)
    volume = plic_volume(code[...], width[...])
    both = jnp.concatenate([reader[...].astype(F32), landing[...].astype(F32)], axis=0).astype(BF16)
    column_of_row = (iota((ROWS, COLS), 0) // 8 == iota((ROWS, COLS), 1)).astype(F32).astype(BF16)
    spread = mm(column_of_row, both, ((1,), (1,)))
    row16, lane16 = iota((ROWS, 16), 0), iota((ROWS, 16), 1)
    reader_rows = jnp.sum(jnp.where(lane16 == row16 % 8, spread, 0.0), axis=1, keepdims=True)
    landing_rows = jnp.sum(jnp.where(lane16 == row16 % 8 + 8, spread, 0.0), axis=1, keepdims=True)
    across = mm(both, column_of_row, ((1,), (1,)))
    reader_lanes = jnp.sum(
        jnp.where(iota((16, ROWS), 0) == iota((16, ROWS), 1) % 8, across, 0.0), axis=0, keepdims=True
    )
    same = (reader_rows == reader_lanes) & (iota((ROWS, ROWS), 1) < iota((ROWS, ROWS), 0))
    rank = jnp.sum(jnp.where(same, 1.0, 0.0), axis=1, keepdims=True)

    row, lane = iota((ROWS, 128), 0), iota((ROWS, 128), 1)
    wide = jnp.broadcast_to(volume[:, None, :], (COLS, PLANES, 128)).reshape(ROWS, 128)
    own = jnp.where(lane // 16 == row % 8, wide, 0.0)
    repeat = (iota((128, 128), 0) % 16 == iota((128, 128), 1) % 16).astype(F32).astype(BF16)
    rows_of_volume = sum(mm(piece, repeat) for piece in pieces(own, 3))
    volume_out[...] = rows_of_volume.T[:XR, :]
    chosen = (reader_lanes == iota((R_AX, ROWS), 0).astype(F32)).astype(F32).astype(BF16)
    slotted = jnp.where((lane // 16).astype(F32) == rank, rows_of_volume, 0.0)
    out[:R_AX, :] = sum(mm(chosen, piece) for piece in pieces(slotted, 3))
    target = landing_rows * 8.0 + (row % 8).astype(F32) + 1.0
    marked = jnp.where(lane.astype(F32) == rank, target, 0.0)
    out[R_AX:, :] = mm(chosen, marked.astype(BF16))
    for copy in copies:
        copy.wait()


def arrival_kernel(received, volume, out):
    values = received[pl.ds(2, R_AX, stride=4), :]
    targets = received[pl.ds(3, R_AX, stride=4), :]
    turned = values.T
    row = lax.broadcasted_iota(jnp.int32, (R_AX, ROWS), 1).astype(F32) + 1.0
    total = -volume[...]
    for slot in range(SLOTS):
        chosen = (targets[:, slot : slot + 1] == row).astype(F32).astype(BF16)
        for piece in pieces(turned[slot * XR : (slot + 1) * XR, :], 3):
            total += mm(piece, chosen)
    out[...] = total


def halves(table):
    high = table.astype(ml_dtypes.bfloat16)
    low = (table - high.astype(np.float64)).astype(ml_dtypes.bfloat16)
    return high, low


def filter_tables():
    outer, sector = np.arange(33)[:, None], np.arange(64)[None, :]
    phase = 2 * np.pi * (outer * sector % 64) / 64
    first = np.zeros((2 * KD, 64))
    first[:33], first[KD : KD + 33] = np.cos(phase), -np.sin(phase)
    weight = np.where((outer == 0) | (outer == 32), 1.0, 2.0) / 2048
    last = np.zeros((64, 2 * KD))
    last[:, :33], last[:, KD : KD + 33] = (weight * np.cos(phase)).T, (-weight * np.sin(phase)).T
    column, plane = np.arange(ROWS) // PLANES, np.arange(ROWS) % PLANES
    inner = 2 * np.pi * (column[:, None] * column[None, :] % 32) / 32
    same = plane[:, None] == plane[None, :]
    block = np.concatenate([np.where(same, np.cos(inner), 0.0), np.where(same, -np.sin(inner), 0.0)], axis=1)
    turn = 2 * np.pi * np.arange(KD)[:, None] * column[None, :] / 2048
    mode = np.arange(KD)[:, None] + 64 * column[None, :]
    shift = 2 * np.pi * (2 * mode % 2048) / 2048
    turns = [np.cos(turn), -np.sin(turn), np.cos(shift), np.sin(shift)]
    twiddle = np.concatenate(turns, axis=0).astype(np.float32)
    return (*halves(first), *halves(block), twiddle, *halves(last))


def dot3(a, b):
    (ah, al), (bh, bl) = a, b
    return mm(ah, bh) + (mm(al, bh) + mm(ah, bl))


def filter_kernel(received, first_h, first_l, block_h, block_l, twiddle, last_h, last_l, send, out, semaphore):
    sectors = jnp.concatenate(
        [received[pl.ds(0, R_AX, stride=4), :], received[pl.ds(1, R_AX, stride=4), :]], axis=1
    )
    outer = dot3((first_h[...], first_l[...]), pieces(sectors, 2))
    re, im = outer[:KD], outer[KD:]
    t_re, t_im, s_re, s_im = (twiddle[k * KD : (k + 1) * KD, :] for k in range(4))
    turned = jnp.concatenate([re * t_re - im * t_im, re * t_im + im * t_re], axis=0)
    block = (block_h[...], block_l[...])
    inner = dot3(pieces(turned, 2), block)
    re = inner[:KD, :ROWS] - inner[KD:, ROWS:]
    im = inner[:KD, ROWS:] + inner[KD:, :ROWS]
    re, im = re * s_re - im * s_im, re * s_im + im * s_re
    mode = lax.broadcasted_iota(jnp.int32, (KD, ROWS), 0) + 64 * (
        lax.broadcasted_iota(jnp.int32, (KD, ROWS), 1) // PLANES
    )
    folded = jnp.minimum(mode, 2048 - mode).astype(F32)
    cutoff = (lax.axis_index("az") + 1).astype(F32) * 2.0
    scaled = folded / cutoff
    damped = jnp.exp(-(scaled * scaled))
    back = dot3(pieces(jnp.concatenate([re * damped, im * damped], axis=0), 2), block)
    re = back[:KD, :ROWS] + back[KD:, ROWS:]
    im = back[KD:, :ROWS] - back[:KD, ROWS:]
    turned = jnp.concatenate([re * t_re + im * t_im, im * t_re - re * t_im], axis=0)
    result = dot3((last_h[...], last_l[...]), pieces(turned, 2))
    out[pl.ds(0, R_AX, stride=2), :] = result[:, :128]
    out[pl.ds(1, R_AX, stride=2), :] = result[:, 128:]
    copy_out(out, send, semaphore)


def final_kernel(received, delta, swept, _, result, out, semaphore):
    near = jnp.concatenate(
        [received[pl.ds(0, R_AX, stride=2), :], received[pl.ds(1, R_AX, stride=2), :]], axis=1
    )
    near = jnp.concatenate([near[:XR] + delta[...], near[XR:], jnp.zeros((R_AX, ROWS), F32)], axis=0)
    cycle = lax.broadcasted_iota(jnp.int32, (ROWS, 128), 1)
    out[...] = jnp.where(cycle < R_AX, near.T, swept[...])
    copy_out(out, result.at[:, pl.ds(0, 128)], semaphore)


VMEM, HBM = pltpu.VMEM, pltpu.HBM
DMA = pltpu.SemaphoreType.DMA


def call(kernel, inputs, outputs, scratch=(), cost=1.0, aliases=None):
    arrays, specs = [], []
    for given in inputs:
        array, space = given if isinstance(given, tuple) else (given, VMEM)
        arrays.append(pltpu.with_memory_space_constraint(array, HBM) if space is HBM else array)
        specs.append(pl.BlockSpec(memory_space=space))
    out_specs = [pl.BlockSpec(memory_space=o.memory_space) for o in outputs]
    return pl.pallas_call(
        kernel,
        in_specs=specs,
        out_specs=out_specs,
        out_shape=list(outputs),
        scratch_shapes=list(scratch),
        input_output_aliases=aliases or {},
        cost_estimate=pl.CostEstimate(flops=int(cost * 1e6), bytes_accessed=int(cost * 3e6), transcendentals=0),
        compiler_params=pltpu.CompilerParams(vmem_limit_bytes=16 * 1024 * 1024),
    )(*arrays)


def local(
    fraction,
    courant_axial,
    courant_azimuth,
    courant_radial,
    plane_code,
    strip_width,
    tile_reader,
    landing_column,
):
    ax_count, az_count = lax.axis_size("ax"), lax.axis_size("az")
    higher_ax, higher_az = ([(i, (i + 1) % n) for i in range(n)] for n in (ax_count, az_count))
    lower_ax, lower_az = ([(j, i) for i, j in pairs] for pairs in (higher_ax, higher_az))
    fields = [(a.reshape(ROWS, NR), HBM) for a in (fraction, courant_axial, courant_azimuth, courant_radial)]

    *near_tiles, near_up, near_down = call(
        pack_first,
        fields,
        [VMEM((ROWS, 128), F32)] * 4 + [VMEM((len(BELOW) * COLS, 128), F32), VMEM((len(ABOVE) * COLS, 128), F32)],
        [DMA((4,))],
    )
    near_below = lax.ppermute(near_up, "ax", higher_ax)
    near_above = lax.ppermute(near_down, "ax", lower_ax)

    tables = filter_tables()
    results = call(
        crossing_kernel,
        [plane_code, strip_width, tile_reader.T, landing_column.T, *fields, *((t, HBM) for t in map(jnp.asarray, tables))],
        [VMEM((2 * R_AX, 128), F32), VMEM((XR, ROWS), F32)]
        + [VMEM(((TILES - 1) * ROWS, 128), F32)] * 4
        + [VMEM(t.shape, t.dtype) for t in tables],
        [DMA((len(tables) + 4 * (TILES - 1),))],
    )
    (crossing, volume), tiles, held_tables = results[:2], results[2:6], results[6:]

    (near_right,) = call(pack_near_columns, [*near_tiles, near_below, near_above], [VMEM((NEAR_ROWS, 128), F32)])
    near_left = lax.ppermute(near_right, "az", higher_az)
    (send,) = call(
        near_kernel,
        [*near_tiles, near_below, near_above, near_left, crossing],
        [HBM((4 * R_AX, 128), F32)],
        [VMEM((36 * 8, 128), F32)] * 4 + [VMEM((ROWS, 128), F32), VMEM((4 * R_AX, 128), F32), DMA],
    )
    got = lax.all_to_all(send.reshape(R_AX, 4, 128), "az", 0, 0, tiled=True).reshape(4 * R_AX, 128)

    far_right, far_left = call(
        pack_far_columns,
        [*fields, (send, HBM)],
        [VMEM((len(LEFT) * 8, NR), F32), VMEM((len(RIGHT) * 8, NR), F32)],
        [DMA((8,))],
    )
    left = lax.ppermute(far_right, "az", higher_az)
    right = lax.ppermute(far_left, "az", lower_az)
    far_up, far_down = call(
        pack_far_planes,
        [*tiles, left, right],
        [VMEM((FAR_BELOW_ROWS, 128), F32), VMEM((FAR_ABOVE_ROWS, 128), F32)],
    )
    far_below = lax.ppermute(far_up, "ax", higher_ax)
    far_above = lax.ppermute(far_down, "ax", lower_ax)

    swept, first_tile = call(
        far_kernel,
        [*near_tiles, *tiles, near_below, near_above, far_below, far_above, left, right],
        [HBM((ROWS, NR), F32), VMEM((ROWS, 128), F32)],
        [VMEM((TILES, 36 * 8, 128), F32)] * 4 + [VMEM((ROWS, NR), F32), DMA],
        cost=4.0,
    )

    (back,) = call(
        filter_kernel, [got, *held_tables], [HBM((2 * R_AX, 128), F32)], [VMEM((2 * R_AX, 128), F32), DMA]
    )
    returned = lax.all_to_all(back.reshape(R_AX, 2, 128), "az", 0, 0, tiled=True).reshape(2 * R_AX, 128)
    (delta,) = call(arrival_kernel, [got, volume], [VMEM((XR, ROWS), F32)])
    (out,) = call(
        final_kernel,
        [returned, delta, first_tile, (swept, HBM)],
        [HBM((ROWS, NR), F32)],
        [VMEM((ROWS, 128), F32), DMA],
        aliases={3: 0},
    )
    return out.reshape(COLS, PLANES, NR)


def solution(mesh):
    return jax.shard_map(
        local,
        mesh=mesh,
        in_specs=(
            P("az", "ax", None),
            P("az", "ax", None),
            P("az", "ax", None),
            P("az", "ax", None),
            P("az", "ax"),
            P("az", "ax"),
            P("az", "ax"),
            P("az", "ax"),
        ),
        out_specs=P("az", "ax", None),
        check_vma=False,
    )
```

```python
import functools
import math

import jax
import jax.numpy as jnp
import ml_dtypes
import numpy as np
from jax import lax
from jax.experimental import pallas as pl
from jax.experimental.pallas import tpu as pltpu
from jax.sharding import PartitionSpec as P

R_AX = 64
XR = 16
COLS = 32
PLANES = 8
ROWS = COLS * PLANES
NR = 512
SLOTS = 8
KD = 40

F32 = jnp.float32
BF16 = jnp.bfloat16

BELOW = ((0, -2), (0, -1), (1, -2), (1, -1), (2, -1), (3, -1))
ABOVE = ((0, 8), (0, 9), (1, 8), (2, 8), (3, 8))
HALO_PLANES = ((-2, -1, 8, 9), (-2, -1, 8), (-1, 8), (-1, 8))

NEAR_LEFT = tuple((f, c) for f in range(3) for c in range(-4, 0)) + tuple((3, c) for c in range(-3, 0))
NEAR_CORNERS = tuple((f, c, p) for f, c in NEAR_LEFT for p in HALO_PLANES[f])
NEAR_ROWS = 8 * len(NEAR_LEFT) + 48
LEFT = ((0, -2), (0, -1), (1, -2), (1, -1), (2, -2), (2, -1), (3, -1))
RIGHT = ((0, 32), (0, 33), (1, 32), (1, 33), (2, 32), (3, 32))
TILES = NR // 128


def far_layout(planes):
    entries, row = [], 0
    for tile in range(TILES):
        for field, plane in planes:
            left = sum(f == field for f, _ in LEFT)
            right = sum(f == field for f, _ in RIGHT)
            if tile:
                runs = ((-left, left + COLS + right),)
            else:
                runs = ((-left, left), (COLS, right))
            for column, count in runs:
                entries.append((tile, field, plane, column, count, row))
                row += count
    return entries, -(-row // 8) * 8


FAR_BELOW, FAR_BELOW_ROWS = far_layout(BELOW)
FAR_ABOVE, FAR_ABOVE_ROWS = far_layout(ABOVE)


def plane_slot(plane):
    return plane % 16 - 8


def copy_all(pairs, semaphores, first=0):
    copies = [pltpu.make_async_copy(a, b, semaphores.at[first + k]) for k, (a, b) in enumerate(pairs)]
    for copy in copies:
        copy.start()
    return copies


def copy_out(source, target, semaphore):
    copy = pltpu.make_async_copy(source, target, semaphore)
    copy.start()
    copy.wait()


def pack_first(*refs):
    fields, tiles, (up, down, right, left, semaphores) = refs[:4], refs[4:8], refs[8:]
    copies = copy_all([(f.at[:, pl.ds(0, 128)], tile) for f, tile in zip(fields, tiles)], semaphores)
    pairs = []
    for columns, out, shift in ((LEFT, right, COLS), (RIGHT, left, -COLS)):
        for field in range(4):
            at = [k for k, (f, _) in enumerate(columns) if f == field]
            source = fields[field].at[pl.ds((columns[at[0]][1] + shift) * 8, len(at) * 8), :]
            pairs.append((source, out.at[pl.ds(at[0] * 8, len(at) * 8), :]))
    far_copies = copy_all(pairs, semaphores, 4)
    for field, copy in enumerate(copies):
        copy.wait()
        for planes, out, shift in ((BELOW, up, PLANES), (ABOVE, down, -PLANES)):
            for k, (of, plane) in enumerate(planes):
                if of == field:
                    out[k * COLS : (k + 1) * COLS, :] = tiles[field][pl.ds(plane + shift, COLS, stride=PLANES), :]
    for copy in far_copies:
        copy.wait()


def pack_near_columns(*refs):
    tiles, (below, above, _, _, right) = refs[:4], refs[4:]
    for k, (field, column) in enumerate(NEAR_LEFT):
        right[k * 8 : k * 8 + 8, :] = tiles[field][(column + COLS) * 8 : (column + COLS + 1) * 8, :]
    right[len(NEAR_LEFT) * 8 :, :] = jnp.zeros((48, 128), F32)
    for k, (field, column, plane) in enumerate(NEAR_CORNERS):
        planes, source = (BELOW, below) if plane < 0 else (ABOVE, above)
        row = planes.index((field, plane)) * COLS + column + COLS
        at = len(NEAR_LEFT) * 8 + k
        right[at : at + 1, :] = source[row : row + 1, :]


def pack_far_planes(*refs):
    fields, (left, right, up, down, *tiles, semaphores) = refs[:4], refs[4:]
    pairs = []
    for field, tile in zip(fields, tiles):
        for k in range(1, TILES):
            pairs.append((field.at[:, pl.ds(k * 128, 128)], tile.at[pl.ds((k - 1) * ROWS, ROWS), :]))
    for copy in copy_all(pairs, semaphores):
        copy.wait()
    for entries, out, shift in ((FAR_BELOW, up, PLANES), (FAR_ABOVE, down, -PLANES)):
        for tile, field, plane, column, count, row in entries:
            lanes = pl.ds(tile * 128, 128)
            for at in range(count):
                for columns, source in ((LEFT, left), (RIGHT, right)):
                    if (field, column + at) in columns:
                        origin = columns.index((field, column + at)) * 8 + plane + shift
                        out[row + at : row + at + 1, :] = source[origin : origin + 1, lanes]
            if tile:
                rows = pl.ds((tile - 1) * ROWS + plane + shift, COLS, stride=PLANES)
                out[row - column : row - column + COLS, :] = tiles[field][rows, :]
        used = sum(e[4] for e in entries)
        if used < out.shape[0]:
            out[used:, :] = jnp.zeros((out.shape[0] - used, 128), F32)


def upwind(courant, below_cell, above_cell):
    return courant * jnp.where(courant > 0.0, below_cell, above_cell)


def sweep(lowest, load_own, load_halo, store, lanes, unrolled):
    plane = lax.broadcasted_iota(jnp.int32, (8, lanes), 0)
    cycle = lax.broadcasted_iota(jnp.int32, (8, lanes), 1)
    first, last = plane == 0, plane == 7
    radius = cycle.astype(F32)
    outer_radius = radius + 1.0
    inverse = 1.0 / (radius + 0.5)
    axis_cell, rim_cell = cycle == 0, cycle == NR - 1

    def load(field, column):
        return load_own(field, column), load_halo(field, column)

    def next_plane(pair):
        own, halo = (pltpu.roll(a, 7, 0) for a in pair)
        return jnp.where(last, halo, own), jnp.where(last, own, halo)

    def previous_plane(pair):
        own, halo = (pltpu.roll(a, 1, 0) for a in pair)
        return jnp.where(first, halo, own), jnp.where(first, own, halo)

    def flux(courant, low, high):
        return tuple(upwind(c, a, b) for c, a, b in zip(courant, low, high))

    def update(values, upper, lower):
        return tuple(v - (a - b) for v, a, b in zip(values, upper, lower))

    def axial(values, courant):
        face = flux(courant, values, next_plane(values))
        return update(values, face, previous_plane(face))

    def axial_own(values, courant):
        own, halo = flux(courant, values, next_plane(values))
        lower = jnp.where(first, pltpu.roll(halo, 1, 0), pltpu.roll(own, 1, 0))
        return values[0] - (own - lower)

    def radial_one(values, courant):
        above_cell = jnp.where(rim_cell, 0.0, pltpu.roll(values, lanes - 1, 1))
        outer = outer_radius * upwind(courant, values, above_cell)
        inner = jnp.where(axis_cell, 0.0, pltpu.roll(outer, 1, 1))
        return values - (outer - inner) * inverse

    def radial(values, courant):
        return tuple(radial_one(v, c) for v, c in zip(values, courant))

    def step(column, state, stage):
        v1_old, face_a_old, v3_old, face_b_old = state
        v1 = axial(load(0, column), load(1, column))
        face_a = v3 = face_b = None
        if stage >= 1:
            face_a = flux(load(2, column - 1), v1_old, v1)
        if stage >= 2:
            v2 = update(v1_old, face_a, face_a_old)
            v3 = radial(v2, load(3, column - 1))
        if stage >= 3:
            face_b = flux(load(2, column - 2), v3_old, v3)
        if stage >= 4:
            v4 = update(v3_old, face_b, face_b_old)
            store(column - 2, axial_own(v4, load(1, column - 2)))
        return v1, face_a, v3, face_b

    state = (None, None, None, None)
    for stage in range(6):
        state = step(lowest + stage, state, stage)
    if unrolled:
        for stage in range(6, 34):
            state = step(lowest + stage, state, stage)
    else:
        state = lax.fori_loop(lowest + 6, lowest + 34, lambda column, s: step(column, s, 6), state, unroll=4)
    for stage in (34, 35):
        state = step(lowest + stage, state, stage)


def near_kernel(*refs):
    fields, (below, above, left, crossing, send) = refs[:4], refs[4:9]
    halos, (swept, out, semaphore) = refs[9:13], refs[13:]
    lowest = -4
    for planes, source in ((BELOW, below), (ABOVE, above)):
        for k, (field, plane) in enumerate(planes):
            rows = pl.ds(-lowest * 8 + plane_slot(plane), COLS, stride=8)
            halos[field][rows, :] = source[k * COLS : (k + 1) * COLS, :]
    for k, (field, column, plane) in enumerate(NEAR_CORNERS):
        at = (column - lowest) * 8 + plane_slot(plane)
        row = len(NEAR_LEFT) * 8 + k
        halos[field][at : at + 1, :] = left[row : row + 1, :]

    def load_own(field, column):
        if column < 0:
            at = NEAR_LEFT.index((field, column)) * 8
            return left[at : at + 8, :]
        return fields[field][column * 8 : column * 8 + 8, :]

    def load_halo(field, column):
        return halos[field][(column - lowest) * 8 : (column - lowest + 1) * 8, :]

    def store(column, values):
        swept[(column + 2) * 8 : (column + 3) * 8, :] = values

    sweep(lowest, load_own, load_halo, store, 128, True)
    turned = swept[...].T
    out[pl.ds(0, R_AX, stride=4), :] = turned[:R_AX, :128]
    out[pl.ds(1, R_AX, stride=4), :] = turned[:R_AX, 128:]
    out[pl.ds(2, R_AX, stride=4), :] = crossing[:R_AX, :]
    out[pl.ds(3, R_AX, stride=4), :] = crossing[R_AX:, :]
    copy_out(out, send, semaphore)


def far_kernel(*refs):
    sources, (near_below, near_above, below, above, left, right) = refs[:4], refs[4:10]
    (result, first_tile), halos, fields, (out, semaphores) = refs[10:12], refs[12:16], refs[16:20], refs[20:]
    copies = copy_all(zip(sources, fields), semaphores)
    lowest = -2
    for planes, near, entries, far in ((BELOW, near_below, FAR_BELOW, below), (ABOVE, near_above, FAR_ABOVE, above)):
        for k, (field, plane) in enumerate(planes):
            rows = pl.ds(-lowest * 8 + plane_slot(plane), COLS, stride=8)
            halos[field].at[0][rows, :] = near[k * COLS : (k + 1) * COLS, :]
        for tile, field, plane, column, count, row in entries:
            rows = pl.ds((column - lowest) * 8 + plane_slot(plane), count, stride=8)
            halos[field].at[tile][rows, :] = far[row : row + count, :]

    def load_own(field, column):
        for columns, source in ((LEFT, left), (RIGHT, right)):
            if isinstance(column, int) and (field, column) in columns:
                at = columns.index((field, column)) * 8
                return source[at : at + 8, :]
        return fields[field][pl.ds(column * 8 if isinstance(column, int) else pl.multiple_of(column * 8, 8), 8), :]

    def load_halo(field, column):
        at = (column - lowest) * 8
        rows = pl.ds(at if isinstance(at, int) else pl.multiple_of(at, 8), 8)
        return jnp.concatenate([halos[field].at[tile][rows, :] for tile in range(TILES)], axis=1)

    def store(column, values):
        rows = pl.ds(column * 8 if isinstance(column, int) else pl.multiple_of(column * 8, 8), 8)
        out[rows, :] = values
        first_tile[rows, :] = values[:, :128]

    for copy in copies:
        copy.wait()
    sweep(lowest, load_own, load_halo, store, NR, False)
    copy_out(out, result, semaphores.at[4])


def pieces(values, count):
    out = []
    for _ in range(count):
        piece = values.astype(BF16)
        out.append(piece)
        values = values - piece.astype(F32)
    return out


def mm(a, b, dims=((1,), (0,))):
    return lax.dot_general(a, b, (dims, ((), ())), preferred_element_type=F32)


def plic_volume(plane_code, strip_width):
    normal = lax.shift_right_logical(plane_code, 6).astype(F32)
    offset = lax.bitwise_and(plane_code, 63).astype(F32)
    plane_angle = math.pi / 16 + (normal + 0.5) * (3 * math.pi / 512)
    normal_along = jnp.cos(plane_angle)
    across = jnp.sin(plane_angle)
    plane_level = (offset + 0.5) * (normal_along + across) / 64.0
    strip_span = strip_width * normal_along

    def square(shift_value):
        positive = jnp.maximum(shift_value, 0.0)
        return positive * positive

    strip_area = (
        square(plane_level)
        - square(plane_level - strip_span)
        - square(plane_level - across)
        + square(plane_level - strip_span - across)
    ) / (2.0 * strip_span * across)
    return strip_width * strip_area


def crossing_kernel(*refs):
    (code, width, reader, landing), tables, (out, volume_out) = refs[:4], refs[4:11], refs[11:13]
    copies = copy_all(zip(tables, refs[13:20]), refs[20])
    iota = functools.partial(lax.broadcasted_iota, jnp.int32)
    volume = plic_volume(code[...], width[...])
    both = jnp.concatenate([reader[...].astype(F32), landing[...].astype(F32)], axis=0).astype(BF16)
    column_of_row = (iota((ROWS, COLS), 0) // 8 == iota((ROWS, COLS), 1)).astype(F32).astype(BF16)
    spread = mm(column_of_row, both, ((1,), (1,)))
    row16, lane16 = iota((ROWS, 16), 0), iota((ROWS, 16), 1)
    reader_rows = jnp.sum(jnp.where(lane16 == row16 % 8, spread, 0.0), axis=1, keepdims=True)
    landing_rows = jnp.sum(jnp.where(lane16 == row16 % 8 + 8, spread, 0.0), axis=1, keepdims=True)
    across = mm(both, column_of_row, ((1,), (1,)))
    reader_lanes = jnp.sum(
        jnp.where(iota((16, ROWS), 0) == iota((16, ROWS), 1) % 8, across, 0.0), axis=0, keepdims=True
    )
    same = (reader_rows == reader_lanes) & (iota((ROWS, ROWS), 1) < iota((ROWS, ROWS), 0))
    rank = jnp.sum(jnp.where(same, 1.0, 0.0), axis=1, keepdims=True)

    row, lane = iota((ROWS, 128), 0), iota((ROWS, 128), 1)
    wide = jnp.broadcast_to(volume[:, None, :], (COLS, PLANES, 128)).reshape(ROWS, 128)
    own = jnp.where(lane // 16 == row % 8, wide, 0.0)
    repeat = (iota((128, 128), 0) % 16 == iota((128, 128), 1) % 16).astype(F32).astype(BF16)
    rows_of_volume = sum(mm(piece, repeat) for piece in pieces(own, 3))
    volume_out[...] = rows_of_volume.T[:XR, :]
    chosen = (reader_lanes == iota((R_AX, ROWS), 0).astype(F32)).astype(F32).astype(BF16)
    slotted = jnp.where((lane // 16).astype(F32) == rank, rows_of_volume, 0.0)
    out[:R_AX, :] = sum(mm(chosen, piece) for piece in pieces(slotted, 3))
    target = landing_rows * 8.0 + (row % 8).astype(F32) + 1.0
    marked = jnp.where(lane.astype(F32) == rank, target, 0.0)
    out[R_AX:, :] = mm(chosen, marked.astype(BF16))
    for copy in copies:
        copy.wait()


def arrival_kernel(received, volume, out):
    values = received[pl.ds(2, R_AX, stride=4), :]
    targets = received[pl.ds(3, R_AX, stride=4), :]
    turned = values.T
    row = lax.broadcasted_iota(jnp.int32, (R_AX, ROWS), 1).astype(F32) + 1.0
    total = -volume[...]
    for slot in range(SLOTS):
        chosen = (targets[:, slot : slot + 1] == row).astype(F32).astype(BF16)
        for piece in pieces(turned[slot * XR : (slot + 1) * XR, :], 3):
            total += mm(piece, chosen)
    out[...] = total


def halves(table):
    high = table.astype(ml_dtypes.bfloat16)
    low = (table - high.astype(np.float64)).astype(ml_dtypes.bfloat16)
    return high, low


def filter_tables():
    outer, sector = np.arange(33)[:, None], np.arange(64)[None, :]
    phase = 2 * np.pi * (outer * sector % 64) / 64
    first = np.zeros((2 * KD, 64))
    first[:33], first[KD : KD + 33] = np.cos(phase), -np.sin(phase)
    weight = np.where((outer == 0) | (outer == 32), 1.0, 2.0) / 2048
    last = np.zeros((64, 2 * KD))
    last[:, :33], last[:, KD : KD + 33] = (weight * np.cos(phase)).T, (-weight * np.sin(phase)).T
    column, plane = np.arange(ROWS) // PLANES, np.arange(ROWS) % PLANES
    inner = 2 * np.pi * (column[:, None] * column[None, :] % 32) / 32
    same = plane[:, None] == plane[None, :]
    block = np.concatenate([np.where(same, np.cos(inner), 0.0), np.where(same, -np.sin(inner), 0.0)], axis=1)
    turn = 2 * np.pi * np.arange(KD)[:, None] * column[None, :] / 2048
    mode = np.arange(KD)[:, None] + 64 * column[None, :]
    shift = 2 * np.pi * (2 * mode % 2048) / 2048
    turns = [np.cos(turn), -np.sin(turn), np.cos(shift), np.sin(shift)]
    twiddle = np.concatenate(turns, axis=0).astype(np.float32)
    return (*halves(first), *halves(block), twiddle, *halves(last))


def dot3(a, b):
    (ah, al), (bh, bl) = a, b
    return mm(ah, bh) + (mm(al, bh) + mm(ah, bl))


def filter_kernel(received, first_h, first_l, block_h, block_l, twiddle, last_h, last_l, send, out, semaphore):
    sectors = jnp.concatenate(
        [received[pl.ds(0, R_AX, stride=4), :], received[pl.ds(1, R_AX, stride=4), :]], axis=1
    )
    outer = dot3((first_h[...], first_l[...]), pieces(sectors, 2))
    re, im = outer[:KD], outer[KD:]
    t_re, t_im, s_re, s_im = (twiddle[k * KD : (k + 1) * KD, :] for k in range(4))
    turned = jnp.concatenate([re * t_re - im * t_im, re * t_im + im * t_re], axis=0)
    block = (block_h[...], block_l[...])
    inner = dot3(pieces(turned, 2), block)
    re = inner[:KD, :ROWS] - inner[KD:, ROWS:]
    im = inner[:KD, ROWS:] + inner[KD:, :ROWS]
    re, im = re * s_re - im * s_im, re * s_im + im * s_re
    mode = lax.broadcasted_iota(jnp.int32, (KD, ROWS), 0) + 64 * (
        lax.broadcasted_iota(jnp.int32, (KD, ROWS), 1) // PLANES
    )
    folded = jnp.minimum(mode, 2048 - mode).astype(F32)
    cutoff = (lax.axis_index("az") + 1).astype(F32) * 2.0
    scaled = folded / cutoff
    damped = jnp.exp(-(scaled * scaled))
    back = dot3(pieces(jnp.concatenate([re * damped, im * damped], axis=0), 2), block)
    re = back[:KD, :ROWS] + back[KD:, ROWS:]
    im = back[KD:, :ROWS] - back[:KD, ROWS:]
    turned = jnp.concatenate([re * t_re + im * t_im, im * t_re - re * t_im], axis=0)
    result = dot3((last_h[...], last_l[...]), pieces(turned, 2))
    out[pl.ds(0, R_AX, stride=2), :] = result[:, :128]
    out[pl.ds(1, R_AX, stride=2), :] = result[:, 128:]
    copy_out(out, send, semaphore)


def final_kernel(received, delta, swept, _, result, out, semaphore):
    near = jnp.concatenate(
        [received[pl.ds(0, R_AX, stride=2), :], received[pl.ds(1, R_AX, stride=2), :]], axis=1
    )
    near = jnp.concatenate([near[:XR] + delta[...], near[XR:], jnp.zeros((R_AX, ROWS), F32)], axis=0)
    cycle = lax.broadcasted_iota(jnp.int32, (ROWS, 128), 1)
    out[...] = jnp.where(cycle < R_AX, near.T, swept[...])
    copy_out(out, result.at[:, pl.ds(0, 128)], semaphore)


VMEM, HBM = pltpu.VMEM, pltpu.HBM
DMA = pltpu.SemaphoreType.DMA


def call(kernel, inputs, outputs, scratch=(), cost=1.0, aliases=None):
    arrays, specs = [], []
    for given in inputs:
        array, space = given if isinstance(given, tuple) else (given, VMEM)
        arrays.append(pltpu.with_memory_space_constraint(array, HBM) if space is HBM else array)
        specs.append(pl.BlockSpec(memory_space=space))
    out_specs = [pl.BlockSpec(memory_space=o.memory_space) for o in outputs]
    return pl.pallas_call(
        kernel,
        in_specs=specs,
        out_specs=out_specs,
        out_shape=list(outputs),
        scratch_shapes=list(scratch),
        input_output_aliases=aliases or {},
        cost_estimate=pl.CostEstimate(flops=int(cost * 1e6), bytes_accessed=int(cost * 3e6), transcendentals=0),
        compiler_params=pltpu.CompilerParams(vmem_limit_bytes=16 * 1024 * 1024),
    )(*arrays)


def local(
    fraction,
    courant_axial,
    courant_azimuth,
    courant_radial,
    plane_code,
    strip_width,
    tile_reader,
    landing_column,
):
    ax_count, az_count = lax.axis_size("ax"), lax.axis_size("az")
    higher_ax, higher_az = ([(i, (i + 1) % n) for i in range(n)] for n in (ax_count, az_count))
    lower_ax, lower_az = ([(j, i) for i, j in pairs] for pairs in (higher_ax, higher_az))
    fields = [(a.reshape(ROWS, NR), HBM) for a in (fraction, courant_axial, courant_azimuth, courant_radial)]

    *near_tiles, near_up, near_down, far_right, far_left = call(
        pack_first,
        fields,
        [VMEM((ROWS, 128), F32)] * 4
        + [VMEM((len(BELOW) * COLS, 128), F32), VMEM((len(ABOVE) * COLS, 128), F32)]
        + [VMEM((len(LEFT) * 8, NR), F32), VMEM((len(RIGHT) * 8, NR), F32)],
        [DMA((12,))],
    )
    near_below = lax.ppermute(near_up, "ax", higher_ax)
    near_above = lax.ppermute(near_down, "ax", lower_ax)
    left = lax.ppermute(far_right, "az", higher_az)
    right = lax.ppermute(far_left, "az", lower_az)

    tables = filter_tables()
    crossing, volume, *held_tables = call(
        crossing_kernel,
        [plane_code, strip_width, tile_reader.T, landing_column.T, *((jnp.asarray(t), HBM) for t in tables)],
        [VMEM((2 * R_AX, 128), F32), VMEM((XR, ROWS), F32)] + [VMEM(t.shape, t.dtype) for t in tables],
        [DMA((len(tables),))],
    )

    (near_right,) = call(
        pack_near_columns,
        [*near_tiles, near_below, near_above, (left, pl.ANY), (right, pl.ANY)],
        [VMEM((NEAR_ROWS, 128), F32)],
    )
    near_left = lax.ppermute(near_right, "az", higher_az)
    (send,) = call(
        near_kernel,
        [*near_tiles, near_below, near_above, near_left, crossing],
        [HBM((4 * R_AX, 128), F32)],
        [VMEM((36 * 8, 128), F32)] * 4 + [VMEM((ROWS, 128), F32), VMEM((4 * R_AX, 128), F32), DMA],
    )
    got = lax.all_to_all(send.reshape(R_AX, 4, 128), "az", 0, 0, tiled=True).reshape(4 * R_AX, 128)

    far_up, far_down = call(
        pack_far_planes,
        [*fields, left, right],
        [VMEM((FAR_BELOW_ROWS, 128), F32), VMEM((FAR_ABOVE_ROWS, 128), F32)],
        [VMEM(((TILES - 1) * ROWS, 128), F32)] * 4 + [DMA((4 * (TILES - 1),))],
    )
    far_below = lax.ppermute(far_up, "ax", higher_ax)
    far_above = lax.ppermute(far_down, "ax", lower_ax)

    swept, first_tile = call(
        far_kernel,
        [*fields, near_below, near_above, far_below, far_above, left, right],
        [HBM((ROWS, NR), F32), VMEM((ROWS, 128), F32)],
        [VMEM((TILES, 36 * 8, 128), F32)] * 4 + [VMEM((ROWS, NR), F32)] * 5 + [DMA((5,))],
        cost=4.0,
    )

    (back,) = call(
        filter_kernel, [got, *held_tables], [HBM((2 * R_AX, 128), F32)], [VMEM((2 * R_AX, 128), F32), DMA]
    )
    returned = lax.all_to_all(back.reshape(R_AX, 2, 128), "az", 0, 0, tiled=True).reshape(2 * R_AX, 128)
    (delta,) = call(arrival_kernel, [got, volume], [VMEM((XR, ROWS), F32)])
    (out,) = call(
        final_kernel,
        [returned, delta, first_tile, (swept, HBM)],
        [HBM((ROWS, NR), F32)],
        [VMEM((ROWS, 128), F32), DMA],
        aliases={3: 0},
    )
    return out.reshape(COLS, PLANES, NR)


def solution(mesh):
    return jax.shard_map(
        local,
        mesh=mesh,
        in_specs=(
            P("az", "ax", None),
            P("az", "ax", None),
            P("az", "ax", None),
            P("az", "ax", None),
            P("az", "ax"),
            P("az", "ax"),
            P("az", "ax"),
            P("az", "ax"),
        ),
        out_specs=P("az", "ax", None),
        check_vma=False,
    )
```

```python
import functools
import math

import jax
import jax.numpy as jnp
import ml_dtypes
import numpy as np
from jax import lax
from jax.experimental import pallas as pl
from jax.experimental.pallas import tpu as pltpu
from jax.sharding import PartitionSpec as P

R_AX = 64
XR = 16
COLS = 32
PLANES = 8
ROWS = COLS * PLANES
NR = 512
SLOTS = 8
KD = 40

F32 = jnp.float32
BF16 = jnp.bfloat16

BELOW = ((0, -2), (0, -1), (1, -2), (1, -1), (2, -1), (3, -1))
ABOVE = ((0, 8), (0, 9), (1, 8), (2, 8), (3, 8))
HALO_PLANES = ((-2, -1, 8, 9), (-2, -1, 8), (-1, 8), (-1, 8))

LOWEST = -4
LEFT = tuple((f, c) for f in range(3) for c in range(-4, 0)) + tuple((3, c) for c in range(-3, 0))
LEFT_COUNT = (4, 4, 4, 3)
TILES = NR // 128
KEPT = ROWS - 16


def halo_layout(planes, tiles):
    entries, row = [], 0
    for tile in tiles:
        for field, plane in planes:
            entries.append((tile, field, plane, LEFT_COUNT[field], row))
            row += LEFT_COUNT[field] + COLS
    return entries, -(-row // 8) * 8


NEAR_BELOW, NEAR_BELOW_ROWS = halo_layout(BELOW, (0,))
NEAR_ABOVE, NEAR_ABOVE_ROWS = halo_layout(ABOVE, (0,))
FAR_BELOW, FAR_BELOW_ROWS = halo_layout(BELOW, range(1, TILES))
FAR_ABOVE, FAR_ABOVE_ROWS = halo_layout(ABOVE, range(1, TILES))


def plane_slot(plane):
    return plane % 16 - 8


def copy_out(source, target, semaphore):
    copy = pltpu.make_async_copy(source, target, semaphore)
    copy.start()
    copy.wait()


def copy_all(pairs, semaphores, first=0):
    copies = [pltpu.make_async_copy(a, b, semaphores.at[first + k]) for k, (a, b) in enumerate(pairs)]
    for copy in copies:
        copy.start()
    return copies


def pack_columns(*refs):
    fields, (right, semaphores) = refs[:4], refs[4:]
    pairs, row = [], 0
    for field, count in zip(fields, LEFT_COUNT):
        pairs.append((field.at[pl.ds(ROWS - count * 8, count * 8), :], right.at[pl.ds(row, count * 8), :]))
        row += count * 8
    for copy in copy_all(pairs, semaphores):
        copy.wait()


def pack_planes(entries, out, shift, load, left):
    for tile, field, plane, count, row in entries:
        for at in range(count):
            origin = LEFT.index((field, at - count)) * 8 + plane + shift
            out[row + at : row + at + 1, :] = left[origin : origin + 1, pl.ds(tile * 128, 128)]
        out[row + count : row + count + COLS, :] = load(tile, field, plane + shift)
    used = entries[-1][4] + entries[-1][3] + COLS
    if used < out.shape[0]:
        out[used:, :] = jnp.zeros((out.shape[0] - used, 128), F32)


def pack_near_planes(*refs):
    tiles, (left, up, down) = refs[:4], refs[4:]

    def load(_, field, plane):
        return tiles[field][pl.ds(plane, COLS, stride=PLANES), :]

    pack_planes(NEAR_BELOW, up, PLANES, load, left)
    pack_planes(NEAR_ABOVE, down, -PLANES, load, left)


def pack_far_planes(*refs):
    fields, (left, up, down, *tiles, semaphores) = refs[:4], refs[4:]
    pairs = []
    for field, tile in zip(fields, tiles):
        for k in range(1, TILES):
            pairs.append((field.at[:, pl.ds(k * 128, 128)], tile.at[pl.ds((k - 1) * ROWS, ROWS), :]))
    for copy in copy_all(pairs, semaphores):
        copy.wait()

    def load(tile, field, plane):
        return tiles[field][pl.ds((tile - 1) * ROWS + plane, COLS, stride=PLANES), :]

    pack_planes(FAR_BELOW, up, PLANES, load, left)
    pack_planes(FAR_ABOVE, down, -PLANES, load, left)


def upwind(courant, below_cell, above_cell):
    return courant * jnp.where(courant > 0.0, below_cell, above_cell)


def sweep(count, load_own, load_halo, store, lanes, unrolled):
    plane = lax.broadcasted_iota(jnp.int32, (8, lanes), 0)
    cycle = lax.broadcasted_iota(jnp.int32, (8, lanes), 1)
    first, last = plane == 0, plane == 7
    radius = cycle.astype(F32)
    outer_radius = radius + 1.0
    inverse = 1.0 / (radius + 0.5)
    axis_cell, rim_cell = cycle == 0, cycle == NR - 1

    def load(field, column):
        return load_own(field, column), load_halo(field, column)

    def next_plane(pair):
        own, halo = (pltpu.roll(a, 7, 0) for a in pair)
        return jnp.where(last, halo, own), jnp.where(last, own, halo)

    def previous_plane(pair):
        own, halo = (pltpu.roll(a, 1, 0) for a in pair)
        return jnp.where(first, halo, own), jnp.where(first, own, halo)

    def flux(courant, low, high):
        return tuple(upwind(c, a, b) for c, a, b in zip(courant, low, high))

    def update(values, upper, lower):
        return tuple(v - (a - b) for v, a, b in zip(values, upper, lower))

    def axial(values, courant):
        face = flux(courant, values, next_plane(values))
        return update(values, face, previous_plane(face))

    def axial_own(values, courant):
        own, halo = flux(courant, values, next_plane(values))
        lower = jnp.where(first, pltpu.roll(halo, 1, 0), pltpu.roll(own, 1, 0))
        return values[0] - (own - lower)

    def radial_one(values, courant):
        above_cell = jnp.where(rim_cell, 0.0, pltpu.roll(values, lanes - 1, 1))
        outer = outer_radius * upwind(courant, values, above_cell)
        inner = jnp.where(axis_cell, 0.0, pltpu.roll(outer, 1, 1))
        return values - (outer - inner) * inverse

    def radial(values, courant):
        return tuple(radial_one(v, c) for v, c in zip(values, courant))

    def step(column, state, stage):
        v1_old, face_a_old, v3_old, face_b_old = state
        v1 = axial(load(0, column), load(1, column))
        face_a = v3 = face_b = None
        if stage >= 1:
            face_a = flux(load(2, column - 1), v1_old, v1)
        if stage >= 2:
            v2 = update(v1_old, face_a, face_a_old)
            v3 = radial(v2, load(3, column - 1))
        if stage >= 3:
            face_b = flux(load(2, column - 2), v3_old, v3)
        if stage >= 4:
            v4 = update(v3_old, face_b, face_b_old)
            store(column - 2, axial_own(v4, load(1, column - 2)))
        return v1, face_a, v3, face_b

    state = (None, None, None, None)
    for stage in range(6):
        state = step(LOWEST + stage, state, stage)
    stage = 6
    if not unrolled:
        state = lax.fori_loop(LOWEST + 6, LOWEST + 34, lambda column, s: step(column, s, 6), state, unroll=4)
        stage = 34
    for stage in range(stage, count):
        state = step(LOWEST + stage, state, stage)


def fill_halos(halos, entries, source):
    for tile, field, plane, count, row in entries:
        rows = pl.ds((-count - LOWEST) * 8 + plane_slot(plane), count + COLS, stride=8)
        halos[field].at[tile][rows, :] = source[row : row + count + COLS, :]


def row_slice(column):
    return pl.ds(column * 8 if isinstance(column, int) else pl.multiple_of(column * 8, 8), 8)


def loaders(fields, left, halos, tiles):
    def load_own(field, column):
        if isinstance(column, int) and column < 0:
            return left[row_slice(LEFT.index((field, column))), pl.ds(0, tiles * 128)]
        return fields[field][row_slice(column), :]

    def load_halo(field, column):
        parts = [halos[field].at[tile][row_slice(column - LOWEST), :] for tile in range(tiles)]
        return jnp.concatenate(parts, axis=1) if tiles > 1 else parts[0]

    return load_own, load_halo


def near_kernel(*refs):
    fields, (below, above, left, crossing, send) = refs[:4], refs[4:9]
    halos, (swept, out, semaphore) = refs[9:13], refs[13:]
    fill_halos(halos, NEAR_BELOW, below)
    fill_halos(halos, NEAR_ABOVE, above)

    def store(column, values):
        swept[row_slice(column + 2), :] = values

    sweep(COLS + 4, *loaders(fields, left, halos, 1), store, 128, True)
    turned = swept[...].T
    out[pl.ds(0, R_AX, stride=4), :] = turned[:R_AX, :128]
    out[pl.ds(1, R_AX, stride=4), :] = turned[:R_AX, 128:]
    out[pl.ds(2, R_AX, stride=4), :] = crossing[:R_AX, :]
    out[pl.ds(3, R_AX, stride=4), :] = crossing[R_AX:, :]
    copy_out(out, send, semaphore)


def fill_far_halos(halos, near_below, near_above, below, above):
    for entries, source in ((NEAR_BELOW, near_below), (NEAR_ABOVE, near_above), (FAR_BELOW, below), (FAR_ABOVE, above)):
        fill_halos(halos, entries, source)


def far_first_kernel(*refs):
    sources, planes, (left, out), halos = refs[:4], refs[4:8], refs[8:10], refs[10:14]
    fields, semaphores = refs[14:18], refs[18]
    copies = copy_all([(f.at[pl.ds(0, 16), :], held) for f, held in zip(sources, fields)], semaphores)
    fill_far_halos(halos, *planes)
    for copy in copies:
        copy.wait()

    def store(column, values):
        out[row_slice(column + 2), :] = values

    sweep(6, *loaders(fields, left, halos, TILES), store, NR, True)


def far_kernel(*refs):
    sources, planes, (left, result, first_tile), halos = refs[:4], refs[4:8], refs[8:11], refs[11:15]
    fields, (out, semaphores) = refs[15:19], refs[19:]
    copies = copy_all(zip(sources, fields), semaphores)
    fill_far_halos(halos, *planes)
    for copy in copies:
        copy.wait()

    def store(column, values):
        if not isinstance(column, int) or column >= 0:
            out[row_slice(column), :] = values
            first_tile[row_slice(column), :] = values[:, :128]

    sweep(COLS + 4, *loaders(fields, left, halos, TILES), store, NR, False)
    copy_out(out, result.at[pl.ds(0, KEPT), :], semaphores.at[4])


def pieces(values, count):
    out = []
    for _ in range(count):
        piece = values.astype(BF16)
        out.append(piece)
        values = values - piece.astype(F32)
    return out


def mm(a, b, dims=((1,), (0,))):
    return lax.dot_general(a, b, (dims, ((), ())), preferred_element_type=F32)


def plic_volume(plane_code, strip_width):
    normal = lax.shift_right_logical(plane_code, 6).astype(F32)
    offset = lax.bitwise_and(plane_code, 63).astype(F32)
    plane_angle = math.pi / 16 + (normal + 0.5) * (3 * math.pi / 512)
    normal_along = jnp.cos(plane_angle)
    across = jnp.sin(plane_angle)
    plane_level = (offset + 0.5) * (normal_along + across) / 64.0
    strip_span = strip_width * normal_along

    def square(shift_value):
        positive = jnp.maximum(shift_value, 0.0)
        return positive * positive

    strip_area = (
        square(plane_level)
        - square(plane_level - strip_span)
        - square(plane_level - across)
        + square(plane_level - strip_span - across)
    ) / (2.0 * strip_span * across)
    return strip_width * strip_area


def crossing_kernel(*refs):
    (code, width, reader, landing), fields, tables, (out, volume_out) = refs[:4], refs[4:8], refs[8:15], refs[15:17]
    sources = [f.at[:, pl.ds(0, 128)] for f in fields] + list(tables)
    copies = copy_all(zip(sources, refs[17:28]), refs[28])
    iota = functools.partial(lax.broadcasted_iota, jnp.int32)
    volume = plic_volume(code[...], width[...])
    both = jnp.concatenate([reader[...].astype(F32), landing[...].astype(F32)], axis=0).astype(BF16)
    column_of_row = (iota((ROWS, COLS), 0) // 8 == iota((ROWS, COLS), 1)).astype(F32).astype(BF16)
    spread = mm(column_of_row, both, ((1,), (1,)))
    row16, lane16 = iota((ROWS, 16), 0), iota((ROWS, 16), 1)
    reader_rows = jnp.sum(jnp.where(lane16 == row16 % 8, spread, 0.0), axis=1, keepdims=True)
    landing_rows = jnp.sum(jnp.where(lane16 == row16 % 8 + 8, spread, 0.0), axis=1, keepdims=True)
    across = mm(both, column_of_row, ((1,), (1,)))
    reader_lanes = jnp.sum(
        jnp.where(iota((16, ROWS), 0) == iota((16, ROWS), 1) % 8, across, 0.0), axis=0, keepdims=True
    )
    same = (reader_rows == reader_lanes) & (iota((ROWS, ROWS), 1) < iota((ROWS, ROWS), 0))
    rank = jnp.sum(jnp.where(same, 1.0, 0.0), axis=1, keepdims=True)

    row, lane = iota((ROWS, 128), 0), iota((ROWS, 128), 1)
    wide = jnp.broadcast_to(volume[:, None, :], (COLS, PLANES, 128)).reshape(ROWS, 128)
    own = jnp.where(lane // 16 == row % 8, wide, 0.0)
    repeat = (iota((128, 128), 0) % 16 == iota((128, 128), 1) % 16).astype(F32).astype(BF16)
    rows_of_volume = sum(mm(piece, repeat) for piece in pieces(own, 3))
    volume_out[...] = rows_of_volume.T[:XR, :]
    chosen = (reader_lanes == iota((R_AX, ROWS), 0).astype(F32)).astype(F32).astype(BF16)
    slotted = jnp.where((lane // 16).astype(F32) == rank, rows_of_volume, 0.0)
    out[:R_AX, :] = sum(mm(chosen, piece) for piece in pieces(slotted, 3))
    target = landing_rows * 8.0 + (row % 8).astype(F32) + 1.0
    marked = jnp.where(lane.astype(F32) == rank, target, 0.0)
    out[R_AX:, :] = mm(chosen, marked.astype(BF16))
    for copy in copies:
        copy.wait()


def arrival_kernel(received, volume, out):
    values = received[pl.ds(2, R_AX, stride=4), :]
    targets = received[pl.ds(3, R_AX, stride=4), :]
    turned = values.T
    row = lax.broadcasted_iota(jnp.int32, (R_AX, ROWS), 1).astype(F32) + 1.0
    total = -volume[...]
    for slot in range(SLOTS):
        chosen = (targets[:, slot : slot + 1] == row).astype(F32).astype(BF16)
        for piece in pieces(turned[slot * XR : (slot + 1) * XR, :], 3):
            total += mm(piece, chosen)
    out[...] = total


def halves(table):
    high = table.astype(ml_dtypes.bfloat16)
    low = (table - high.astype(np.float64)).astype(ml_dtypes.bfloat16)
    return high, low


def filter_tables():
    outer, sector = np.arange(33)[:, None], np.arange(64)[None, :]
    phase = 2 * np.pi * (outer * sector % 64) / 64
    first = np.zeros((2 * KD, 64))
    first[:33], first[KD : KD + 33] = np.cos(phase), -np.sin(phase)
    weight = np.where((outer == 0) | (outer == 32), 1.0, 2.0) / 2048
    last = np.zeros((64, 2 * KD))
    last[:, :33], last[:, KD : KD + 33] = (weight * np.cos(phase)).T, (-weight * np.sin(phase)).T
    column, plane = np.arange(ROWS) // PLANES, np.arange(ROWS) % PLANES
    inner = 2 * np.pi * (column[:, None] * column[None, :] % 32) / 32
    same = plane[:, None] == plane[None, :]
    block = np.concatenate([np.where(same, np.cos(inner), 0.0), np.where(same, -np.sin(inner), 0.0)], axis=1)
    turn = 2 * np.pi * np.arange(KD)[:, None] * column[None, :] / 2048
    mode = np.arange(KD)[:, None] + 64 * column[None, :]
    shift = 2 * np.pi * (2 * mode % 2048) / 2048
    turns = [np.cos(turn), -np.sin(turn), np.cos(shift), np.sin(shift)]
    twiddle = np.concatenate(turns, axis=0).astype(np.float32)
    return (*halves(first), *halves(block), twiddle, *halves(last))


def dot3(a, b):
    (ah, al), (bh, bl) = a, b
    return mm(ah, bh) + (mm(al, bh) + mm(ah, bl))


def filter_kernel(received, first_h, first_l, block_h, block_l, twiddle, last_h, last_l, send, out, semaphore):
    sectors = jnp.concatenate(
        [received[pl.ds(0, R_AX, stride=4), :], received[pl.ds(1, R_AX, stride=4), :]], axis=1
    )
    outer = dot3((first_h[...], first_l[...]), pieces(sectors, 2))
    re, im = outer[:KD], outer[KD:]
    t_re, t_im, s_re, s_im = (twiddle[k * KD : (k + 1) * KD, :] for k in range(4))
    turned = jnp.concatenate([re * t_re - im * t_im, re * t_im + im * t_re], axis=0)
    block = (block_h[...], block_l[...])
    inner = dot3(pieces(turned, 2), block)
    re = inner[:KD, :ROWS] - inner[KD:, ROWS:]
    im = inner[:KD, ROWS:] + inner[KD:, :ROWS]
    re, im = re * s_re - im * s_im, re * s_im + im * s_re
    mode = lax.broadcasted_iota(jnp.int32, (KD, ROWS), 0) + 64 * (
        lax.broadcasted_iota(jnp.int32, (KD, ROWS), 1) // PLANES
    )
    folded = jnp.minimum(mode, 2048 - mode).astype(F32)
    cutoff = (lax.axis_index("az") + 1).astype(F32) * 2.0
    scaled = folded / cutoff
    damped = jnp.exp(-(scaled * scaled))
    back = dot3(pieces(jnp.concatenate([re * damped, im * damped], axis=0), 2), block)
    re = back[:KD, :ROWS] + back[KD:, ROWS:]
    im = back[KD:, :ROWS] - back[:KD, ROWS:]
    turned = jnp.concatenate([re * t_re + im * t_im, im * t_re - re * t_im], axis=0)
    result = dot3((last_h[...], last_l[...]), pieces(turned, 2))
    out[pl.ds(0, R_AX, stride=2), :] = result[:, :128]
    out[pl.ds(1, R_AX, stride=2), :] = result[:, 128:]
    copy_out(out, send, semaphore)


def final_kernel(received, delta, swept, last, _, result, out, semaphores):
    rest = (pl.ds(KEPT, ROWS - KEPT), pl.ds(128, NR - 128))
    copy = pltpu.make_async_copy(last.at[:, pl.ds(128, NR - 128)], result.at[rest], semaphores.at[1])
    copy.start()
    near = jnp.concatenate(
        [received[pl.ds(0, R_AX, stride=2), :], received[pl.ds(1, R_AX, stride=2), :]], axis=1
    )
    near = jnp.concatenate([near[:XR] + delta[...], near[XR:], jnp.zeros((R_AX, ROWS), F32)], axis=0)
    cycle = lax.broadcasted_iota(jnp.int32, (ROWS, 128), 1)
    first_tile = jnp.concatenate([swept[...], last[:, :128]], axis=0)
    out[...] = jnp.where(cycle < R_AX, near.T, first_tile)
    copy_out(out, result.at[:, pl.ds(0, 128)], semaphores.at[0])
    copy.wait()


VMEM, HBM = pltpu.VMEM, pltpu.HBM
DMA = pltpu.SemaphoreType.DMA


def call(kernel, inputs, outputs, scratch=(), cost=1.0, aliases=None):
    arrays, specs = [], []
    for given in inputs:
        array, space = given if isinstance(given, tuple) else (given, VMEM)
        arrays.append(pltpu.with_memory_space_constraint(array, HBM) if space is HBM else array)
        specs.append(pl.BlockSpec(memory_space=space))
    out_specs = [pl.BlockSpec(memory_space=o.memory_space) for o in outputs]
    return pl.pallas_call(
        kernel,
        in_specs=specs,
        out_specs=out_specs,
        out_shape=list(outputs),
        scratch_shapes=list(scratch),
        input_output_aliases=aliases or {},
        cost_estimate=pl.CostEstimate(flops=int(cost * 1e6), bytes_accessed=int(cost * 3e6), transcendentals=0),
        compiler_params=pltpu.CompilerParams(vmem_limit_bytes=16 * 1024 * 1024),
    )(*arrays)


def local(
    fraction,
    courant_axial,
    courant_azimuth,
    courant_radial,
    plane_code,
    strip_width,
    tile_reader,
    landing_column,
):
    ax_count, az_count = lax.axis_size("ax"), lax.axis_size("az")
    higher_ax, higher_az = ([(i, (i + 1) % n) for i in range(n)] for n in (ax_count, az_count))
    lower_ax, lower_az = ([(j, i) for i, j in pairs] for pairs in (higher_ax, higher_az))
    fields = [(a.reshape(ROWS, NR), HBM) for a in (fraction, courant_axial, courant_azimuth, courant_radial)]

    (right,) = call(pack_columns, fields, [VMEM((len(LEFT) * 8, NR), F32)], [DMA((4,))])
    left = lax.ppermute(right, "az", higher_az)

    tables = filter_tables()
    crossing, volume, *held = call(
        crossing_kernel,
        [plane_code, strip_width, tile_reader.T, landing_column.T, *fields, *((jnp.asarray(t), HBM) for t in tables)],
        [VMEM((2 * R_AX, 128), F32), VMEM((XR, ROWS), F32)]
        + [VMEM((ROWS, 128), F32)] * 4
        + [VMEM(t.shape, t.dtype) for t in tables],
        [DMA((4 + len(tables),))],
    )
    near_tiles, held_tables = held[:4], held[4:]

    near_up, near_down = call(
        pack_near_planes,
        [*near_tiles, left],
        [VMEM((NEAR_BELOW_ROWS, 128), F32), VMEM((NEAR_ABOVE_ROWS, 128), F32)],
    )
    near_below = lax.ppermute(near_up, "ax", higher_ax)
    near_above = lax.ppermute(near_down, "ax", lower_ax)
    (send,) = call(
        near_kernel,
        [*near_tiles, near_below, near_above, left, crossing],
        [HBM((4 * R_AX, 128), F32)],
        [VMEM((1, 36 * 8, 128), F32)] * 4 + [VMEM((ROWS, 128), F32), VMEM((4 * R_AX, 128), F32), DMA],
    )
    got = lax.all_to_all(send.reshape(R_AX, 4, 128), "az", 0, 0, tiled=True).reshape(4 * R_AX, 128)

    far_up, far_down = call(
        pack_far_planes,
        [*fields, left],
        [VMEM((FAR_BELOW_ROWS, 128), F32), VMEM((FAR_ABOVE_ROWS, 128), F32)],
        [VMEM(((TILES - 1) * ROWS, 128), F32)] * 4 + [DMA((4 * (TILES - 1),))],
    )
    far_below = lax.ppermute(far_up, "ax", higher_ax)
    far_above = lax.ppermute(far_down, "ax", lower_ax)
    far_inputs = [*fields, near_below, near_above, far_below, far_above, left]
    far_halos = [VMEM((TILES, 36 * 8, 128), F32)] * 4
    (first_columns,) = call(
        far_first_kernel, far_inputs, [VMEM((16, NR), F32)], far_halos + [VMEM((16, NR), F32)] * 4 + [DMA((4,))]
    )
    last_columns = lax.ppermute(first_columns, "az", lower_az)
    swept, first_tile = call(
        far_kernel,
        far_inputs,
        [HBM((ROWS, NR), F32), VMEM((KEPT, 128), F32)],
        far_halos + [VMEM((ROWS, NR), F32)] * 4 + [VMEM((KEPT, NR), F32), DMA((5,))],
        cost=4.0,
    )

    (back,) = call(
        filter_kernel, [got, *held_tables], [HBM((2 * R_AX, 128), F32)], [VMEM((2 * R_AX, 128), F32), DMA]
    )
    returned = lax.all_to_all(back.reshape(R_AX, 2, 128), "az", 0, 0, tiled=True).reshape(2 * R_AX, 128)
    (delta,) = call(arrival_kernel, [got, volume], [VMEM((XR, ROWS), F32)])
    (out,) = call(
        final_kernel,
        [returned, delta, first_tile, last_columns, (swept, HBM)],
        [HBM((ROWS, NR), F32)],
        [VMEM((ROWS, 128), F32), DMA((2,))],
        aliases={4: 0},
    )
    return out.reshape(COLS, PLANES, NR)


def solution(mesh):
    return jax.shard_map(
        local,
        mesh=mesh,
        in_specs=(
            P("az", "ax", None),
            P("az", "ax", None),
            P("az", "ax", None),
            P("az", "ax", None),
            P("az", "ax"),
            P("az", "ax"),
            P("az", "ax"),
            P("az", "ax"),
        ),
        out_specs=P("az", "ax", None),
        check_vma=False,
    )
```

```python
import functools
import math

import jax
import jax.numpy as jnp
import ml_dtypes
import numpy as np
from jax import lax
from jax.experimental import pallas as pl
from jax.experimental.pallas import tpu as pltpu
from jax.sharding import PartitionSpec as P

R_AX = 64
XR = 16
COLS = 32
PLANES = 8
ROWS = COLS * PLANES
NR = 512
SLOTS = 8
KD = 40

F32 = jnp.float32
BF16 = jnp.bfloat16

BELOW = ((0, -2), (0, -1), (1, -2), (1, -1), (2, -1), (3, -1))
ABOVE = ((0, 8), (0, 9), (1, 8), (2, 8), (3, 8))
HALO_PLANES = ((-2, -1, 8, 9), (-2, -1, 8), (-1, 8), (-1, 8))

LOWEST = -4
LEFT = tuple((f, c) for f in range(3) for c in range(-4, 0)) + tuple((3, c) for c in range(-3, 0))
LEFT_COUNT = (4, 4, 4, 3)
TILES = NR // 128
KEPT = ROWS - 16


def halo_layout(planes, tiles):
    entries, row = [], 0
    for tile in tiles:
        for field, plane in planes:
            entries.append((tile, field, plane, LEFT_COUNT[field], row))
            row += LEFT_COUNT[field] + COLS
    return entries, -(-row // 8) * 8


NEAR_BELOW, NEAR_BELOW_ROWS = halo_layout(BELOW, (0,))
NEAR_ABOVE, NEAR_ABOVE_ROWS = halo_layout(ABOVE, (0,))
FAR_BELOW, FAR_BELOW_ROWS = halo_layout(BELOW, range(1, TILES))
FAR_ABOVE, FAR_ABOVE_ROWS = halo_layout(ABOVE, range(1, TILES))


def plane_slot(plane):
    return plane % 16 - 8


def copy_out(source, target, semaphore):
    copy = pltpu.make_async_copy(source, target, semaphore)
    copy.start()
    copy.wait()


def copy_all(pairs, semaphores, first=0):
    copies = [pltpu.make_async_copy(a, b, semaphores.at[first + k]) for k, (a, b) in enumerate(pairs)]
    for copy in copies:
        copy.start()
    return copies


def pack_columns(*refs):
    fields, (right, semaphores) = refs[:4], refs[4:]
    pairs, row = [], 0
    for field, count in zip(fields, LEFT_COUNT):
        pairs.append((field.at[pl.ds(ROWS - count * 8, count * 8), :], right.at[pl.ds(row, count * 8), :]))
        row += count * 8
    for copy in copy_all(pairs, semaphores):
        copy.wait()


def pack_planes(entries, out, shift, load, left):
    for tile, field, plane, count, row in entries:
        for at in range(count):
            origin = LEFT.index((field, at - count)) * 8 + plane + shift
            out[row + at : row + at + 1, :] = left[origin : origin + 1, pl.ds(tile * 128, 128)]
        out[row + count : row + count + COLS, :] = load(tile, field, plane + shift)
    used = entries[-1][4] + entries[-1][3] + COLS
    if used < out.shape[0]:
        out[used:, :] = jnp.zeros((out.shape[0] - used, 128), F32)


def pack_near_planes(*refs):
    tiles, (left, up, down) = refs[:4], refs[4:]

    def load(_, field, plane):
        return tiles[field][pl.ds(plane, COLS, stride=PLANES), :]

    pack_planes(NEAR_BELOW, up, PLANES, load, left)
    pack_planes(NEAR_ABOVE, down, -PLANES, load, left)


def pack_far_planes(*refs):
    fields, (left, up, down, *tiles, semaphores) = refs[:4], refs[4:]
    pairs = []
    for field, tile in zip(fields, tiles):
        for k in range(1, TILES):
            pairs.append((field.at[:, pl.ds(k * 128, 128)], tile.at[pl.ds((k - 1) * ROWS, ROWS), :]))
    for copy in copy_all(pairs, semaphores):
        copy.wait()

    def load(tile, field, plane):
        return tiles[field][pl.ds((tile - 1) * ROWS + plane, COLS, stride=PLANES), :]

    pack_planes(FAR_BELOW, up, PLANES, load, left)
    pack_planes(FAR_ABOVE, down, -PLANES, load, left)


def upwind(courant, below_cell, above_cell):
    return courant * jnp.where(courant > 0.0, below_cell, above_cell)


def sweep(count, load_own, load_halo, store, lanes, segments=None):
    plane = lax.broadcasted_iota(jnp.int32, (8, lanes), 0)
    cycle = lax.broadcasted_iota(jnp.int32, (8, lanes), 1)
    first, last = plane == 0, plane == 7
    radius = cycle.astype(F32)
    outer_radius = radius + 1.0
    inverse = 1.0 / (radius + 0.5)
    axis_cell, rim_cell = cycle == 0, cycle == NR - 1

    def load(field, column):
        return load_own(field, column), load_halo(field, column)

    def next_plane(pair):
        own, halo = (pltpu.roll(a, 7, 0) for a in pair)
        return jnp.where(last, halo, own), jnp.where(last, own, halo)

    def previous_plane(pair):
        own, halo = (pltpu.roll(a, 1, 0) for a in pair)
        return jnp.where(first, halo, own), jnp.where(first, own, halo)

    def flux(courant, low, high):
        return tuple(upwind(c, a, b) for c, a, b in zip(courant, low, high))

    def update(values, upper, lower):
        return tuple(v - (a - b) for v, a, b in zip(values, upper, lower))

    def axial(values, courant):
        face = flux(courant, values, next_plane(values))
        return update(values, face, previous_plane(face))

    def axial_own(values, courant):
        own, halo = flux(courant, values, next_plane(values))
        lower = jnp.where(first, pltpu.roll(halo, 1, 0), pltpu.roll(own, 1, 0))
        return values[0] - (own - lower)

    def radial_one(values, courant):
        above_cell = jnp.where(rim_cell, 0.0, pltpu.roll(values, lanes - 1, 1))
        outer = outer_radius * upwind(courant, values, above_cell)
        inner = jnp.where(axis_cell, 0.0, pltpu.roll(outer, 1, 1))
        return values - (outer - inner) * inverse

    def radial(values, courant):
        return tuple(radial_one(v, c) for v, c in zip(values, courant))

    def step(column, state, stage):
        v1_old, face_a_old, v3_old, face_b_old = state
        v1 = axial(load(0, column), load(1, column))
        face_a = v3 = face_b = None
        if stage >= 1:
            face_a = flux(load(2, column - 1), v1_old, v1)
        if stage >= 2:
            v2 = update(v1_old, face_a, face_a_old)
            v3 = radial(v2, load(3, column - 1))
        if stage >= 3:
            face_b = flux(load(2, column - 2), v3_old, v3)
        if stage >= 4:
            v4 = update(v3_old, face_b, face_b_old)
            store(column - 2, axial_own(v4, load(1, column - 2)))
        return v1, face_a, v3, face_b

    state = (None, None, None, None)
    for stage in range(6):
        state = step(LOWEST + stage, state, stage)
    stage = 6
    for start, stop, before in segments or ():
        before()
        state = lax.fori_loop(start, stop, lambda column, s: step(column, s, 6), state, unroll=4)
        stage = stop - LOWEST
    for stage in range(stage, count):
        state = step(LOWEST + stage, state, stage)


def fill_halos(halos, entries, source):
    for tile, field, plane, count, row in entries:
        rows = pl.ds((-count - LOWEST) * 8 + plane_slot(plane), count + COLS, stride=8)
        halos[field].at[tile][rows, :] = source[row : row + count + COLS, :]


def row_slice(column):
    return pl.ds(column * 8 if isinstance(column, int) else pl.multiple_of(column * 8, 8), 8)


def loaders(fields, left, halos, tiles):
    def load_own(field, column):
        if isinstance(column, int) and column < 0:
            return left[row_slice(LEFT.index((field, column))), pl.ds(0, tiles * 128)]
        return fields[field][row_slice(column), :]

    def load_halo(field, column):
        parts = [halos[field].at[tile][row_slice(column - LOWEST), :] for tile in range(tiles)]
        return jnp.concatenate(parts, axis=1) if tiles > 1 else parts[0]

    return load_own, load_halo


def near_kernel(*refs):
    fields, (below, above, left, crossing, _, _, out), halos, swept = refs[:4], refs[4:11], refs[11:15], refs[15]
    fill_halos(halos, NEAR_BELOW, below)
    fill_halos(halos, NEAR_ABOVE, above)

    def store(column, values):
        swept[row_slice(column + 2), :] = values

    sweep(COLS + 4, *loaders(fields, left, halos, 1), store, 128)
    turned = swept[...].T
    out[pl.ds(0, R_AX, stride=4), :] = turned[:R_AX, :128]
    out[pl.ds(1, R_AX, stride=4), :] = turned[:R_AX, 128:]
    out[pl.ds(2, R_AX, stride=4), :] = crossing[:R_AX, :]
    out[pl.ds(3, R_AX, stride=4), :] = crossing[R_AX:, :]


def fill_far_halos(halos, near_below, near_above, below, above):
    for entries, source in ((NEAR_BELOW, near_below), (NEAR_ABOVE, near_above), (FAR_BELOW, below), (FAR_ABOVE, above)):
        fill_halos(halos, entries, source)


def far_first_kernel(*refs):
    sources, planes, (left, out), halos = refs[:4], refs[4:8], refs[8:10], refs[10:14]
    fields, semaphores = refs[14:18], refs[18]
    copies = copy_all([(f.at[pl.ds(0, 16), :], held) for f, held in zip(sources, fields)], semaphores)
    fill_far_halos(halos, *planes)
    for copy in copies:
        copy.wait()

    def store(column, values):
        out[row_slice(column + 2), :] = values

    sweep(6, *loaders(fields, left, halos, TILES), store, NR)


def far_kernel(*refs):
    sources, planes, (left, result, first_tile), halos = refs[:4], refs[4:8], refs[8:11], refs[11:15]
    fields, (out, semaphores) = refs[15:19], refs[19:]
    arrive = [(0, 80), (80, 144), (144, 208), (208, 256)]
    leave = [(0, 64), (64, 128), (128, 192), (192, KEPT)]
    incoming = [
        copy_all([(f.at[pl.ds(a, b - a), :], held.at[pl.ds(a, b - a), :]) for f, held in zip(sources, fields)], semaphores, 4 * k)
        for k, (a, b) in enumerate(arrive)
    ]
    outgoing = []
    fill_far_halos(halos, *planes)

    def store(column, values):
        if not isinstance(column, int) or column >= 0:
            out[row_slice(column), :] = values
            first_tile[row_slice(column), :] = values[:, :128]

    def send(piece):
        a, b = leave[piece]
        pairs = [(out.at[pl.ds(a, b - a), :], result.at[pl.ds(a, b - a), :])]
        outgoing.extend(copy_all(pairs, semaphores, 16 + piece))

    def pause(piece):
        for copy in incoming[piece]:
            copy.wait()
        if piece:
            send(piece - 1)

    for copy in incoming[0]:
        copy.wait()
    segments = [(2, 10, lambda: None)] + [(8 * k + 2, min(8 * k + 10, 30), functools.partial(pause, k)) for k in (1, 2, 3)]
    sweep(COLS + 4, *loaders(fields, left, halos, TILES), store, NR, segments)
    send(3)
    for copy in outgoing:
        copy.wait()


def pieces(values, count):
    out = []
    for _ in range(count):
        piece = values.astype(BF16)
        out.append(piece)
        values = values - piece.astype(F32)
    return out


def mm(a, b, dims=((1,), (0,))):
    return lax.dot_general(a, b, (dims, ((), ())), preferred_element_type=F32)


def plic_volume(plane_code, strip_width):
    normal = lax.shift_right_logical(plane_code, 6).astype(F32)
    offset = lax.bitwise_and(plane_code, 63).astype(F32)
    plane_angle = math.pi / 16 + (normal + 0.5) * (3 * math.pi / 512)
    normal_along = jnp.cos(plane_angle)
    across = jnp.sin(plane_angle)
    plane_level = (offset + 0.5) * (normal_along + across) / 64.0
    strip_span = strip_width * normal_along

    def square(shift_value):
        positive = jnp.maximum(shift_value, 0.0)
        return positive * positive

    strip_area = (
        square(plane_level)
        - square(plane_level - strip_span)
        - square(plane_level - across)
        + square(plane_level - strip_span - across)
    ) / (2.0 * strip_span * across)
    return strip_width * strip_area


def crossing_kernel(*refs):
    (code, width, reader, landing), fields, tables, (out, volume_out) = refs[:4], refs[4:8], refs[8:15], refs[15:17]
    sources = [f.at[:, pl.ds(0, 128)] for f in fields] + list(tables)
    copies = copy_all(zip(sources, refs[17:28]), refs[28])
    iota = functools.partial(lax.broadcasted_iota, jnp.int32)
    volume = plic_volume(code[...], width[...])
    both = jnp.concatenate([reader[...].astype(F32), landing[...].astype(F32)], axis=0).astype(BF16)
    column_of_row = (iota((ROWS, COLS), 0) // 8 == iota((ROWS, COLS), 1)).astype(F32).astype(BF16)
    spread = mm(column_of_row, both, ((1,), (1,)))
    row16, lane16 = iota((ROWS, 16), 0), iota((ROWS, 16), 1)
    reader_rows = jnp.sum(jnp.where(lane16 == row16 % 8, spread, 0.0), axis=1, keepdims=True)
    landing_rows = jnp.sum(jnp.where(lane16 == row16 % 8 + 8, spread, 0.0), axis=1, keepdims=True)
    across = mm(both, column_of_row, ((1,), (1,)))
    reader_lanes = jnp.sum(
        jnp.where(iota((16, ROWS), 0) == iota((16, ROWS), 1) % 8, across, 0.0), axis=0, keepdims=True
    )
    same = (reader_rows == reader_lanes) & (iota((ROWS, ROWS), 1) < iota((ROWS, ROWS), 0))
    rank = jnp.sum(jnp.where(same, 1.0, 0.0), axis=1, keepdims=True)

    row, lane = iota((ROWS, 128), 0), iota((ROWS, 128), 1)
    wide = jnp.broadcast_to(volume[:, None, :], (COLS, PLANES, 128)).reshape(ROWS, 128)
    own = jnp.where(lane // 16 == row % 8, wide, 0.0)
    repeat = (iota((128, 128), 0) % 16 == iota((128, 128), 1) % 16).astype(F32).astype(BF16)
    rows_of_volume = sum(mm(piece, repeat) for piece in pieces(own, 3))
    volume_out[...] = rows_of_volume.T[:XR, :]
    chosen = (reader_lanes == iota((R_AX, ROWS), 0).astype(F32)).astype(F32).astype(BF16)
    slotted = jnp.where((lane // 16).astype(F32) == rank, rows_of_volume, 0.0)
    out[:R_AX, :] = sum(mm(chosen, piece) for piece in pieces(slotted, 3))
    target = landing_rows * 8.0 + (row % 8).astype(F32) + 1.0
    marked = jnp.where(lane.astype(F32) == rank, target, 0.0)
    out[R_AX:, :] = mm(chosen, marked.astype(BF16))
    for copy in copies:
        copy.wait()


def arrival_kernel(received, volume, out):
    values = received[pl.ds(2, R_AX, stride=4), :]
    targets = received[pl.ds(3, R_AX, stride=4), :]
    turned = values.T
    row = lax.broadcasted_iota(jnp.int32, (R_AX, ROWS), 1).astype(F32) + 1.0
    total = -volume[...]
    for slot in range(SLOTS):
        chosen = (targets[:, slot : slot + 1] == row).astype(F32).astype(BF16)
        for piece in pieces(turned[slot * XR : (slot + 1) * XR, :], 3):
            total += mm(piece, chosen)
    out[...] = total


def halves(table):
    high = table.astype(ml_dtypes.bfloat16)
    low = (table - high.astype(np.float64)).astype(ml_dtypes.bfloat16)
    return high, low


def filter_tables():
    outer, sector = np.arange(33)[:, None], np.arange(64)[None, :]
    phase = 2 * np.pi * (outer * sector % 64) / 64
    first = np.zeros((2 * KD, 64))
    first[:33], first[KD : KD + 33] = np.cos(phase), -np.sin(phase)
    weight = np.where((outer == 0) | (outer == 32), 1.0, 2.0) / 2048
    last = np.zeros((64, 2 * KD))
    last[:, :33], last[:, KD : KD + 33] = (weight * np.cos(phase)).T, (-weight * np.sin(phase)).T
    column, plane = np.arange(ROWS) // PLANES, np.arange(ROWS) % PLANES
    inner = 2 * np.pi * (column[:, None] * column[None, :] % 32) / 32
    same = plane[:, None] == plane[None, :]
    block = np.concatenate([np.where(same, np.cos(inner), 0.0), np.where(same, -np.sin(inner), 0.0)], axis=1)
    turn = 2 * np.pi * np.arange(KD)[:, None] * column[None, :] / 2048
    mode = np.arange(KD)[:, None] + 64 * column[None, :]
    shift = 2 * np.pi * (2 * mode % 2048) / 2048
    turns = [np.cos(turn), -np.sin(turn), np.cos(shift), np.sin(shift)]
    twiddle = np.concatenate(turns, axis=0).astype(np.float32)
    return (*halves(first), *halves(block), twiddle, *halves(last))


def dot3(a, b):
    (ah, al), (bh, bl) = a, b
    return mm(ah, bh) + (mm(al, bh) + mm(ah, bl))


def filter_kernel(received, first_h, first_l, block_h, block_l, twiddle, last_h, last_l, out):
    sectors = jnp.concatenate(
        [received[pl.ds(0, R_AX, stride=4), :], received[pl.ds(1, R_AX, stride=4), :]], axis=1
    )
    outer = dot3((first_h[...], first_l[...]), pieces(sectors, 2))
    re, im = outer[:KD], outer[KD:]
    t_re, t_im, s_re, s_im = (twiddle[k * KD : (k + 1) * KD, :] for k in range(4))
    turned = jnp.concatenate([re * t_re - im * t_im, re * t_im + im * t_re], axis=0)
    block = (block_h[...], block_l[...])
    inner = dot3(pieces(turned, 2), block)
    re = inner[:KD, :ROWS] - inner[KD:, ROWS:]
    im = inner[:KD, ROWS:] + inner[KD:, :ROWS]
    re, im = re * s_re - im * s_im, re * s_im + im * s_re
    mode = lax.broadcasted_iota(jnp.int32, (KD, ROWS), 0) + 64 * (
        lax.broadcasted_iota(jnp.int32, (KD, ROWS), 1) // PLANES
    )
    folded = jnp.minimum(mode, 2048 - mode).astype(F32)
    cutoff = (lax.axis_index("az") + 1).astype(F32) * 2.0
    scaled = folded / cutoff
    damped = jnp.exp(-(scaled * scaled))
    back = dot3(pieces(jnp.concatenate([re * damped, im * damped], axis=0), 2), block)
    re = back[:KD, :ROWS] + back[KD:, ROWS:]
    im = back[KD:, :ROWS] - back[:KD, ROWS:]
    turned = jnp.concatenate([re * t_re + im * t_im, im * t_re - re * t_im], axis=0)
    result = dot3((last_h[...], last_l[...]), pieces(turned, 2))
    out[pl.ds(0, R_AX, stride=2), :] = result[:, :128]
    out[pl.ds(1, R_AX, stride=2), :] = result[:, 128:]


def final_kernel(received, delta, swept, last, _, result, out, semaphores):
    rest = (pl.ds(KEPT, ROWS - KEPT), pl.ds(128, NR - 128))
    copy = pltpu.make_async_copy(last.at[:, pl.ds(128, NR - 128)], result.at[rest], semaphores.at[1])
    copy.start()
    near = jnp.concatenate(
        [received[pl.ds(0, R_AX, stride=2), :], received[pl.ds(1, R_AX, stride=2), :]], axis=1
    )
    near = jnp.concatenate([near[:XR] + delta[...], near[XR:], jnp.zeros((R_AX, ROWS), F32)], axis=0)
    cycle = lax.broadcasted_iota(jnp.int32, (ROWS, 128), 1)
    first_tile = jnp.concatenate([swept[...], last[:, :128]], axis=0)
    out[...] = jnp.where(cycle < R_AX, near.T, first_tile)
    copy_out(out, result.at[:, pl.ds(0, 128)], semaphores.at[0])
    copy.wait()


VMEM, HBM = pltpu.VMEM, pltpu.HBM
DMA = pltpu.SemaphoreType.DMA


def call(kernel, inputs, outputs, scratch=(), cost=1.0, aliases=None):
    arrays, specs = [], []
    for given in inputs:
        array, space = given if isinstance(given, tuple) else (given, VMEM)
        arrays.append(pltpu.with_memory_space_constraint(array, HBM) if space is HBM else array)
        specs.append(pl.BlockSpec(memory_space=space))
    out_specs = [pl.BlockSpec(memory_space=getattr(o, "memory_space", VMEM)) for o in outputs]
    return pl.pallas_call(
        kernel,
        in_specs=specs,
        out_specs=out_specs,
        out_shape=list(outputs),
        scratch_shapes=list(scratch),
        input_output_aliases=aliases or {},
        cost_estimate=pl.CostEstimate(flops=int(cost * 1e6), bytes_accessed=int(cost * 3e6), transcendentals=0),
        compiler_params=pltpu.CompilerParams(vmem_limit_bytes=16 * 1024 * 1024),
    )(*arrays)


def free(*dims):
    return jax.ShapeDtypeStruct(dims, F32)


def local(
    fraction,
    courant_axial,
    courant_azimuth,
    courant_radial,
    plane_code,
    strip_width,
    tile_reader,
    landing_column,
):
    ax_count, az_count = lax.axis_size("ax"), lax.axis_size("az")
    higher_ax, higher_az = ([(i, (i + 1) % n) for i in range(n)] for n in (ax_count, az_count))
    lower_ax, lower_az = ([(j, i) for i, j in pairs] for pairs in (higher_ax, higher_az))
    fields = [(a.reshape(ROWS, NR), HBM) for a in (fraction, courant_axial, courant_azimuth, courant_radial)]

    (right,) = call(pack_columns, fields, [VMEM((len(LEFT) * 8, NR), F32)], [DMA((4,))])
    left = lax.ppermute(right, "az", higher_az)

    tables = filter_tables()
    crossing, volume, *held = call(
        crossing_kernel,
        [plane_code, strip_width, tile_reader.T, landing_column.T, *fields, *((jnp.asarray(t), HBM) for t in tables)],
        [VMEM((2 * R_AX, 128), F32), VMEM((XR, ROWS), F32)]
        + [VMEM((ROWS, 128), F32)] * 4
        + [VMEM(t.shape, t.dtype) for t in tables],
        [DMA((4 + len(tables),))],
    )
    near_tiles, held_tables = held[:4], held[4:]

    near_up, near_down = call(
        pack_near_planes,
        [*near_tiles, left],
        [VMEM((NEAR_BELOW_ROWS, 128), F32), VMEM((NEAR_ABOVE_ROWS, 128), F32)],
    )
    near_below = lax.ppermute(near_up, "ax", higher_ax)
    near_above = lax.ppermute(near_down, "ax", lower_ax)
    far_up, far_down = call(
        pack_far_planes,
        [*fields, left],
        [VMEM((FAR_BELOW_ROWS, 128), F32), VMEM((FAR_ABOVE_ROWS, 128), F32)],
        [VMEM(((TILES - 1) * ROWS, 128), F32)] * 4 + [DMA((4 * (TILES - 1),))],
    )
    (send,) = call(
        near_kernel,
        [*near_tiles, near_below, near_above, left, crossing, (far_up, pl.ANY), (far_down, pl.ANY)],
        [free(4 * R_AX, 128)],
        [VMEM((1, 36 * 8, 128), F32)] * 4 + [VMEM((ROWS, 128), F32)],
    )
    got = lax.all_to_all(send.reshape(R_AX, 4, 128), "az", 0, 0, tiled=True).reshape(4 * R_AX, 128)

    far_below = lax.ppermute(far_up, "ax", higher_ax)
    far_above = lax.ppermute(far_down, "ax", lower_ax)
    far_inputs = [*fields, near_below, near_above, far_below, far_above, left]
    far_halos = [VMEM((TILES, 36 * 8, 128), F32)] * 4
    (first_columns,) = call(
        far_first_kernel, far_inputs, [VMEM((16, NR), F32)], far_halos + [VMEM((16, NR), F32)] * 4 + [DMA((4,))]
    )
    last_columns = lax.ppermute(first_columns, "az", lower_az)
    swept, first_tile = call(
        far_kernel,
        far_inputs,
        [HBM((ROWS, NR), F32), VMEM((KEPT, 128), F32)],
        far_halos + [VMEM((ROWS, NR), F32)] * 4 + [VMEM((KEPT, NR), F32), DMA((20,))],
        cost=4.0,
    )

    (back,) = call(filter_kernel, [got, *held_tables], [free(2 * R_AX, 128)])
    returned = lax.all_to_all(back.reshape(R_AX, 2, 128), "az", 0, 0, tiled=True).reshape(2 * R_AX, 128)
    (delta,) = call(arrival_kernel, [got, volume], [VMEM((XR, ROWS), F32)])
    (out,) = call(
        final_kernel,
        [returned, delta, first_tile, last_columns, (swept, HBM)],
        [HBM((ROWS, NR), F32)],
        [VMEM((ROWS, 128), F32), DMA((2,))],
        aliases={4: 0},
    )
    return out.reshape(COLS, PLANES, NR)


def solution(mesh):
    return jax.shard_map(
        local,
        mesh=mesh,
        in_specs=(
            P("az", "ax", None),
            P("az", "ax", None),
            P("az", "ax", None),
            P("az", "ax", None),
            P("az", "ax"),
            P("az", "ax"),
            P("az", "ax"),
            P("az", "ax"),
        ),
        out_specs=P("az", "ax", None),
        check_vma=False,
    )
```

```python
import functools
import math

import jax
import jax.numpy as jnp
import ml_dtypes
import numpy as np
from jax import lax
from jax.experimental import pallas as pl
from jax.experimental.pallas import tpu as pltpu
from jax.sharding import PartitionSpec as P

R_AX = 64
XR = 16
COLS = 32
PLANES = 8
ROWS = COLS * PLANES
NR = 512
SLOTS = 8
KD = 40

F32 = jnp.float32
BF16 = jnp.bfloat16

BELOW = ((0, -2), (0, -1), (1, -2), (1, -1), (2, -1), (3, -1))
ABOVE = ((0, 8), (0, 9), (1, 8), (2, 8), (3, 8))
HALO_PLANES = ((-2, -1, 8, 9), (-2, -1, 8), (-1, 8), (-1, 8))

LOWEST = -4
LEFT = tuple((f, c) for f in range(3) for c in range(-4, 0)) + tuple((3, c) for c in range(-3, 0))
LEFT_COUNT = (4, 4, 4, 3)
TILES = NR // 128
KEPT = ROWS - 16


def halo_layout(planes, tiles):
    entries, row = [], 0
    for tile in tiles:
        for field, plane in planes:
            entries.append((tile, field, plane, LEFT_COUNT[field], row))
            row += LEFT_COUNT[field] + COLS
    return entries, -(-row // 8) * 8


NEAR_BELOW, NEAR_BELOW_ROWS = halo_layout(BELOW, (0,))
NEAR_ABOVE, NEAR_ABOVE_ROWS = halo_layout(ABOVE, (0,))
FAR_BELOW, FAR_BELOW_ROWS = halo_layout(BELOW, range(1, TILES))
FAR_ABOVE, FAR_ABOVE_ROWS = halo_layout(ABOVE, range(1, TILES))


def plane_slot(plane):
    return plane % 16 - 8


def copy_out(source, target, semaphore):
    copy = pltpu.make_async_copy(source, target, semaphore)
    copy.start()
    copy.wait()


def copy_all(pairs, semaphores, first=0):
    copies = [pltpu.make_async_copy(a, b, semaphores.at[first + k]) for k, (a, b) in enumerate(pairs)]
    for copy in copies:
        copy.start()
    return copies


def pack_columns(*refs):
    fields, (right, semaphores) = refs[:4], refs[-2:]
    lanes = right.shape[1]
    pairs, row = [], 0
    for field, count in zip(fields, LEFT_COUNT):
        source = field.at[pl.ds(ROWS - count * 8, count * 8), pl.ds(0 if lanes == 128 else NR - lanes, lanes)]
        pairs.append((source, right.at[pl.ds(row, count * 8), :]))
        row += count * 8
    for copy in copy_all(pairs, semaphores):
        copy.wait()


def pack_planes(entries, out, shift, load, left):
    for tile, field, plane, count, row in entries:
        for at in range(count):
            origin = LEFT.index((field, at - count)) * 8 + plane + shift
            out[row + at : row + at + 1, :] = left[origin : origin + 1, pl.ds(max(tile - 1, 0) * 128, 128)]
        out[row + count : row + count + COLS, :] = load(tile, field, plane + shift)
    used = entries[-1][4] + entries[-1][3] + COLS
    if used < out.shape[0]:
        out[used:, :] = jnp.zeros((out.shape[0] - used, 128), F32)


def pack_near_planes(*refs):
    tiles, (left, up, down) = refs[:4], refs[4:]

    def load(_, field, plane):
        return tiles[field][pl.ds(plane, COLS, stride=PLANES), :]

    pack_planes(NEAR_BELOW, up, PLANES, load, left)
    pack_planes(NEAR_ABOVE, down, -PLANES, load, left)


def pack_far_planes(*refs):
    fields, (left, up, down, *tiles, semaphores) = refs[:4], refs[4:]
    pairs = []
    for field, tile in zip(fields, tiles):
        for k in range(1, TILES):
            pairs.append((field.at[:, pl.ds(k * 128, 128)], tile.at[pl.ds((k - 1) * ROWS, ROWS), :]))
    for copy in copy_all(pairs, semaphores):
        copy.wait()

    def load(tile, field, plane):
        return tiles[field][pl.ds((tile - 1) * ROWS + plane, COLS, stride=PLANES), :]

    pack_planes(FAR_BELOW, up, PLANES, load, left)
    pack_planes(FAR_ABOVE, down, -PLANES, load, left)


def upwind(courant, below_cell, above_cell):
    return courant * jnp.where(courant > 0.0, below_cell, above_cell)


def sweep(count, load_own, load_halo, store, lanes, segments=None):
    plane = lax.broadcasted_iota(jnp.int32, (8, lanes), 0)
    cycle = lax.broadcasted_iota(jnp.int32, (8, lanes), 1)
    first, last = plane == 0, plane == 7
    radius = cycle.astype(F32)
    outer_radius = radius + 1.0
    inverse = 1.0 / (radius + 0.5)
    axis_cell, rim_cell = cycle == 0, cycle == NR - 1

    def load(field, column):
        return load_own(field, column), load_halo(field, column)

    def next_plane(pair):
        own, halo = (pltpu.roll(a, 7, 0) for a in pair)
        return jnp.where(last, halo, own), jnp.where(last, own, halo)

    def previous_plane(pair):
        own, halo = (pltpu.roll(a, 1, 0) for a in pair)
        return jnp.where(first, halo, own), jnp.where(first, own, halo)

    def flux(courant, low, high):
        return tuple(upwind(c, a, b) for c, a, b in zip(courant, low, high))

    def update(values, upper, lower):
        return tuple(v - (a - b) for v, a, b in zip(values, upper, lower))

    def axial(values, courant):
        face = flux(courant, values, next_plane(values))
        return update(values, face, previous_plane(face))

    def axial_own(values, courant):
        own, halo = flux(courant, values, next_plane(values))
        lower = jnp.where(first, pltpu.roll(halo, 1, 0), pltpu.roll(own, 1, 0))
        return values[0] - (own - lower)

    def radial_one(values, courant):
        above_cell = jnp.where(rim_cell, 0.0, pltpu.roll(values, lanes - 1, 1))
        outer = outer_radius * upwind(courant, values, above_cell)
        inner = jnp.where(axis_cell, 0.0, pltpu.roll(outer, 1, 1))
        return values - (outer - inner) * inverse

    def radial(values, courant):
        return tuple(radial_one(v, c) for v, c in zip(values, courant))

    def step(column, state, stage):
        v1_old, face_a_old, v3_old, face_b_old = state
        v1 = axial(load(0, column), load(1, column))
        face_a = v3 = face_b = None
        if stage >= 1:
            face_a = flux(load(2, column - 1), v1_old, v1)
        if stage >= 2:
            v2 = update(v1_old, face_a, face_a_old)
            v3 = radial(v2, load(3, column - 1))
        if stage >= 3:
            face_b = flux(load(2, column - 2), v3_old, v3)
        if stage >= 4:
            v4 = update(v3_old, face_b, face_b_old)
            store(column - 2, axial_own(v4, load(1, column - 2)))
        return v1, face_a, v3, face_b

    state = (None, None, None, None)
    for stage in range(6):
        state = step(LOWEST + stage, state, stage)
    stage = 6
    for start, stop, before in segments or ():
        before()
        state = lax.fori_loop(start, stop, lambda column, s: step(column, s, 6), state, unroll=4)
        stage = stop - LOWEST
    for stage in range(stage, count):
        state = step(LOWEST + stage, state, stage)


def fill_halos(halos, entries, source):
    for tile, field, plane, count, row in entries:
        rows = pl.ds((-count - LOWEST) * 8 + plane_slot(plane), count + COLS, stride=8)
        halos[field].at[tile][rows, :] = source[row : row + count + COLS, :]


def row_slice(column):
    return pl.ds(column * 8 if isinstance(column, int) else pl.multiple_of(column * 8, 8), 8)


def loaders(fields, left, halos, tiles):
    def load_own(field, column):
        if isinstance(column, int) and column < 0:
            parts = [part[row_slice(LEFT.index((field, column))), :] for part in left]
            return jnp.concatenate(parts, axis=1) if tiles > 1 else parts[0]
        return fields[field][row_slice(column), :]

    def load_halo(field, column):
        parts = [halos[field].at[tile][row_slice(column - LOWEST), :] for tile in range(tiles)]
        return jnp.concatenate(parts, axis=1) if tiles > 1 else parts[0]

    return load_own, load_halo


def near_kernel(*refs):
    fields, (below, above, left, crossing, out), halos, swept = refs[:4], refs[4:9], refs[9:13], refs[13]
    fill_halos(halos, NEAR_BELOW, below)
    fill_halos(halos, NEAR_ABOVE, above)

    def store(column, values):
        swept[row_slice(column + 2), :] = values

    sweep(COLS + 4, *loaders(fields, [left], halos, 1), store, 128)
    turned = swept[...].T
    out[pl.ds(0, R_AX, stride=4), :] = turned[:R_AX, :128]
    out[pl.ds(1, R_AX, stride=4), :] = turned[:R_AX, 128:]
    out[pl.ds(2, R_AX, stride=4), :] = crossing[:R_AX, :]
    out[pl.ds(3, R_AX, stride=4), :] = crossing[R_AX:, :]


def fill_far_halos(halos, near_below, near_above, below, above):
    for entries, source in ((NEAR_BELOW, near_below), (NEAR_ABOVE, near_above), (FAR_BELOW, below), (FAR_ABOVE, above)):
        fill_halos(halos, entries, source)


def far_first_kernel(*refs):
    sources, planes, left, out, halos = refs[:4], refs[4:8], refs[8:10], refs[10], refs[11:15]
    fields, semaphores = refs[15:19], refs[19]
    copies = copy_all([(f.at[pl.ds(0, 16), :], held) for f, held in zip(sources, fields)], semaphores)
    fill_far_halos(halos, *planes)
    for copy in copies:
        copy.wait()

    def store(column, values):
        out[row_slice(column + 2), :] = values

    sweep(6, *loaders(fields, left, halos, TILES), store, NR)


def far_kernel(*refs):
    sources, planes, left, (result, first_tile), halos = refs[:4], refs[4:8], refs[8:10], refs[10:12], refs[12:16]
    fields, (out, semaphores) = refs[16:20], refs[20:]
    arrive = [(0, 80), (80, 144), (144, 208), (208, 256)]
    leave = [(0, 64), (64, 128), (128, 192), (192, KEPT)]
    incoming = [
        copy_all([(f.at[pl.ds(a, b - a), :], held.at[pl.ds(a, b - a), :]) for f, held in zip(sources, fields)], semaphores, 4 * k)
        for k, (a, b) in enumerate(arrive)
    ]
    outgoing = []
    fill_far_halos(halos, *planes)

    def store(column, values):
        if not isinstance(column, int) or column >= 0:
            out[row_slice(column), :] = values
            first_tile[row_slice(column), :] = values[:, :128]

    def send(piece):
        a, b = leave[piece]
        pairs = [(out.at[pl.ds(a, b - a), :], result.at[pl.ds(a, b - a), :])]
        outgoing.extend(copy_all(pairs, semaphores, 16 + piece))

    def pause(piece):
        for copy in incoming[piece]:
            copy.wait()
        if piece:
            send(piece - 1)

    for copy in incoming[0]:
        copy.wait()
    segments = [(2, 10, lambda: None)] + [(8 * k + 2, min(8 * k + 10, 30), functools.partial(pause, k)) for k in (1, 2, 3)]
    sweep(COLS + 4, *loaders(fields, left, halos, TILES), store, NR, segments)
    send(3)
    for copy in outgoing:
        copy.wait()


def pieces(values, count):
    out = []
    for _ in range(count):
        piece = values.astype(BF16)
        out.append(piece)
        values = values - piece.astype(F32)
    return out


def mm(a, b, dims=((1,), (0,))):
    return lax.dot_general(a, b, (dims, ((), ())), preferred_element_type=F32)


def plic_volume(plane_code, strip_width):
    normal = lax.shift_right_logical(plane_code, 6).astype(F32)
    offset = lax.bitwise_and(plane_code, 63).astype(F32)
    plane_angle = math.pi / 16 + (normal + 0.5) * (3 * math.pi / 512)
    normal_along = jnp.cos(plane_angle)
    across = jnp.sin(plane_angle)
    plane_level = (offset + 0.5) * (normal_along + across) / 64.0
    strip_span = strip_width * normal_along

    def square(shift_value):
        positive = jnp.maximum(shift_value, 0.0)
        return positive * positive

    strip_area = (
        square(plane_level)
        - square(plane_level - strip_span)
        - square(plane_level - across)
        + square(plane_level - strip_span - across)
    ) / (2.0 * strip_span * across)
    return strip_width * strip_area


def crossing_kernel(*refs):
    (code, width, reader, landing), fields, tables, (out, volume_out) = refs[:4], refs[4:8], refs[8:15], refs[15:17]
    sources = [f.at[:, pl.ds(0, 128)] for f in fields] + list(tables)
    copies = copy_all(zip(sources, refs[17:28]), refs[28])
    iota = functools.partial(lax.broadcasted_iota, jnp.int32)
    volume = plic_volume(code[...], width[...])
    both = jnp.concatenate([reader[...].astype(F32), landing[...].astype(F32)], axis=0).astype(BF16)
    column_of_row = (iota((ROWS, COLS), 0) // 8 == iota((ROWS, COLS), 1)).astype(F32).astype(BF16)
    spread = mm(column_of_row, both, ((1,), (1,)))
    row16, lane16 = iota((ROWS, 16), 0), iota((ROWS, 16), 1)
    reader_rows = jnp.sum(jnp.where(lane16 == row16 % 8, spread, 0.0), axis=1, keepdims=True)
    landing_rows = jnp.sum(jnp.where(lane16 == row16 % 8 + 8, spread, 0.0), axis=1, keepdims=True)
    across = mm(both, column_of_row, ((1,), (1,)))
    reader_lanes = jnp.sum(
        jnp.where(iota((16, ROWS), 0) == iota((16, ROWS), 1) % 8, across, 0.0), axis=0, keepdims=True
    )
    same = (reader_rows == reader_lanes) & (iota((ROWS, ROWS), 1) < iota((ROWS, ROWS), 0))
    rank = jnp.sum(jnp.where(same, 1.0, 0.0), axis=1, keepdims=True)

    row, lane = iota((ROWS, 128), 0), iota((ROWS, 128), 1)
    wide = jnp.broadcast_to(volume[:, None, :], (COLS, PLANES, 128)).reshape(ROWS, 128)
    own = jnp.where(lane // 16 == row % 8, wide, 0.0)
    repeat = (iota((128, 128), 0) % 16 == iota((128, 128), 1) % 16).astype(F32).astype(BF16)
    rows_of_volume = sum(mm(piece, repeat) for piece in pieces(own, 3))
    volume_out[...] = rows_of_volume.T[:XR, :]
    chosen = (reader_lanes == iota((R_AX, ROWS), 0).astype(F32)).astype(F32).astype(BF16)
    slotted = jnp.where((lane // 16).astype(F32) == rank, rows_of_volume, 0.0)
    out[:R_AX, :] = sum(mm(chosen, piece) for piece in pieces(slotted, 3))
    target = landing_rows * 8.0 + (row % 8).astype(F32) + 1.0
    marked = jnp.where(lane.astype(F32) == rank, target, 0.0)
    out[R_AX:, :] = mm(chosen, marked.astype(BF16))
    for copy in copies:
        copy.wait()


def arrival_kernel(received, volume, out):
    values = received[pl.ds(2, R_AX, stride=4), :]
    targets = received[pl.ds(3, R_AX, stride=4), :]
    turned = values.T
    row = lax.broadcasted_iota(jnp.int32, (R_AX, ROWS), 1).astype(F32) + 1.0
    total = -volume[...]
    for slot in range(SLOTS):
        chosen = (targets[:, slot : slot + 1] == row).astype(F32).astype(BF16)
        for piece in pieces(turned[slot * XR : (slot + 1) * XR, :], 3):
            total += mm(piece, chosen)
    out[...] = total


def halves(table):
    high = table.astype(ml_dtypes.bfloat16)
    low = (table - high.astype(np.float64)).astype(ml_dtypes.bfloat16)
    return high, low


def filter_tables():
    outer, sector = np.arange(33)[:, None], np.arange(64)[None, :]
    phase = 2 * np.pi * (outer * sector % 64) / 64
    first = np.zeros((2 * KD, 64))
    first[:33], first[KD : KD + 33] = np.cos(phase), -np.sin(phase)
    weight = np.where((outer == 0) | (outer == 32), 1.0, 2.0) / 2048
    last = np.zeros((64, 2 * KD))
    last[:, :33], last[:, KD : KD + 33] = (weight * np.cos(phase)).T, (-weight * np.sin(phase)).T
    column, plane = np.arange(ROWS) // PLANES, np.arange(ROWS) % PLANES
    inner = 2 * np.pi * (column[:, None] * column[None, :] % 32) / 32
    same = plane[:, None] == plane[None, :]
    block = np.concatenate([np.where(same, np.cos(inner), 0.0), np.where(same, -np.sin(inner), 0.0)], axis=1)
    turn = 2 * np.pi * np.arange(KD)[:, None] * column[None, :] / 2048
    mode = np.arange(KD)[:, None] + 64 * column[None, :]
    shift = 2 * np.pi * (2 * mode % 2048) / 2048
    turns = [np.cos(turn), -np.sin(turn), np.cos(shift), np.sin(shift)]
    twiddle = np.concatenate(turns, axis=0).astype(np.float32)
    return (*halves(first), *halves(block), twiddle, *halves(last))


def dot3(a, b):
    (ah, al), (bh, bl) = a, b
    rows = ah.shape[0]
    both = mm(jnp.concatenate([ah, al], axis=0), bh)
    return both[:rows] + (both[rows:] + mm(ah, bl))


def filter_kernel(received, first_h, first_l, block_h, block_l, twiddle, last_h, last_l, out):
    sectors = jnp.concatenate(
        [received[pl.ds(0, R_AX, stride=4), :], received[pl.ds(1, R_AX, stride=4), :]], axis=1
    )
    outer = dot3((first_h[...], first_l[...]), pieces(sectors, 2))
    re, im = outer[:KD], outer[KD:]
    t_re, t_im, s_re, s_im = (twiddle[k * KD : (k + 1) * KD, :] for k in range(4))
    turned = jnp.concatenate([re * t_re - im * t_im, re * t_im + im * t_re], axis=0)
    block = (block_h[...], block_l[...])
    inner = dot3(pieces(turned, 2), block)
    re = inner[:KD, :ROWS] - inner[KD:, ROWS:]
    im = inner[:KD, ROWS:] + inner[KD:, :ROWS]
    re, im = re * s_re - im * s_im, re * s_im + im * s_re
    mode = lax.broadcasted_iota(jnp.int32, (KD, ROWS), 0) + 64 * (
        lax.broadcasted_iota(jnp.int32, (KD, ROWS), 1) // PLANES
    )
    folded = jnp.minimum(mode, 2048 - mode).astype(F32)
    cutoff = (lax.axis_index("az") + 1).astype(F32) * 2.0
    scaled = folded / cutoff
    damped = jnp.exp(-(scaled * scaled))
    back = dot3(pieces(jnp.concatenate([re * damped, im * damped], axis=0), 2), block)
    re = back[:KD, :ROWS] + back[KD:, ROWS:]
    im = back[KD:, :ROWS] - back[:KD, ROWS:]
    turned = jnp.concatenate([re * t_re + im * t_im, im * t_re - re * t_im], axis=0)
    result = dot3((last_h[...], last_l[...]), pieces(turned, 2))
    out[pl.ds(0, R_AX, stride=2), :] = result[:, :128]
    out[pl.ds(1, R_AX, stride=2), :] = result[:, 128:]


def final_kernel(received, delta, swept, last, _, result, out, semaphores):
    rest = (pl.ds(KEPT, ROWS - KEPT), pl.ds(128, NR - 128))
    copy = pltpu.make_async_copy(last.at[:, pl.ds(128, NR - 128)], result.at[rest], semaphores.at[1])
    copy.start()
    near = jnp.concatenate(
        [received[pl.ds(0, R_AX, stride=2), :], received[pl.ds(1, R_AX, stride=2), :]], axis=1
    )
    near = jnp.concatenate([near[:XR] + delta[...], near[XR:], jnp.zeros((R_AX, ROWS), F32)], axis=0)
    cycle = lax.broadcasted_iota(jnp.int32, (ROWS, 128), 1)
    first_tile = jnp.concatenate([swept[...], last[:, :128]], axis=0)
    out[...] = jnp.where(cycle < R_AX, near.T, first_tile)
    copy_out(out, result.at[:, pl.ds(0, 128)], semaphores.at[0])
    copy.wait()


VMEM, HBM = pltpu.VMEM, pltpu.HBM
DMA = pltpu.SemaphoreType.DMA


def call(kernel, inputs, outputs, scratch=(), cost=1.0, aliases=None):
    arrays, specs = [], []
    for given in inputs:
        array, space = given if isinstance(given, tuple) else (given, VMEM)
        arrays.append(pltpu.with_memory_space_constraint(array, HBM) if space is HBM else array)
        specs.append(pl.BlockSpec(memory_space=space))
    out_specs = [pl.BlockSpec(memory_space=getattr(o, "memory_space", VMEM)) for o in outputs]
    return pl.pallas_call(
        kernel,
        in_specs=specs,
        out_specs=out_specs,
        out_shape=list(outputs),
        scratch_shapes=list(scratch),
        input_output_aliases=aliases or {},
        cost_estimate=pl.CostEstimate(flops=int(cost * 1e6), bytes_accessed=int(cost * 3e6), transcendentals=0),
        compiler_params=pltpu.CompilerParams(vmem_limit_bytes=16 * 1024 * 1024),
    )(*arrays)


def free(*dims):
    return jax.ShapeDtypeStruct(dims, F32)


def local(
    fraction,
    courant_axial,
    courant_azimuth,
    courant_radial,
    plane_code,
    strip_width,
    tile_reader,
    landing_column,
):
    ax_count, az_count = lax.axis_size("ax"), lax.axis_size("az")
    higher_ax, higher_az = ([(i, (i + 1) % n) for i in range(n)] for n in (ax_count, az_count))
    lower_ax, lower_az = ([(j, i) for i, j in pairs] for pairs in (higher_ax, higher_az))
    fields = [(a.reshape(ROWS, NR), HBM) for a in (fraction, courant_axial, courant_azimuth, courant_radial)]

    (near_right,) = call(pack_columns, fields, [VMEM((len(LEFT) * 8, 128), F32)], [DMA((4,))])
    near_left = lax.ppermute(near_right, "az", higher_az)

    tables = filter_tables()
    crossing, volume, *held = call(
        crossing_kernel,
        [plane_code, strip_width, tile_reader.T, landing_column.T, *fields, *((jnp.asarray(t), HBM) for t in tables)],
        [VMEM((2 * R_AX, 128), F32), VMEM((XR, ROWS), F32)]
        + [VMEM((ROWS, 128), F32)] * 4
        + [VMEM(t.shape, t.dtype) for t in tables],
        [DMA((4 + len(tables),))],
    )
    near_tiles, held_tables = held[:4], held[4:]

    near_up, near_down = call(
        pack_near_planes,
        [*near_tiles, near_left],
        [VMEM((NEAR_BELOW_ROWS, 128), F32), VMEM((NEAR_ABOVE_ROWS, 128), F32)],
    )
    near_below = lax.ppermute(near_up, "ax", higher_ax)
    near_above = lax.ppermute(near_down, "ax", lower_ax)
    (far_right,) = call(
        pack_columns, [*fields, (near_up, pl.ANY)], [VMEM((len(LEFT) * 8, NR - 128), F32)], [DMA((4,))]
    )
    far_left = lax.ppermute(far_right, "az", higher_az)
    far_up, far_down = call(
        pack_far_planes,
        [*fields, far_left],
        [VMEM((FAR_BELOW_ROWS, 128), F32), VMEM((FAR_ABOVE_ROWS, 128), F32)],
        [VMEM(((TILES - 1) * ROWS, 128), F32)] * 4 + [DMA((4 * (TILES - 1),))],
    )
    (send,) = call(
        near_kernel,
        [*near_tiles, near_below, near_above, near_left, crossing],
        [free(4 * R_AX, 128)],
        [VMEM((1, 36 * 8, 128), F32)] * 4 + [VMEM((ROWS, 128), F32)],
    )
    got = lax.all_to_all(send.reshape(R_AX, 4, 128), "az", 0, 0, tiled=True).reshape(4 * R_AX, 128)

    far_below = lax.ppermute(far_up, "ax", higher_ax)
    far_above = lax.ppermute(far_down, "ax", lower_ax)
    far_inputs = [*fields, near_below, near_above, far_below, far_above, near_left, far_left]
    far_halos = [VMEM((TILES, 36 * 8, 128), F32)] * 4
    (first_columns,) = call(
        far_first_kernel, far_inputs, [VMEM((16, NR), F32)], far_halos + [VMEM((16, NR), F32)] * 4 + [DMA((4,))]
    )
    last_columns = lax.ppermute(first_columns, "az", lower_az)
    swept, first_tile = call(
        far_kernel,
        far_inputs,
        [HBM((ROWS, NR), F32), VMEM((KEPT, 128), F32)],
        far_halos + [VMEM((ROWS, NR), F32)] * 4 + [VMEM((KEPT, NR), F32), DMA((20,))],
        cost=4.0,
    )

    (back,) = call(filter_kernel, [got, *held_tables], [free(2 * R_AX, 128)])
    returned = lax.all_to_all(back.reshape(R_AX, 2, 128), "az", 0, 0, tiled=True).reshape(2 * R_AX, 128)
    (delta,) = call(arrival_kernel, [got, volume], [VMEM((XR, ROWS), F32)])
    (out,) = call(
        final_kernel,
        [returned, delta, first_tile, last_columns, (swept, HBM)],
        [HBM((ROWS, NR), F32)],
        [VMEM((ROWS, 128), F32), DMA((2,))],
        aliases={4: 0},
    )
    return out.reshape(COLS, PLANES, NR)


def solution(mesh):
    return jax.shard_map(
        local,
        mesh=mesh,
        in_specs=(
            P("az", "ax", None),
            P("az", "ax", None),
            P("az", "ax", None),
            P("az", "ax", None),
            P("az", "ax"),
            P("az", "ax"),
            P("az", "ax"),
            P("az", "ax"),
        ),
        out_specs=P("az", "ax", None),
        check_vma=False,
    )
```

```python
import functools
import math

import jax
import jax.numpy as jnp
import ml_dtypes
import numpy as np
from jax import lax
from jax.experimental import pallas as pl
from jax.experimental.pallas import tpu as pltpu
from jax.sharding import PartitionSpec as P

R_AX = 64
XR = 16
COLS = 32
PLANES = 8
ROWS = COLS * PLANES
NR = 512
SLOTS = 8
KD = 40

F32 = jnp.float32
BF16 = jnp.bfloat16

BELOW = ((0, -2), (0, -1), (1, -2), (1, -1), (2, -1), (3, -1))
ABOVE = ((0, 8), (0, 9), (1, 8), (2, 8), (3, 8))
HALO_PLANES = ((-2, -1, 8, 9), (-2, -1, 8), (-1, 8), (-1, 8))

LOWEST = -4
LEFT = tuple((f, c) for f in range(3) for c in range(-4, 0)) + tuple((3, c) for c in range(-3, 0))
LEFT_COUNT = (4, 4, 4, 3)
TILES = NR // 128
KEPT = ROWS - 16


def halo_layout(planes, tiles):
    entries, row = [], 0
    for tile in tiles:
        for field, plane in planes:
            entries.append((tile, field, plane, LEFT_COUNT[field], row))
            row += LEFT_COUNT[field] + COLS
    return entries, -(-row // 8) * 8


NEAR_BELOW, NEAR_BELOW_ROWS = halo_layout(BELOW, (0,))
NEAR_ABOVE, NEAR_ABOVE_ROWS = halo_layout(ABOVE, (0,))
FAR_BELOW, FAR_BELOW_ROWS = halo_layout(BELOW, range(1, TILES))
FAR_ABOVE, FAR_ABOVE_ROWS = halo_layout(ABOVE, range(1, TILES))


def plane_slot(plane):
    return plane % 16 - 8


def copy_out(source, target, semaphore):
    copy = pltpu.make_async_copy(source, target, semaphore)
    copy.start()
    copy.wait()


def copy_all(pairs, semaphores, first=0):
    copies = [pltpu.make_async_copy(a, b, semaphores.at[first + k]) for k, (a, b) in enumerate(pairs)]
    for copy in copies:
        copy.start()
    return copies


def bring_tiles(*refs):
    fields, tiles, (right, semaphores) = refs[:4], refs[4:8], refs[8:]
    copies = copy_all([(f.at[:, pl.ds(0, 128)], tile) for f, tile in zip(fields, tiles)], semaphores, 4)
    pack_columns(*fields, right, semaphores)
    for copy in copies:
        copy.wait()


def pack_columns(*refs):
    fields, (right, semaphores) = refs[:4], refs[4:]
    lanes = right.shape[1]
    pairs, row = [], 0
    for field, count in zip(fields, LEFT_COUNT):
        source = field.at[pl.ds(ROWS - count * 8, count * 8), pl.ds(0 if lanes == 128 else NR - lanes, lanes)]
        pairs.append((source, right.at[pl.ds(row, count * 8), :]))
        row += count * 8
    for copy in copy_all(pairs, semaphores):
        copy.wait()


def pack_planes(entries, out, shift, load, left):
    for tile, field, plane, count, row in entries:
        for at in range(count):
            origin = LEFT.index((field, at - count)) * 8 + plane + shift
            out[row + at : row + at + 1, :] = left[origin : origin + 1, pl.ds(max(tile - 1, 0) * 128, 128)]
        out[row + count : row + count + COLS, :] = load(tile, field, plane + shift)
    used = entries[-1][4] + entries[-1][3] + COLS
    if used < out.shape[0]:
        out[used:, :] = jnp.zeros((out.shape[0] - used, 128), F32)


def pack_near_planes(*refs):
    tiles, (left, up, down) = refs[:4], refs[4:]

    def load(_, field, plane):
        return tiles[field][pl.ds(plane, COLS, stride=PLANES), :]

    pack_planes(NEAR_BELOW, up, PLANES, load, left)
    pack_planes(NEAR_ABOVE, down, -PLANES, load, left)


def pack_far_planes(*refs):
    fields, (left, up, down, *tiles, semaphores) = refs[:4], refs[4:]
    pairs = []
    for field, tile in zip(fields, tiles):
        for k in range(1, TILES):
            pairs.append((field.at[:, pl.ds(k * 128, 128)], tile.at[pl.ds((k - 1) * ROWS, ROWS), :]))
    for copy in copy_all(pairs, semaphores):
        copy.wait()

    def load(tile, field, plane):
        return tiles[field][pl.ds((tile - 1) * ROWS + plane, COLS, stride=PLANES), :]

    pack_planes(FAR_BELOW, up, PLANES, load, left)
    pack_planes(FAR_ABOVE, down, -PLANES, load, left)


def upwind(courant, below_cell, above_cell):
    return courant * jnp.where(courant > 0.0, below_cell, above_cell)


def sweep(count, load_own, load_halo, store, lanes, segments=None):
    plane = lax.broadcasted_iota(jnp.int32, (8, lanes), 0)
    cycle = lax.broadcasted_iota(jnp.int32, (8, lanes), 1)
    first, last = plane == 0, plane == 7
    radius = cycle.astype(F32)
    outer_radius = radius + 1.0
    inverse = 1.0 / (radius + 0.5)
    axis_cell, rim_cell = cycle == 0, cycle == NR - 1

    def load(field, column):
        return load_own(field, column), load_halo(field, column)

    def next_plane(pair):
        own, halo = (pltpu.roll(a, 7, 0) for a in pair)
        return jnp.where(last, halo, own), jnp.where(last, own, halo)

    def previous_plane(pair):
        own, halo = (pltpu.roll(a, 1, 0) for a in pair)
        return jnp.where(first, halo, own), jnp.where(first, own, halo)

    def flux(courant, low, high):
        return tuple(upwind(c, a, b) for c, a, b in zip(courant, low, high))

    def update(values, upper, lower):
        return tuple(v - (a - b) for v, a, b in zip(values, upper, lower))

    def axial(values, courant):
        face = flux(courant, values, next_plane(values))
        return update(values, face, previous_plane(face))

    def axial_own(values, courant):
        own, halo = flux(courant, values, next_plane(values))
        lower = jnp.where(first, pltpu.roll(halo, 1, 0), pltpu.roll(own, 1, 0))
        return values[0] - (own - lower)

    def radial_one(values, courant):
        above_cell = jnp.where(rim_cell, 0.0, pltpu.roll(values, lanes - 1, 1))
        outer = outer_radius * upwind(courant, values, above_cell)
        inner = jnp.where(axis_cell, 0.0, pltpu.roll(outer, 1, 1))
        return values - (outer - inner) * inverse

    def radial(values, courant):
        return tuple(radial_one(v, c) for v, c in zip(values, courant))

    def step(column, state, stage):
        v1_old, face_a_old, v3_old, face_b_old = state
        v1 = axial(load(0, column), load(1, column))
        face_a = v3 = face_b = None
        if stage >= 1:
            face_a = flux(load(2, column - 1), v1_old, v1)
        if stage >= 2:
            v2 = update(v1_old, face_a, face_a_old)
            v3 = radial(v2, load(3, column - 1))
        if stage >= 3:
            face_b = flux(load(2, column - 2), v3_old, v3)
        if stage >= 4:
            v4 = update(v3_old, face_b, face_b_old)
            store(column - 2, axial_own(v4, load(1, column - 2)))
        return v1, face_a, v3, face_b

    state = (None, None, None, None)
    for stage in range(6):
        state = step(LOWEST + stage, state, stage)
    stage = 6
    for start, stop, before in segments or ():
        before()
        state = lax.fori_loop(start, stop, lambda column, s: step(column, s, 6), state, unroll=4)
        stage = stop - LOWEST
    for stage in range(stage, count):
        state = step(LOWEST + stage, state, stage)


def fill_halos(halos, entries, source):
    for tile, field, plane, count, row in entries:
        rows = pl.ds((-count - LOWEST) * 8 + plane_slot(plane), count + COLS, stride=8)
        halos[field].at[tile][rows, :] = source[row : row + count + COLS, :]


def row_slice(column):
    return pl.ds(column * 8 if isinstance(column, int) else pl.multiple_of(column * 8, 8), 8)


def loaders(fields, left, halos, tiles):
    def load_own(field, column):
        if isinstance(column, int) and column < 0:
            parts = [part[row_slice(LEFT.index((field, column))), :] for part in left]
            return jnp.concatenate(parts, axis=1) if tiles > 1 else parts[0]
        return fields[field][row_slice(column), :]

    def load_halo(field, column):
        parts = [halos[field].at[tile][row_slice(column - LOWEST), :] for tile in range(tiles)]
        return jnp.concatenate(parts, axis=1) if tiles > 1 else parts[0]

    return load_own, load_halo


def near_kernel(*refs):
    fields, (below, above, left, crossing, out), halos, swept = refs[:4], refs[4:9], refs[9:13], refs[13]
    fill_halos(halos, NEAR_BELOW, below)
    fill_halos(halos, NEAR_ABOVE, above)

    def store(column, values):
        swept[row_slice(column + 2), :] = values

    sweep(COLS + 4, *loaders(fields, [left], halos, 1), store, 128)
    turned = swept[...].T
    out[pl.ds(0, R_AX, stride=4), :] = turned[:R_AX, :128]
    out[pl.ds(1, R_AX, stride=4), :] = turned[:R_AX, 128:]
    out[pl.ds(2, R_AX, stride=4), :] = crossing[:R_AX, :]
    out[pl.ds(3, R_AX, stride=4), :] = crossing[R_AX:, :]


def fill_far_halos(halos, near_below, near_above, below, above):
    for entries, source in ((NEAR_BELOW, near_below), (NEAR_ABOVE, near_above), (FAR_BELOW, below), (FAR_ABOVE, above)):
        fill_halos(halos, entries, source)


def far_first_kernel(*refs):
    sources, planes, left, out, halos = refs[:4], refs[4:8], refs[8:10], refs[10], refs[11:15]
    fields, semaphores = refs[15:19], refs[19]
    copies = copy_all([(f.at[pl.ds(0, 16), :], held) for f, held in zip(sources, fields)], semaphores)
    fill_far_halos(halos, *planes)
    for copy in copies:
        copy.wait()

    def store(column, values):
        out[row_slice(column + 2), :] = values

    sweep(6, *loaders(fields, left, halos, TILES), store, NR)


def far_kernel(*refs):
    sources, planes, left, (result, first_tile), halos = refs[:4], refs[4:8], refs[8:10], refs[10:12], refs[12:16]
    fields, (out, semaphores) = refs[16:20], refs[20:]
    arrive = [(0, 80), (80, 144), (144, 208), (208, 256)]
    leave = [(0, 64), (64, 128), (128, 192), (192, KEPT)]
    incoming = [
        copy_all([(f.at[pl.ds(a, b - a), :], held.at[pl.ds(a, b - a), :]) for f, held in zip(sources, fields)], semaphores, 4 * k)
        for k, (a, b) in enumerate(arrive)
    ]
    outgoing = []
    fill_far_halos(halos, *planes)

    def store(column, values):
        if not isinstance(column, int) or column >= 0:
            out[row_slice(column), :] = values
            first_tile[row_slice(column), :] = values[:, :128]

    def send(piece):
        a, b = leave[piece]
        pairs = [(out.at[pl.ds(a, b - a), :], result.at[pl.ds(a, b - a), :])]
        outgoing.extend(copy_all(pairs, semaphores, 16 + piece))

    def pause(piece):
        for copy in incoming[piece]:
            copy.wait()
        if piece:
            send(piece - 1)

    for copy in incoming[0]:
        copy.wait()
    segments = [(2, 10, lambda: None)] + [(8 * k + 2, min(8 * k + 10, 30), functools.partial(pause, k)) for k in (1, 2, 3)]
    sweep(COLS + 4, *loaders(fields, left, halos, TILES), store, NR, segments)
    send(3)
    for copy in outgoing:
        copy.wait()


def pieces(values, count):
    out = []
    for _ in range(count):
        piece = values.astype(BF16)
        out.append(piece)
        values = values - piece.astype(F32)
    return out


def mm(a, b, dims=((1,), (0,))):
    return lax.dot_general(a, b, (dims, ((), ())), preferred_element_type=F32)


def plic_volume(plane_code, strip_width):
    normal = lax.shift_right_logical(plane_code, 6).astype(F32)
    offset = lax.bitwise_and(plane_code, 63).astype(F32)
    plane_angle = math.pi / 16 + (normal + 0.5) * (3 * math.pi / 512)
    normal_along = jnp.cos(plane_angle)
    across = jnp.sin(plane_angle)
    plane_level = (offset + 0.5) * (normal_along + across) / 64.0
    strip_span = strip_width * normal_along

    def square(shift_value):
        positive = jnp.maximum(shift_value, 0.0)
        return positive * positive

    strip_area = (
        square(plane_level)
        - square(plane_level - strip_span)
        - square(plane_level - across)
        + square(plane_level - strip_span - across)
    ) / (2.0 * strip_span * across)
    return strip_width * strip_area


def crossing_kernel(*refs):
    (code, width, reader, landing), tables, (out, volume_out) = refs[:4], refs[4:11], refs[12:14]
    copies = copy_all(zip(tables, refs[14:21]), refs[21])
    iota = functools.partial(lax.broadcasted_iota, jnp.int32)
    volume = plic_volume(code[...], width[...])
    both = jnp.concatenate([reader[...].astype(F32), landing[...].astype(F32)], axis=0).astype(BF16)
    column_of_row = (iota((ROWS, COLS), 0) // 8 == iota((ROWS, COLS), 1)).astype(F32).astype(BF16)
    spread = mm(column_of_row, both, ((1,), (1,)))
    row16, lane16 = iota((ROWS, 16), 0), iota((ROWS, 16), 1)
    reader_rows = jnp.sum(jnp.where(lane16 == row16 % 8, spread, 0.0), axis=1, keepdims=True)
    landing_rows = jnp.sum(jnp.where(lane16 == row16 % 8 + 8, spread, 0.0), axis=1, keepdims=True)
    across = mm(both, column_of_row, ((1,), (1,)))
    reader_lanes = jnp.sum(
        jnp.where(iota((16, ROWS), 0) == iota((16, ROWS), 1) % 8, across, 0.0), axis=0, keepdims=True
    )
    same = (reader_rows == reader_lanes) & (iota((ROWS, ROWS), 1) < iota((ROWS, ROWS), 0))
    rank = jnp.sum(jnp.where(same, 1.0, 0.0), axis=1, keepdims=True)

    row, lane = iota((ROWS, 128), 0), iota((ROWS, 128), 1)
    wide = jnp.broadcast_to(volume[:, None, :], (COLS, PLANES, 128)).reshape(ROWS, 128)
    own = jnp.where(lane // 16 == row % 8, wide, 0.0)
    repeat = (iota((128, 128), 0) % 16 == iota((128, 128), 1) % 16).astype(F32).astype(BF16)
    rows_of_volume = sum(mm(piece, repeat) for piece in pieces(own, 3))
    volume_out[...] = rows_of_volume.T[:XR, :]
    chosen = (reader_lanes == iota((R_AX, ROWS), 0).astype(F32)).astype(F32).astype(BF16)
    slotted = jnp.where((lane // 16).astype(F32) == rank, rows_of_volume, 0.0)
    out[:R_AX, :] = sum(mm(chosen, piece) for piece in pieces(slotted, 3))
    target = landing_rows * 8.0 + (row % 8).astype(F32) + 1.0
    marked = jnp.where(lane.astype(F32) == rank, target, 0.0)
    out[R_AX:, :] = mm(chosen, marked.astype(BF16))
    for copy in copies:
        copy.wait()


def arrival_kernel(received, volume, out):
    values = received[pl.ds(2, R_AX, stride=4), :]
    targets = received[pl.ds(3, R_AX, stride=4), :]
    turned = values.T
    row = lax.broadcasted_iota(jnp.int32, (R_AX, ROWS), 1).astype(F32) + 1.0
    total = -volume[...]
    for slot in range(SLOTS):
        chosen = (targets[:, slot : slot + 1] == row).astype(F32).astype(BF16)
        for piece in pieces(turned[slot * XR : (slot + 1) * XR, :], 3):
            total += mm(piece, chosen)
    out[...] = total


def halves(table):
    high = table.astype(ml_dtypes.bfloat16)
    low = (table - high.astype(np.float64)).astype(ml_dtypes.bfloat16)
    return high, low


def filter_tables():
    outer, sector = np.arange(33)[:, None], np.arange(64)[None, :]
    phase = 2 * np.pi * (outer * sector % 64) / 64
    first = np.zeros((2 * KD, 64))
    first[:33], first[KD : KD + 33] = np.cos(phase), -np.sin(phase)
    weight = np.where((outer == 0) | (outer == 32), 1.0, 2.0) / 2048
    last = np.zeros((64, 2 * KD))
    last[:, :33], last[:, KD : KD + 33] = (weight * np.cos(phase)).T, (-weight * np.sin(phase)).T
    column, plane = np.arange(ROWS) // PLANES, np.arange(ROWS) % PLANES
    inner = 2 * np.pi * (column[:, None] * column[None, :] % 32) / 32
    same = plane[:, None] == plane[None, :]
    block = np.concatenate([np.where(same, np.cos(inner), 0.0), np.where(same, -np.sin(inner), 0.0)], axis=1)
    turn = 2 * np.pi * np.arange(KD)[:, None] * column[None, :] / 2048
    mode = np.arange(KD)[:, None] + 64 * column[None, :]
    shift = 2 * np.pi * (2 * mode % 2048) / 2048
    turns = [np.cos(turn), -np.sin(turn), np.cos(shift), np.sin(shift)]
    twiddle = np.concatenate(turns, axis=0).astype(np.float32)
    return (*halves(first), *halves(block), twiddle, *halves(last))


def dot3(a, b):
    (ah, al), (bh, bl) = a, b
    rows = ah.shape[0]
    both = mm(jnp.concatenate([ah, al], axis=0), bh)
    return both[:rows] + (both[rows:] + mm(ah, bl))


def filter_kernel(received, first_h, first_l, block_h, block_l, twiddle, last_h, last_l, out):
    sectors = jnp.concatenate(
        [received[pl.ds(0, R_AX, stride=4), :], received[pl.ds(1, R_AX, stride=4), :]], axis=1
    )
    outer = dot3((first_h[...], first_l[...]), pieces(sectors, 2))
    re, im = outer[:KD], outer[KD:]
    t_re, t_im, s_re, s_im = (twiddle[k * KD : (k + 1) * KD, :] for k in range(4))
    turned = jnp.concatenate([re * t_re - im * t_im, re * t_im + im * t_re], axis=0)
    block = (block_h[...], block_l[...])
    inner = dot3(pieces(turned, 2), block)
    re = inner[:KD, :ROWS] - inner[KD:, ROWS:]
    im = inner[:KD, ROWS:] + inner[KD:, :ROWS]
    re, im = re * s_re - im * s_im, re * s_im + im * s_re
    mode = lax.broadcasted_iota(jnp.int32, (KD, ROWS), 0) + 64 * (
        lax.broadcasted_iota(jnp.int32, (KD, ROWS), 1) // PLANES
    )
    folded = jnp.minimum(mode, 2048 - mode).astype(F32)
    cutoff = (lax.axis_index("az") + 1).astype(F32) * 2.0
    scaled = folded / cutoff
    damped = jnp.exp(-(scaled * scaled))
    back = dot3(pieces(jnp.concatenate([re * damped, im * damped], axis=0), 2), block)
    re = back[:KD, :ROWS] + back[KD:, ROWS:]
    im = back[KD:, :ROWS] - back[:KD, ROWS:]
    turned = jnp.concatenate([re * t_re + im * t_im, im * t_re - re * t_im], axis=0)
    result = dot3((last_h[...], last_l[...]), pieces(turned, 2))
    out[pl.ds(0, R_AX, stride=2), :] = result[:, :128]
    out[pl.ds(1, R_AX, stride=2), :] = result[:, 128:]


def final_kernel(received, delta, swept, last, _, result, out, semaphores):
    rest = (pl.ds(KEPT, ROWS - KEPT), pl.ds(128, NR - 128))
    copy = pltpu.make_async_copy(last.at[:, pl.ds(128, NR - 128)], result.at[rest], semaphores.at[1])
    copy.start()
    near = jnp.concatenate(
        [received[pl.ds(0, R_AX, stride=2), :], received[pl.ds(1, R_AX, stride=2), :]], axis=1
    )
    near = jnp.concatenate([near[:XR] + delta[...], near[XR:], jnp.zeros((R_AX, ROWS), F32)], axis=0)
    cycle = lax.broadcasted_iota(jnp.int32, (ROWS, 128), 1)
    first_tile = jnp.concatenate([swept[...], last[:, :128]], axis=0)
    out[...] = jnp.where(cycle < R_AX, near.T, first_tile)
    copy_out(out, result.at[:, pl.ds(0, 128)], semaphores.at[0])
    copy.wait()


VMEM, HBM = pltpu.VMEM, pltpu.HBM
DMA = pltpu.SemaphoreType.DMA


def call(kernel, inputs, outputs, scratch=(), cost=1.0, aliases=None):
    arrays, specs = [], []
    for given in inputs:
        array, space = given if isinstance(given, tuple) else (given, VMEM)
        arrays.append(pltpu.with_memory_space_constraint(array, HBM) if space is HBM else array)
        specs.append(pl.BlockSpec(memory_space=space))
    out_specs = [pl.BlockSpec(memory_space=getattr(o, "memory_space", VMEM)) for o in outputs]
    return pl.pallas_call(
        kernel,
        in_specs=specs,
        out_specs=out_specs,
        out_shape=list(outputs),
        scratch_shapes=list(scratch),
        input_output_aliases=aliases or {},
        cost_estimate=pl.CostEstimate(flops=int(cost * 1e6), bytes_accessed=int(cost * 3e6), transcendentals=0),
        compiler_params=pltpu.CompilerParams(vmem_limit_bytes=16 * 1024 * 1024),
    )(*arrays)


def free(*dims):
    return jax.ShapeDtypeStruct(dims, F32)


def local(
    fraction,
    courant_axial,
    courant_azimuth,
    courant_radial,
    plane_code,
    strip_width,
    tile_reader,
    landing_column,
):
    ax_count, az_count = lax.axis_size("ax"), lax.axis_size("az")
    higher_ax, higher_az = ([(i, (i + 1) % n) for i in range(n)] for n in (ax_count, az_count))
    lower_ax, lower_az = ([(j, i) for i, j in pairs] for pairs in (higher_ax, higher_az))
    fields = [(a.reshape(ROWS, NR), HBM) for a in (fraction, courant_axial, courant_azimuth, courant_radial)]

    (near_right,) = call(pack_columns, fields, [VMEM((len(LEFT) * 8, 128), F32)], [DMA((4,))])
    near_left = lax.ppermute(near_right, "az", higher_az)

    *near_tiles, far_right = call(
        bring_tiles,
        fields,
        [VMEM((ROWS, 128), F32)] * 4 + [VMEM((len(LEFT) * 8, NR - 128), F32)],
        [DMA((8,))],
    )
    far_left = lax.ppermute(far_right, "az", higher_az)
    near_up, near_down = call(
        pack_near_planes,
        [*near_tiles, near_left],
        [VMEM((NEAR_BELOW_ROWS, 128), F32), VMEM((NEAR_ABOVE_ROWS, 128), F32)],
    )
    tables = filter_tables()
    crossing, volume, *held_tables = call(
        crossing_kernel,
        [plane_code, strip_width, tile_reader.T, landing_column.T]
        + [(jnp.asarray(t), HBM) for t in tables]
        + [(near_up, pl.ANY)],
        [VMEM((2 * R_AX, 128), F32), VMEM((XR, ROWS), F32)] + [VMEM(t.shape, t.dtype) for t in tables],
        [DMA((len(tables),))],
    )
    near_below = lax.ppermute(near_up, "ax", higher_ax)
    near_above = lax.ppermute(near_down, "ax", lower_ax)
    far_up, far_down = call(
        pack_far_planes,
        [*fields, far_left],
        [VMEM((FAR_BELOW_ROWS, 128), F32), VMEM((FAR_ABOVE_ROWS, 128), F32)],
        [VMEM(((TILES - 1) * ROWS, 128), F32)] * 4 + [DMA((4 * (TILES - 1),))],
    )
    (send,) = call(
        near_kernel,
        [*near_tiles, near_below, near_above, near_left, crossing],
        [free(4 * R_AX, 128)],
        [VMEM((1, 36 * 8, 128), F32)] * 4 + [VMEM((ROWS, 128), F32)],
    )
    got = lax.all_to_all(send.reshape(R_AX, 4, 128), "az", 0, 0, tiled=True).reshape(4 * R_AX, 128)

    far_below = lax.ppermute(far_up, "ax", higher_ax)
    far_above = lax.ppermute(far_down, "ax", lower_ax)
    far_inputs = [*fields, near_below, near_above, far_below, far_above, near_left, far_left]
    far_halos = [VMEM((TILES, 36 * 8, 128), F32)] * 4
    (first_columns,) = call(
        far_first_kernel, far_inputs, [VMEM((16, NR), F32)], far_halos + [VMEM((16, NR), F32)] * 4 + [DMA((4,))]
    )
    last_columns = lax.ppermute(first_columns, "az", lower_az)
    swept, first_tile = call(
        far_kernel,
        far_inputs,
        [HBM((ROWS, NR), F32), VMEM((KEPT, 128), F32)],
        far_halos + [VMEM((ROWS, NR), F32)] * 4 + [VMEM((KEPT, NR), F32), DMA((20,))],
        cost=4.0,
    )

    (back,) = call(filter_kernel, [got, *held_tables], [free(2 * R_AX, 128)])
    returned = lax.all_to_all(back.reshape(R_AX, 2, 128), "az", 0, 0, tiled=True).reshape(2 * R_AX, 128)
    (delta,) = call(arrival_kernel, [got, volume], [VMEM((XR, ROWS), F32)])
    (out,) = call(
        final_kernel,
        [returned, delta, first_tile, last_columns, (swept, HBM)],
        [HBM((ROWS, NR), F32)],
        [VMEM((ROWS, 128), F32), DMA((2,))],
        aliases={4: 0},
    )
    return out.reshape(COLS, PLANES, NR)


def solution(mesh):
    return jax.shard_map(
        local,
        mesh=mesh,
        in_specs=(
            P("az", "ax", None),
            P("az", "ax", None),
            P("az", "ax", None),
            P("az", "ax", None),
            P("az", "ax"),
            P("az", "ax"),
            P("az", "ax"),
            P("az", "ax"),
        ),
        out_specs=P("az", "ax", None),
        check_vma=False,
    )
```

```python
import functools
import math

import jax
import jax.numpy as jnp
import ml_dtypes
import numpy as np
from jax import lax
from jax.experimental import pallas as pl
from jax.experimental.pallas import tpu as pltpu
from jax.sharding import PartitionSpec as P

R_AX = 64
XR = 16
COLS = 32
PLANES = 8
ROWS = COLS * PLANES
NR = 512
SLOTS = 8
KD = 40

F32 = jnp.float32
BF16 = jnp.bfloat16

BELOW = ((0, -2), (0, -1), (1, -2), (1, -1), (2, -1), (3, -1))
ABOVE = ((0, 8), (0, 9), (1, 8), (2, 8), (3, 8))
HALO_PLANES = ((-2, -1, 8, 9), (-2, -1, 8), (-1, 8), (-1, 8))

LOWEST = -4
LEFT = tuple((f, c) for f in range(3) for c in range(-4, 0)) + tuple((3, c) for c in range(-3, 0))
LEFT_COUNT = (4, 4, 4, 3)
TILES = NR // 128
KEPT = ROWS - 16


def halo_layout(planes, tiles):
    entries, row = [], 0
    for tile in tiles:
        for field, plane in planes:
            entries.append((tile, field, plane, LEFT_COUNT[field], row))
            row += LEFT_COUNT[field] + COLS
    return entries, -(-row // 8) * 8


NEAR_BELOW, NEAR_BELOW_ROWS = halo_layout(BELOW, (0,))
NEAR_ABOVE, NEAR_ABOVE_ROWS = halo_layout(ABOVE, (0,))
FAR_BELOW, FAR_BELOW_ROWS = halo_layout(BELOW, range(TILES))
FAR_ABOVE, FAR_ABOVE_ROWS = halo_layout(ABOVE, range(TILES))


def plane_slot(plane):
    return plane % 16 - 8


def copy_out(source, target, semaphore):
    copy = pltpu.make_async_copy(source, target, semaphore)
    copy.start()
    copy.wait()


def copy_all(pairs, semaphores, first=0):
    copies = [pltpu.make_async_copy(a, b, semaphores.at[first + k]) for k, (a, b) in enumerate(pairs)]
    for copy in copies:
        copy.start()
    return copies


def bring_tiles(*refs):
    fields, tiles, (right, semaphores) = refs[:4], refs[4:8], refs[8:]
    copies = copy_all([(f.at[:, pl.ds(0, 128)], tile) for f, tile in zip(fields, tiles)], semaphores, 4)
    pack_columns(*fields, right, semaphores)
    for copy in copies:
        copy.wait()


def pack_columns(*refs):
    fields, (right, semaphores) = refs[:4], refs[4:]
    lanes = right.shape[1]
    pairs, row = [], 0
    for field, count in zip(fields, LEFT_COUNT):
        source = field.at[pl.ds(ROWS - count * 8, count * 8), pl.ds(0 if lanes == 128 else NR - lanes, lanes)]
        pairs.append((source, right.at[pl.ds(row, count * 8), :]))
        row += count * 8
    for copy in copy_all(pairs, semaphores):
        copy.wait()


def pack_planes(entries, out, shift, load, left):
    for tile, field, plane, count, row in entries:
        for at in range(count):
            origin = LEFT.index((field, at - count)) * 8 + plane + shift
            part, lane = (left[0], 0) if tile == 0 else (left[1], tile * 128 - 128)
            out[row + at : row + at + 1, :] = part[origin : origin + 1, pl.ds(lane, 128)]
        out[row + count : row + count + COLS, :] = load(tile, field, plane + shift)
    used = entries[-1][4] + entries[-1][3] + COLS
    if used < out.shape[0]:
        out[used:, :] = jnp.zeros((out.shape[0] - used, 128), F32)


BLOCK = COLS + 4
UP_ROWS, DOWN_ROWS = 4 * BLOCK, 112


def squeeze(entries, flat, out):
    lane = lax.broadcasted_iota(jnp.int32, (BLOCK, 128), 1)
    planes = [flat[row + count - 4 : row + count + COLS, :] for _, _, _, count, row in entries]
    last = planes[-1] if len(planes) % 2 else jnp.zeros((BLOCK, 128), F32)
    for k, plane in enumerate(planes[:-1]):
        last = jnp.where(lane == 64 + k, pltpu.roll(plane, k, 1) if k else plane, last)
    blocks = [jnp.where(lane < 64, a, pltpu.roll(b, 64, 1)) for a, b in zip(planes[0::2], planes[1::2])] + [last]
    for k, values in enumerate(blocks):
        out[k * BLOCK : (k + 1) * BLOCK, :] = values
    if len(blocks) * BLOCK < out.shape[0]:
        out[len(blocks) * BLOCK :, :] = jnp.zeros((out.shape[0] - len(blocks) * BLOCK, 128), F32)


def unfold(entries, packed, flat):
    lane = lax.broadcasted_iota(jnp.int32, (BLOCK, 128), 1)
    at = len(entries) // 2 * BLOCK
    last = packed[at : at + BLOCK, :]
    for k, (_, _, _, count, row) in enumerate(entries):
        values = packed[k // 2 * BLOCK : (k // 2 + 1) * BLOCK, :]
        if k % 2:
            values = pltpu.roll(values, 64, 1)
        if k < len(entries) - 1:
            values = jnp.where(lane == 64, pltpu.roll(last, 128 - k, 1) if k else last, values)
        flat[row : row + count + COLS, :] = values[4 - count :]


def pack_near_planes(*refs):
    tiles, (left, up, down, flat_up, flat_down) = refs[:4], refs[4:]

    def load(_, field, plane):
        return tiles[field][pl.ds(plane, COLS, stride=PLANES), :]

    pack_planes(NEAR_BELOW, flat_up, PLANES, load, [left])
    pack_planes(NEAR_ABOVE, flat_down, -PLANES, load, [left])
    squeeze(NEAR_BELOW, flat_up, up)
    squeeze(NEAR_ABOVE, flat_down, down)


def pack_far_planes(*refs):
    fields, left, (up, down, *tiles, semaphores) = refs[:4], refs[4:6], refs[6:]
    pairs = []
    for field, tile in zip(fields, tiles):
        for k in range(TILES):
            pairs.append((field.at[:, pl.ds(k * 128, 128)], tile.at[pl.ds(k * ROWS, ROWS), :]))
    for copy in copy_all(pairs, semaphores):
        copy.wait()

    def load(tile, field, plane):
        return tiles[field][pl.ds(tile * ROWS + plane, COLS, stride=PLANES), :]

    pack_planes(FAR_BELOW, up, PLANES, load, left)
    pack_planes(FAR_ABOVE, down, -PLANES, load, left)


def upwind(courant, below_cell, above_cell):
    return courant * jnp.where(courant > 0.0, below_cell, above_cell)


def sweep(count, load_own, load_halo, store, lanes, segments=None):
    plane = lax.broadcasted_iota(jnp.int32, (8, lanes), 0)
    cycle = lax.broadcasted_iota(jnp.int32, (8, lanes), 1)
    first, last = plane == 0, plane == 7
    radius = cycle.astype(F32)
    outer_radius = radius + 1.0
    inverse = 1.0 / (radius + 0.5)
    axis_cell, rim_cell = cycle == 0, cycle == NR - 1

    def load(field, column):
        return load_own(field, column), load_halo(field, column)

    def next_plane(pair):
        own, halo = (pltpu.roll(a, 7, 0) for a in pair)
        return jnp.where(last, halo, own), jnp.where(last, own, halo)

    def previous_plane(pair):
        own, halo = (pltpu.roll(a, 1, 0) for a in pair)
        return jnp.where(first, halo, own), jnp.where(first, own, halo)

    def flux(courant, low, high):
        return tuple(upwind(c, a, b) for c, a, b in zip(courant, low, high))

    def update(values, upper, lower):
        return tuple(v - (a - b) for v, a, b in zip(values, upper, lower))

    def axial(values, courant):
        face = flux(courant, values, next_plane(values))
        return update(values, face, previous_plane(face))

    def axial_own(values, courant):
        own, halo = flux(courant, values, next_plane(values))
        lower = jnp.where(first, pltpu.roll(halo, 1, 0), pltpu.roll(own, 1, 0))
        return values[0] - (own - lower)

    def radial_one(values, courant):
        above_cell = jnp.where(rim_cell, 0.0, pltpu.roll(values, lanes - 1, 1))
        outer = outer_radius * upwind(courant, values, above_cell)
        inner = jnp.where(axis_cell, 0.0, pltpu.roll(outer, 1, 1))
        return values - (outer - inner) * inverse

    def radial(values, courant):
        return tuple(radial_one(v, c) for v, c in zip(values, courant))

    def step(column, state, stage):
        v1_old, face_a_old, v3_old, face_b_old = state
        v1 = axial(load(0, column), load(1, column))
        face_a = v3 = face_b = None
        if stage >= 1:
            face_a = flux(load(2, column - 1), v1_old, v1)
        if stage >= 2:
            v2 = update(v1_old, face_a, face_a_old)
            v3 = radial(v2, load(3, column - 1))
        if stage >= 3:
            face_b = flux(load(2, column - 2), v3_old, v3)
        if stage >= 4:
            v4 = update(v3_old, face_b, face_b_old)
            store(column - 2, axial_own(v4, load(1, column - 2)))
        return v1, face_a, v3, face_b

    state = (None, None, None, None)
    for stage in range(6):
        state = step(LOWEST + stage, state, stage)
    stage = 6
    for start, stop, before in segments or ():
        before()
        state = lax.fori_loop(start, stop, lambda column, s: step(column, s, 6), state, unroll=4)
        stage = stop - LOWEST
    for stage in range(stage, count):
        state = step(LOWEST + stage, state, stage)


def fill_halos(halos, entries, source):
    for tile, field, plane, count, row in entries:
        rows = pl.ds((-count - LOWEST) * 8 + plane_slot(plane), count + COLS, stride=8)
        halos[field].at[tile][rows, :] = source[row : row + count + COLS, :]


def row_slice(column):
    return pl.ds(column * 8 if isinstance(column, int) else pl.multiple_of(column * 8, 8), 8)


def loaders(fields, left, halos, tiles):
    def load_own(field, column):
        if isinstance(column, int) and column < 0:
            parts = [part[row_slice(LEFT.index((field, column))), :] for part in left]
            return jnp.concatenate(parts, axis=1) if tiles > 1 else parts[0]
        return fields[field][row_slice(column), :]

    def load_halo(field, column):
        parts = [halos[field].at[tile][row_slice(column - LOWEST), :] for tile in range(tiles)]
        return jnp.concatenate(parts, axis=1) if tiles > 1 else parts[0]

    return load_own, load_halo


def near_kernel(*refs):
    fields, (below, above, left, crossing, out), halos = refs[:4], refs[4:9], refs[9:13]
    swept, flat_below, flat_above = refs[13:]
    unfold(NEAR_BELOW, below, flat_below)
    unfold(NEAR_ABOVE, above, flat_above)
    fill_halos(halos, NEAR_BELOW, flat_below)
    fill_halos(halos, NEAR_ABOVE, flat_above)

    def store(column, values):
        swept[row_slice(column + 2), :] = values

    sweep(COLS + 4, *loaders(fields, [left], halos, 1), store, 128)
    turned = swept[...].T
    out[pl.ds(0, R_AX, stride=4), :] = turned[:R_AX, :128]
    out[pl.ds(1, R_AX, stride=4), :] = turned[:R_AX, 128:]
    out[pl.ds(2, R_AX, stride=4), :] = crossing[:R_AX, :]
    out[pl.ds(3, R_AX, stride=4), :] = crossing[R_AX:, :]


def fill_far_halos(halos, below, above):
    fill_halos(halos, FAR_BELOW, below)
    fill_halos(halos, FAR_ABOVE, above)


def far_first_kernel(*refs):
    sources, planes, left, out, halos = refs[:4], refs[4:6], refs[6:8], refs[8], refs[9:13]
    fields, semaphores = refs[13:17], refs[17]
    copies = copy_all([(f.at[pl.ds(0, 16), :], held) for f, held in zip(sources, fields)], semaphores)
    fill_far_halos(halos, *planes)
    for copy in copies:
        copy.wait()

    def store(column, values):
        out[row_slice(column + 2), :] = values

    sweep(6, *loaders(fields, left, halos, TILES), store, NR)


def far_kernel(*refs):
    sources, planes, left, (result, first_tile), halos = refs[:4], refs[4:6], refs[6:8], refs[8:10], refs[10:14]
    fields, (out, semaphores) = refs[14:18], refs[18:]
    arrive = [(0, 80), (80, 144), (144, 208), (208, 256)]
    leave = [(0, 64), (64, 128), (128, 192), (192, KEPT)]
    incoming = [
        copy_all([(f.at[pl.ds(a, b - a), :], held.at[pl.ds(a, b - a), :]) for f, held in zip(sources, fields)], semaphores, 4 * k)
        for k, (a, b) in enumerate(arrive)
    ]
    outgoing = []
    fill_far_halos(halos, *planes)

    def store(column, values):
        if not isinstance(column, int) or column >= 0:
            out[row_slice(column), :] = values
            first_tile[row_slice(column), :] = values[:, :128]

    def send(piece):
        a, b = leave[piece]
        pairs = [(out.at[pl.ds(a, b - a), :], result.at[pl.ds(a, b - a), :])]
        outgoing.extend(copy_all(pairs, semaphores, 16 + piece))

    def pause(piece):
        for copy in incoming[piece]:
            copy.wait()
        if piece:
            send(piece - 1)

    for copy in incoming[0]:
        copy.wait()
    segments = [(2, 10, lambda: None)] + [(8 * k + 2, min(8 * k + 10, 30), functools.partial(pause, k)) for k in (1, 2, 3)]
    sweep(COLS + 4, *loaders(fields, left, halos, TILES), store, NR, segments)
    send(3)
    for copy in outgoing:
        copy.wait()


def pieces(values, count):
    out = []
    for _ in range(count):
        piece = values.astype(BF16)
        out.append(piece)
        values = values - piece.astype(F32)
    return out


def mm(a, b, dims=((1,), (0,))):
    return lax.dot_general(a, b, (dims, ((), ())), preferred_element_type=F32)


def plic_volume(plane_code, strip_width):
    normal = lax.shift_right_logical(plane_code, 6).astype(F32)
    offset = lax.bitwise_and(plane_code, 63).astype(F32)
    plane_angle = math.pi / 16 + (normal + 0.5) * (3 * math.pi / 512)
    normal_along = jnp.cos(plane_angle)
    across = jnp.sin(plane_angle)
    plane_level = (offset + 0.5) * (normal_along + across) / 64.0
    strip_span = strip_width * normal_along

    def square(shift_value):
        positive = jnp.maximum(shift_value, 0.0)
        return positive * positive

    strip_area = (
        square(plane_level)
        - square(plane_level - strip_span)
        - square(plane_level - across)
        + square(plane_level - strip_span - across)
    ) / (2.0 * strip_span * across)
    return strip_width * strip_area


def crossing_kernel(*refs):
    (code, width, reader, landing), tables, (out, volume_out) = refs[:4], refs[4:11], refs[12:14]
    copies = copy_all(zip(tables, refs[14:21]), refs[21])
    iota = functools.partial(lax.broadcasted_iota, jnp.int32)
    volume = plic_volume(code[...], width[...])
    both = jnp.concatenate([reader[...].astype(F32), landing[...].astype(F32)], axis=0).astype(BF16)
    column_of_row = (iota((ROWS, COLS), 0) // 8 == iota((ROWS, COLS), 1)).astype(F32).astype(BF16)
    spread = mm(column_of_row, both, ((1,), (1,)))
    row16, lane16 = iota((ROWS, 16), 0), iota((ROWS, 16), 1)
    reader_rows = jnp.sum(jnp.where(lane16 == row16 % 8, spread, 0.0), axis=1, keepdims=True)
    landing_rows = jnp.sum(jnp.where(lane16 == row16 % 8 + 8, spread, 0.0), axis=1, keepdims=True)
    across = mm(both, column_of_row, ((1,), (1,)))
    reader_lanes = jnp.sum(
        jnp.where(iota((16, ROWS), 0) == iota((16, ROWS), 1) % 8, across, 0.0), axis=0, keepdims=True
    )
    same = (reader_rows == reader_lanes) & (iota((ROWS, ROWS), 1) < iota((ROWS, ROWS), 0))
    rank = jnp.sum(jnp.where(same, 1.0, 0.0), axis=1, keepdims=True)

    row, lane = iota((ROWS, 128), 0), iota((ROWS, 128), 1)
    wide = jnp.broadcast_to(volume[:, None, :], (COLS, PLANES, 128)).reshape(ROWS, 128)
    own = jnp.where(lane // 16 == row % 8, wide, 0.0)
    repeat = (iota((128, 128), 0) % 16 == iota((128, 128), 1) % 16).astype(F32).astype(BF16)
    rows_of_volume = sum(mm(piece, repeat) for piece in pieces(own, 3))
    volume_out[...] = rows_of_volume.T[:XR, :]
    chosen = (reader_lanes == iota((R_AX, ROWS), 0).astype(F32)).astype(F32).astype(BF16)
    slotted = jnp.where((lane // 16).astype(F32) == rank, rows_of_volume, 0.0)
    out[:R_AX, :] = sum(mm(chosen, piece) for piece in pieces(slotted, 3))
    target = landing_rows * 8.0 + (row % 8).astype(F32) + 1.0
    marked = jnp.where(lane.astype(F32) == rank, target, 0.0)
    out[R_AX:, :] = mm(chosen, marked.astype(BF16))
    for copy in copies:
        copy.wait()


def arrival_kernel(received, volume, out):
    values = received[pl.ds(2, R_AX, stride=4), :]
    targets = received[pl.ds(3, R_AX, stride=4), :]
    turned = values.T
    row = lax.broadcasted_iota(jnp.int32, (R_AX, ROWS), 1).astype(F32) + 1.0
    total = -volume[...]
    for slot in range(SLOTS):
        chosen = (targets[:, slot : slot + 1] == row).astype(F32).astype(BF16)
        for piece in pieces(turned[slot * XR : (slot + 1) * XR, :], 3):
            total += mm(piece, chosen)
    out[...] = total


def halves(table):
    high = table.astype(ml_dtypes.bfloat16)
    low = (table - high.astype(np.float64)).astype(ml_dtypes.bfloat16)
    return high, low


def filter_tables():
    outer, sector = np.arange(33)[:, None], np.arange(64)[None, :]
    phase = 2 * np.pi * (outer * sector % 64) / 64
    first = np.zeros((2 * KD, 64))
    first[:33], first[KD : KD + 33] = np.cos(phase), -np.sin(phase)
    weight = np.where((outer == 0) | (outer == 32), 1.0, 2.0) / 2048
    last = np.zeros((64, 2 * KD))
    last[:, :33], last[:, KD : KD + 33] = (weight * np.cos(phase)).T, (-weight * np.sin(phase)).T
    column, plane = np.arange(ROWS) // PLANES, np.arange(ROWS) % PLANES
    inner = 2 * np.pi * (column[:, None] * column[None, :] % 32) / 32
    same = plane[:, None] == plane[None, :]
    block = np.concatenate([np.where(same, np.cos(inner), 0.0), np.where(same, -np.sin(inner), 0.0)], axis=1)
    turn = 2 * np.pi * np.arange(KD)[:, None] * column[None, :] / 2048
    mode = np.arange(KD)[:, None] + 64 * column[None, :]
    shift = 2 * np.pi * (2 * mode % 2048) / 2048
    turns = [np.cos(turn), -np.sin(turn), np.cos(shift), np.sin(shift)]
    twiddle = np.concatenate(turns, axis=0).astype(np.float32)
    return (*halves(first), *halves(block), twiddle, *halves(last))


def dot3(a, b):
    (ah, al), (bh, bl) = a, b
    rows = ah.shape[0]
    both = mm(jnp.concatenate([ah, al], axis=0), bh)
    return both[:rows] + (both[rows:] + mm(ah, bl))


def filter_kernel(received, first_h, first_l, block_h, block_l, twiddle, last_h, last_l, out):
    sectors = jnp.concatenate(
        [received[pl.ds(0, R_AX, stride=4), :], received[pl.ds(1, R_AX, stride=4), :]], axis=1
    )
    outer = dot3((first_h[...], first_l[...]), pieces(sectors, 2))
    re, im = outer[:KD], outer[KD:]
    t_re, t_im, s_re, s_im = (twiddle[k * KD : (k + 1) * KD, :] for k in range(4))
    turned = jnp.concatenate([re * t_re - im * t_im, re * t_im + im * t_re], axis=0)
    block = (block_h[...], block_l[...])
    inner = dot3(pieces(turned, 2), block)
    re = inner[:KD, :ROWS] - inner[KD:, ROWS:]
    im = inner[:KD, ROWS:] + inner[KD:, :ROWS]
    re, im = re * s_re - im * s_im, re * s_im + im * s_re
    mode = lax.broadcasted_iota(jnp.int32, (KD, ROWS), 0) + 64 * (
        lax.broadcasted_iota(jnp.int32, (KD, ROWS), 1) // PLANES
    )
    folded = jnp.minimum(mode, 2048 - mode).astype(F32)
    cutoff = (lax.axis_index("az") + 1).astype(F32) * 2.0
    scaled = folded / cutoff
    damped = jnp.exp(-(scaled * scaled))
    back = dot3(pieces(jnp.concatenate([re * damped, im * damped], axis=0), 2), block)
    re = back[:KD, :ROWS] + back[KD:, ROWS:]
    im = back[KD:, :ROWS] - back[:KD, ROWS:]
    turned = jnp.concatenate([re * t_re + im * t_im, im * t_re - re * t_im], axis=0)
    result = dot3((last_h[...], last_l[...]), pieces(turned, 2))
    out[pl.ds(0, R_AX, stride=2), :] = result[:, :128]
    out[pl.ds(1, R_AX, stride=2), :] = result[:, 128:]


def final_kernel(received, delta, swept, last, _, result, out, semaphores):
    rest = (pl.ds(KEPT, ROWS - KEPT), pl.ds(128, NR - 128))
    copy = pltpu.make_async_copy(last.at[:, pl.ds(128, NR - 128)], result.at[rest], semaphores.at[1])
    copy.start()
    near = jnp.concatenate(
        [received[pl.ds(0, R_AX, stride=2), :], received[pl.ds(1, R_AX, stride=2), :]], axis=1
    )
    near = jnp.concatenate([near[:XR] + delta[...], near[XR:], jnp.zeros((R_AX, ROWS), F32)], axis=0)
    cycle = lax.broadcasted_iota(jnp.int32, (ROWS, 128), 1)
    first_tile = jnp.concatenate([swept[...], last[:, :128]], axis=0)
    out[...] = jnp.where(cycle < R_AX, near.T, first_tile)
    copy_out(out, result.at[:, pl.ds(0, 128)], semaphores.at[0])
    copy.wait()


VMEM, HBM = pltpu.VMEM, pltpu.HBM
DMA = pltpu.SemaphoreType.DMA


def call(kernel, inputs, outputs, scratch=(), cost=1.0, aliases=None):
    arrays, specs = [], []
    for given in inputs:
        array, space = given if isinstance(given, tuple) else (given, VMEM)
        arrays.append(pltpu.with_memory_space_constraint(array, HBM) if space is HBM else array)
        specs.append(pl.BlockSpec(memory_space=space))
    out_specs = [pl.BlockSpec(memory_space=getattr(o, "memory_space", VMEM)) for o in outputs]
    return pl.pallas_call(
        kernel,
        in_specs=specs,
        out_specs=out_specs,
        out_shape=list(outputs),
        scratch_shapes=list(scratch),
        input_output_aliases=aliases or {},
        cost_estimate=pl.CostEstimate(flops=int(cost * 1e6), bytes_accessed=int(cost * 3e6), transcendentals=0),
        compiler_params=pltpu.CompilerParams(vmem_limit_bytes=16 * 1024 * 1024),
    )(*arrays)


def free(*dims):
    return jax.ShapeDtypeStruct(dims, F32)


def local(
    fraction,
    courant_axial,
    courant_azimuth,
    courant_radial,
    plane_code,
    strip_width,
    tile_reader,
    landing_column,
):
    ax_count, az_count = lax.axis_size("ax"), lax.axis_size("az")
    higher_ax, higher_az = ([(i, (i + 1) % n) for i in range(n)] for n in (ax_count, az_count))
    lower_ax, lower_az = ([(j, i) for i, j in pairs] for pairs in (higher_ax, higher_az))
    fields = [(a.reshape(ROWS, NR), HBM) for a in (fraction, courant_axial, courant_azimuth, courant_radial)]

    (near_right,) = call(pack_columns, fields, [VMEM((len(LEFT) * 8, 128), F32)], [DMA((4,))])
    near_left = lax.ppermute(near_right, "az", higher_az)

    *near_tiles, far_right = call(
        bring_tiles,
        fields,
        [VMEM((ROWS, 128), F32)] * 4 + [VMEM((len(LEFT) * 8, NR - 128), F32)],
        [DMA((8,))],
    )
    far_left = lax.ppermute(far_right, "az", higher_az)
    flat = [VMEM((NEAR_BELOW_ROWS, 128), F32), VMEM((NEAR_ABOVE_ROWS, 128), F32)]
    near_up, near_down = call(
        pack_near_planes,
        [*near_tiles, near_left],
        [VMEM((UP_ROWS, 128), F32), VMEM((DOWN_ROWS, 128), F32)],
        flat,
    )
    tables = filter_tables()
    crossing, volume, *held_tables = call(
        crossing_kernel,
        [plane_code, strip_width, tile_reader.T, landing_column.T]
        + [(jnp.asarray(t), HBM) for t in tables]
        + [(near_up, pl.ANY)],
        [VMEM((2 * R_AX, 128), F32), VMEM((XR, ROWS), F32)] + [VMEM(t.shape, t.dtype) for t in tables],
        [DMA((len(tables),))],
    )
    near_below = lax.ppermute(near_up, "ax", higher_ax)
    near_above = lax.ppermute(near_down, "ax", lower_ax)
    far_up, far_down = call(
        pack_far_planes,
        [*fields, near_left, far_left],
        [VMEM((FAR_BELOW_ROWS, 128), F32), VMEM((FAR_ABOVE_ROWS, 128), F32)],
        [VMEM((TILES * ROWS, 128), F32)] * 4 + [DMA((4 * TILES,))],
    )
    (send,) = call(
        near_kernel,
        [*near_tiles, near_below, near_above, near_left, crossing],
        [free(4 * R_AX, 128)],
        [VMEM((1, 36 * 8, 128), F32)] * 4 + [VMEM((ROWS, 128), F32)] + flat,
    )
    got = lax.all_to_all(send.reshape(R_AX, 4, 128), "az", 0, 0, tiled=True).reshape(4 * R_AX, 128)

    far_below = lax.ppermute(far_up, "ax", higher_ax)
    far_above = lax.ppermute(far_down, "ax", lower_ax)
    far_inputs = [*fields, far_below, far_above, near_left, far_left]
    far_halos = [VMEM((TILES, 36 * 8, 128), F32)] * 4
    (first_columns,) = call(
        far_first_kernel, far_inputs, [VMEM((16, NR), F32)], far_halos + [VMEM((16, NR), F32)] * 4 + [DMA((4,))]
    )
    last_columns = lax.ppermute(first_columns, "az", lower_az)
    swept, first_tile = call(
        far_kernel,
        far_inputs,
        [HBM((ROWS, NR), F32), VMEM((KEPT, 128), F32)],
        far_halos + [VMEM((ROWS, NR), F32)] * 4 + [VMEM((KEPT, NR), F32), DMA((20,))],
        cost=4.0,
    )

    (back,) = call(filter_kernel, [got, *held_tables], [free(2 * R_AX, 128)])
    returned = lax.all_to_all(back.reshape(R_AX, 2, 128), "az", 0, 0, tiled=True).reshape(2 * R_AX, 128)
    (delta,) = call(arrival_kernel, [got, volume], [VMEM((XR, ROWS), F32)])
    (out,) = call(
        final_kernel,
        [returned, delta, first_tile, last_columns, (swept, HBM)],
        [HBM((ROWS, NR), F32)],
        [VMEM((ROWS, 128), F32), DMA((2,))],
        aliases={4: 0},
    )
    return out.reshape(COLS, PLANES, NR)


def solution(mesh):
    return jax.shard_map(
        local,
        mesh=mesh,
        in_specs=(
            P("az", "ax", None),
            P("az", "ax", None),
            P("az", "ax", None),
            P("az", "ax", None),
            P("az", "ax"),
            P("az", "ax"),
            P("az", "ax"),
            P("az", "ax"),
        ),
        out_specs=P("az", "ax", None),
        check_vma=False,
    )
```

```python
import functools
import math

import jax
import jax.numpy as jnp
import ml_dtypes
import numpy as np
from jax import lax
from jax.experimental import pallas as pl
from jax.experimental.pallas import tpu as pltpu
from jax.sharding import PartitionSpec as P

R_AX = 64
XR = 16
COLS = 32
PLANES = 8
ROWS = COLS * PLANES
NR = 512
SLOTS = 8
KD = 40

F32 = jnp.float32
BF16 = jnp.bfloat16

BELOW = ((0, -2), (0, -1), (1, -2), (1, -1), (2, -1), (3, -1))
ABOVE = ((0, 8), (0, 9), (1, 8), (2, 8), (3, 8))
HALO_PLANES = ((-2, -1, 8, 9), (-2, -1, 8), (-1, 8), (-1, 8))

LOWEST = -4
LEFT = tuple((f, c) for f in range(3) for c in range(-4, 0)) + tuple((3, c) for c in range(-3, 0))
LEFT_COUNT = (4, 4, 4, 3)
TILES = NR // 128
KEPT = ROWS - 16


def halo_layout(planes, tiles):
    entries, row = [], 0
    for tile in tiles:
        for field, plane in planes:
            entries.append((tile, field, plane, LEFT_COUNT[field], row))
            row += LEFT_COUNT[field] + COLS
    return entries, -(-row // 8) * 8


NEAR_BELOW, NEAR_BELOW_ROWS = halo_layout(BELOW, (0,))
NEAR_ABOVE, NEAR_ABOVE_ROWS = halo_layout(ABOVE, (0,))
FAR_BELOW, FAR_BELOW_ROWS = halo_layout(BELOW, range(1, TILES))
FAR_ABOVE, FAR_ABOVE_ROWS = halo_layout(ABOVE, range(1, TILES))


def plane_slot(plane):
    return plane % 16 - 8


def copy_out(source, target, semaphore):
    copy = pltpu.make_async_copy(source, target, semaphore)
    copy.start()
    copy.wait()


def copy_all(pairs, semaphores, first=0):
    copies = [pltpu.make_async_copy(a, b, semaphores.at[first + k]) for k, (a, b) in enumerate(pairs)]
    for copy in copies:
        copy.start()
    return copies


def bring_tiles(*refs):
    fields, tiles, (right, semaphores) = refs[:4], refs[4:8], refs[8:]
    copies = copy_all([(f.at[:, pl.ds(0, 128)], tile) for f, tile in zip(fields, tiles)], semaphores, 4)
    pack_columns(*fields, right, semaphores)
    for copy in copies:
        copy.wait()


def pack_columns(*refs):
    fields, (right, semaphores) = refs[:4], refs[4:]
    lanes = right.shape[1]
    pairs, row = [], 0
    for field, count in zip(fields, LEFT_COUNT):
        source = field.at[pl.ds(ROWS - count * 8, count * 8), pl.ds(0 if lanes == 128 else NR - lanes, lanes)]
        pairs.append((source, right.at[pl.ds(row, count * 8), :]))
        row += count * 8
    for copy in copy_all(pairs, semaphores):
        copy.wait()


def pack_planes(entries, out, shift, load, left):
    for tile, field, plane, count, row in entries:
        for at in range(count):
            origin = LEFT.index((field, at - count)) * 8 + plane + shift
            out[row + at : row + at + 1, :] = left[origin : origin + 1, pl.ds(max(tile - 1, 0) * 128, 128)]
        out[row + count : row + count + COLS, :] = load(tile, field, plane + shift)
    used = entries[-1][4] + entries[-1][3] + COLS
    if used < out.shape[0]:
        out[used:, :] = jnp.zeros((out.shape[0] - used, 128), F32)


def pack_near_planes(*refs):
    tiles, (left, up, down) = refs[:4], refs[4:]

    def load(_, field, plane):
        return tiles[field][pl.ds(plane, COLS, stride=PLANES), :]

    pack_planes(NEAR_BELOW, up, PLANES, load, left)
    pack_planes(NEAR_ABOVE, down, -PLANES, load, left)


def pack_far_planes(*refs):
    fields, (left, up, down, *tiles, semaphores) = refs[:4], refs[4:]
    pairs = []
    for field, tile in zip(fields, tiles):
        for k in range(1, TILES):
            pairs.append((field.at[:, pl.ds(k * 128, 128)], tile.at[pl.ds((k - 1) * ROWS, ROWS), :]))
    for copy in copy_all(pairs, semaphores):
        copy.wait()

    def load(tile, field, plane):
        return tiles[field][pl.ds((tile - 1) * ROWS + plane, COLS, stride=PLANES), :]

    pack_planes(FAR_BELOW, up, PLANES, load, left)
    pack_planes(FAR_ABOVE, down, -PLANES, load, left)


def upwind(courant, below_cell, above_cell):
    return courant * jnp.where(courant > 0.0, below_cell, above_cell)


def sweep(count, load_own, load_halo, store, lanes, segments=None):
    plane = lax.broadcasted_iota(jnp.int32, (8, lanes), 0)
    cycle = lax.broadcasted_iota(jnp.int32, (8, lanes), 1)
    first, last = plane == 0, plane == 7
    radius = cycle.astype(F32)
    outer_radius = radius + 1.0
    inverse = 1.0 / (radius + 0.5)
    axis_cell, rim_cell = cycle == 0, cycle == NR - 1

    def load(field, column):
        return load_own(field, column), load_halo(field, column)

    def next_plane(pair):
        own, halo = (pltpu.roll(a, 7, 0) for a in pair)
        return jnp.where(last, halo, own), jnp.where(last, own, halo)

    def previous_plane(pair):
        own, halo = (pltpu.roll(a, 1, 0) for a in pair)
        return jnp.where(first, halo, own), jnp.where(first, own, halo)

    def flux(courant, low, high):
        return tuple(upwind(c, a, b) for c, a, b in zip(courant, low, high))

    def update(values, upper, lower):
        return tuple(v - (a - b) for v, a, b in zip(values, upper, lower))

    def axial(values, courant):
        face = flux(courant, values, next_plane(values))
        return update(values, face, previous_plane(face))

    def axial_own(values, courant):
        own, halo = flux(courant, values, next_plane(values))
        lower = jnp.where(first, pltpu.roll(halo, 1, 0), pltpu.roll(own, 1, 0))
        return values[0] - (own - lower)

    def radial_one(values, courant):
        above_cell = jnp.where(rim_cell, 0.0, pltpu.roll(values, lanes - 1, 1))
        outer = outer_radius * upwind(courant, values, above_cell)
        inner = jnp.where(axis_cell, 0.0, pltpu.roll(outer, 1, 1))
        return values - (outer - inner) * inverse

    def radial(values, courant):
        return tuple(radial_one(v, c) for v, c in zip(values, courant))

    def step(column, state, stage):
        v1_old, face_a_old, v3_old, face_b_old = state
        v1 = axial(load(0, column), load(1, column))
        face_a = v3 = face_b = None
        if stage >= 1:
            face_a = flux(load(2, column - 1), v1_old, v1)
        if stage >= 2:
            v2 = update(v1_old, face_a, face_a_old)
            v3 = radial(v2, load(3, column - 1))
        if stage >= 3:
            face_b = flux(load(2, column - 2), v3_old, v3)
        if stage >= 4:
            v4 = update(v3_old, face_b, face_b_old)
            store(column - 2, axial_own(v4, load(1, column - 2)))
        return v1, face_a, v3, face_b

    state = (None, None, None, None)
    for stage in range(6):
        state = step(LOWEST + stage, state, stage)
    stage = 6
    for start, stop, before in segments or ():
        before()
        state = lax.fori_loop(start, stop, lambda column, s: step(column, s, 6), state, unroll=4)
        stage = stop - LOWEST
    for stage in range(stage, count):
        state = step(LOWEST + stage, state, stage)


def fill_halos(halos, entries, source):
    for tile, field, plane, count, row in entries:
        rows = pl.ds((-count - LOWEST) * 8 + plane_slot(plane), count + COLS, stride=8)
        halos[field].at[tile][rows, :] = source[row : row + count + COLS, :]


def row_slice(column):
    return pl.ds(column * 8 if isinstance(column, int) else pl.multiple_of(column * 8, 8), 8)


def loaders(fields, left, halos, tiles):
    def load_own(field, column):
        if isinstance(column, int) and column < 0:
            parts = [part[row_slice(LEFT.index((field, column))), :] for part in left]
            return jnp.concatenate(parts, axis=1) if tiles > 1 else parts[0]
        return fields[field][row_slice(column), :]

    def load_halo(field, column):
        parts = [halos[field].at[tile][row_slice(column - LOWEST), :] for tile in range(tiles)]
        return jnp.concatenate(parts, axis=1) if tiles > 1 else parts[0]

    return load_own, load_halo


def near_kernel(*refs):
    fields, (below, above, left, crossing, out), halos, swept = refs[:4], refs[4:9], refs[9:13], refs[13]
    fill_halos(halos, NEAR_BELOW, below)
    fill_halos(halos, NEAR_ABOVE, above)

    def store(column, values):
        swept[row_slice(column + 2), :] = values

    sweep(COLS + 4, *loaders(fields, [left], halos, 1), store, 128)
    turned = swept[...].T
    out[pl.ds(0, R_AX, stride=4), :] = turned[:R_AX, :128]
    out[pl.ds(1, R_AX, stride=4), :] = turned[:R_AX, 128:]
    out[pl.ds(2, R_AX, stride=4), :] = crossing[:R_AX, :]
    out[pl.ds(3, R_AX, stride=4), :] = crossing[R_AX:, :]


def fill_far_halos(halos, near_below, near_above, below, above):
    for entries, source in ((NEAR_BELOW, near_below), (NEAR_ABOVE, near_above), (FAR_BELOW, below), (FAR_ABOVE, above)):
        fill_halos(halos, entries, source)


def far_first_kernel(*refs):
    sources, planes, left, out, halos = refs[:4], refs[4:8], refs[8:10], refs[10], refs[11:15]
    fields, semaphores = refs[15:19], refs[19]
    copies = copy_all([(f.at[pl.ds(0, 16), :], held) for f, held in zip(sources, fields)], semaphores)
    fill_far_halos(halos, *planes)
    for copy in copies:
        copy.wait()

    def store(column, values):
        out[row_slice(column + 2), :] = values

    sweep(6, *loaders(fields, left, halos, TILES), store, NR)


def far_kernel(*refs):
    sources, planes, left, (result, first_tile), halos = refs[:4], refs[4:8], refs[8:10], refs[10:12], refs[12:16]
    fields, (out, semaphores) = refs[16:20], refs[20:]
    arrive = [(0, 80), (80, 144), (144, 208), (208, 256)]
    leave = [(0, 64), (64, 128), (128, 192), (192, KEPT)]
    incoming = [
        copy_all([(f.at[pl.ds(a, b - a), :], held.at[pl.ds(a, b - a), :]) for f, held in zip(sources, fields)], semaphores, 4 * k)
        for k, (a, b) in enumerate(arrive)
    ]
    outgoing = []
    fill_far_halos(halos, *planes)

    def store(column, values):
        if not isinstance(column, int) or column >= 0:
            out[row_slice(column), :] = values
            first_tile[row_slice(column), :] = values[:, :128]

    def send(piece):
        a, b = leave[piece]
        pairs = [(out.at[pl.ds(a, b - a), :], result.at[pl.ds(a, b - a), :])]
        outgoing.extend(copy_all(pairs, semaphores, 16 + piece))

    def pause(piece):
        for copy in incoming[piece]:
            copy.wait()
        if piece:
            send(piece - 1)

    for copy in incoming[0]:
        copy.wait()
    segments = [(2, 10, lambda: None)] + [(8 * k + 2, min(8 * k + 10, 30), functools.partial(pause, k)) for k in (1, 2, 3)]
    sweep(COLS + 4, *loaders(fields, left, halos, TILES), store, NR, segments)
    send(3)
    for copy in outgoing:
        copy.wait()


def pieces(values, count):
    out = []
    for _ in range(count):
        piece = values.astype(BF16)
        out.append(piece)
        values = values - piece.astype(F32)
    return out


def mm(a, b, dims=((1,), (0,))):
    return lax.dot_general(a, b, (dims, ((), ())), preferred_element_type=F32)


def plic_volume(plane_code, strip_width):
    normal = lax.shift_right_logical(plane_code, 6).astype(F32)
    offset = lax.bitwise_and(plane_code, 63).astype(F32)
    plane_angle = math.pi / 16 + (normal + 0.5) * (3 * math.pi / 512)
    normal_along = jnp.cos(plane_angle)
    across = jnp.sin(plane_angle)
    plane_level = (offset + 0.5) * (normal_along + across) / 64.0
    strip_span = strip_width * normal_along

    def square(shift_value):
        positive = jnp.maximum(shift_value, 0.0)
        return positive * positive

    strip_area = (
        square(plane_level)
        - square(plane_level - strip_span)
        - square(plane_level - across)
        + square(plane_level - strip_span - across)
    ) / (2.0 * strip_span * across)
    return strip_width * strip_area


def crossing_kernel(*refs):
    (code, width, reader, landing), tables, (out, volume_out) = refs[:4], refs[4:11], refs[12:14]
    copies = copy_all(zip(tables, refs[14:21]), refs[21])
    iota = functools.partial(lax.broadcasted_iota, jnp.int32)
    volume = plic_volume(code[...], width[...])
    both = jnp.concatenate([reader[...].astype(F32), landing[...].astype(F32)], axis=0).astype(BF16)
    column_of_row = (iota((ROWS, COLS), 0) // 8 == iota((ROWS, COLS), 1)).astype(F32).astype(BF16)
    spread = mm(column_of_row, both, ((1,), (1,)))
    row16, lane16 = iota((ROWS, 16), 0), iota((ROWS, 16), 1)
    reader_rows = jnp.sum(jnp.where(lane16 == row16 % 8, spread, 0.0), axis=1, keepdims=True)
    landing_rows = jnp.sum(jnp.where(lane16 == row16 % 8 + 8, spread, 0.0), axis=1, keepdims=True)
    across = mm(both, column_of_row, ((1,), (1,)))
    reader_lanes = jnp.sum(
        jnp.where(iota((16, ROWS), 0) == iota((16, ROWS), 1) % 8, across, 0.0), axis=0, keepdims=True
    )
    same = (reader_rows == reader_lanes) & (iota((ROWS, ROWS), 1) < iota((ROWS, ROWS), 0))
    rank = jnp.sum(jnp.where(same, 1.0, 0.0), axis=1, keepdims=True)

    row, lane = iota((ROWS, 128), 0), iota((ROWS, 128), 1)
    wide = jnp.broadcast_to(volume[:, None, :], (COLS, PLANES, 128)).reshape(ROWS, 128)
    own = jnp.where(lane // 16 == row % 8, wide, 0.0)
    repeat = (iota((128, 128), 0) % 16 == iota((128, 128), 1) % 16).astype(F32).astype(BF16)
    rows_of_volume = sum(mm(piece, repeat) for piece in pieces(own, 3))
    volume_out[...] = rows_of_volume.T[:XR, :]
    chosen = (reader_lanes == iota((R_AX, ROWS), 0).astype(F32)).astype(F32).astype(BF16)
    slotted = jnp.where((lane // 16).astype(F32) == rank, rows_of_volume, 0.0)
    out[:R_AX, :] = sum(mm(chosen, piece) for piece in pieces(slotted, 3))
    target = landing_rows * 8.0 + (row % 8).astype(F32) + 1.0
    marked = jnp.where(lane.astype(F32) == rank, target, 0.0)
    out[R_AX:, :] = mm(chosen, marked.astype(BF16))
    for copy in copies:
        copy.wait()


def arrival_kernel(received, volume, out):
    values = received[pl.ds(2, R_AX, stride=4), :]
    targets = received[pl.ds(3, R_AX, stride=4), :]
    turned = values.T
    row = lax.broadcasted_iota(jnp.int32, (R_AX, ROWS), 1).astype(F32) + 1.0
    total = -volume[...]
    for slot in range(SLOTS):
        chosen = (targets[:, slot : slot + 1] == row).astype(F32).astype(BF16)
        for piece in pieces(turned[slot * XR : (slot + 1) * XR, :], 3):
            total += mm(piece, chosen)
    out[...] = total


def halves(table):
    high = table.astype(ml_dtypes.bfloat16)
    low = (table - high.astype(np.float64)).astype(ml_dtypes.bfloat16)
    return high, low


def filter_tables():
    outer, sector = np.arange(33)[:, None], np.arange(64)[None, :]
    phase = 2 * np.pi * (outer * sector % 64) / 64
    first = np.zeros((2 * KD, 64))
    first[:33], first[KD : KD + 33] = np.cos(phase), -np.sin(phase)
    weight = np.where((outer == 0) | (outer == 32), 1.0, 2.0) / 2048
    last = np.zeros((64, 2 * KD))
    last[:, :33], last[:, KD : KD + 33] = (weight * np.cos(phase)).T, (-weight * np.sin(phase)).T
    column, plane = np.arange(ROWS) // PLANES, np.arange(ROWS) % PLANES
    inner = 2 * np.pi * (column[:, None] * column[None, :] % 32) / 32
    same = plane[:, None] == plane[None, :]
    block = np.concatenate([np.where(same, np.cos(inner), 0.0), np.where(same, -np.sin(inner), 0.0)], axis=1)
    turn = 2 * np.pi * np.arange(KD)[:, None] * column[None, :] / 2048
    mode = np.arange(KD)[:, None] + 64 * column[None, :]
    shift = 2 * np.pi * (2 * mode % 2048) / 2048
    turns = [np.cos(turn), -np.sin(turn), np.cos(shift), np.sin(shift)]
    twiddle = np.concatenate(turns, axis=0).astype(np.float32)
    return (*halves(first), *halves(block), twiddle, *halves(last))


def dot3(a, b):
    (ah, al), (bh, bl) = a, b
    if ah.shape[1] % 128 == 0:
        return mm(jnp.concatenate([ah, al, ah], axis=1), jnp.concatenate([bh, bh, bl], axis=0))
    rows = ah.shape[0]
    both = mm(jnp.concatenate([ah, al], axis=0), bh)
    return both[:rows] + (both[rows:] + mm(ah, bl))


def filter_kernel(received, first_h, first_l, block_h, block_l, twiddle, last_h, last_l, out):
    sectors = jnp.concatenate(
        [received[pl.ds(0, R_AX, stride=4), :], received[pl.ds(1, R_AX, stride=4), :]], axis=1
    )
    outer = dot3((first_h[...], first_l[...]), pieces(sectors, 2))
    re, im = outer[:KD], outer[KD:]
    t_re, t_im, s_re, s_im = (twiddle[k * KD : (k + 1) * KD, :] for k in range(4))
    turned = jnp.concatenate([re * t_re - im * t_im, re * t_im + im * t_re], axis=0)
    block = (block_h[...], block_l[...])
    inner = dot3(pieces(turned, 2), block)
    re = inner[:KD, :ROWS] - inner[KD:, ROWS:]
    im = inner[:KD, ROWS:] + inner[KD:, :ROWS]
    re, im = re * s_re - im * s_im, re * s_im + im * s_re
    mode = lax.broadcasted_iota(jnp.int32, (KD, ROWS), 0) + 64 * (
        lax.broadcasted_iota(jnp.int32, (KD, ROWS), 1) // PLANES
    )
    folded = jnp.minimum(mode, 2048 - mode).astype(F32)
    cutoff = (lax.axis_index("az") + 1).astype(F32) * 2.0
    scaled = folded / cutoff
    damped = jnp.exp(-(scaled * scaled))
    back = dot3(pieces(jnp.concatenate([re * damped, im * damped], axis=0), 2), block)
    re = back[:KD, :ROWS] + back[KD:, ROWS:]
    im = back[KD:, :ROWS] - back[:KD, ROWS:]
    turned = jnp.concatenate([re * t_re + im * t_im, im * t_re - re * t_im], axis=0)
    result = dot3((last_h[...], last_l[...]), pieces(turned, 2))
    out[pl.ds(0, R_AX, stride=2), :] = result[:, :128]
    out[pl.ds(1, R_AX, stride=2), :] = result[:, 128:]


def final_kernel(received, delta, swept, last, _, result, out, semaphores):
    rest = (pl.ds(KEPT, ROWS - KEPT), pl.ds(128, NR - 128))
    copy = pltpu.make_async_copy(last.at[:, pl.ds(128, NR - 128)], result.at[rest], semaphores.at[1])
    copy.start()
    near = jnp.concatenate(
        [received[pl.ds(0, R_AX, stride=2), :], received[pl.ds(1, R_AX, stride=2), :]], axis=1
    )
    near = jnp.concatenate([near[:XR] + delta[...], near[XR:], jnp.zeros((R_AX, ROWS), F32)], axis=0)
    cycle = lax.broadcasted_iota(jnp.int32, (ROWS, 128), 1)
    first_tile = jnp.concatenate([swept[...], last[:, :128]], axis=0)
    out[...] = jnp.where(cycle < R_AX, near.T, first_tile)
    copy_out(out, result.at[:, pl.ds(0, 128)], semaphores.at[0])
    copy.wait()


VMEM, HBM = pltpu.VMEM, pltpu.HBM
DMA = pltpu.SemaphoreType.DMA


def call(kernel, inputs, outputs, scratch=(), cost=1.0, aliases=None):
    arrays, specs = [], []
    for given in inputs:
        array, space = given if isinstance(given, tuple) else (given, VMEM)
        arrays.append(pltpu.with_memory_space_constraint(array, HBM) if space is HBM else array)
        specs.append(pl.BlockSpec(memory_space=space))
    out_specs = [pl.BlockSpec(memory_space=getattr(o, "memory_space", VMEM)) for o in outputs]
    return pl.pallas_call(
        kernel,
        in_specs=specs,
        out_specs=out_specs,
        out_shape=list(outputs),
        scratch_shapes=list(scratch),
        input_output_aliases=aliases or {},
        cost_estimate=pl.CostEstimate(flops=int(cost * 1e6), bytes_accessed=int(cost * 3e6), transcendentals=0),
        compiler_params=pltpu.CompilerParams(vmem_limit_bytes=16 * 1024 * 1024),
    )(*arrays)


def free(*dims):
    return jax.ShapeDtypeStruct(dims, F32)


def local(
    fraction,
    courant_axial,
    courant_azimuth,
    courant_radial,
    plane_code,
    strip_width,
    tile_reader,
    landing_column,
):
    ax_count, az_count = lax.axis_size("ax"), lax.axis_size("az")
    higher_ax, higher_az = ([(i, (i + 1) % n) for i in range(n)] for n in (ax_count, az_count))
    lower_ax, lower_az = ([(j, i) for i, j in pairs] for pairs in (higher_ax, higher_az))
    fields = [(a.reshape(ROWS, NR), HBM) for a in (fraction, courant_axial, courant_azimuth, courant_radial)]

    (near_right,) = call(pack_columns, fields, [VMEM((len(LEFT) * 8, 128), F32)], [DMA((4,))])
    near_left = lax.ppermute(near_right, "az", higher_az)

    *near_tiles, far_right = call(
        bring_tiles,
        fields,
        [VMEM((ROWS, 128), F32)] * 4 + [VMEM((len(LEFT) * 8, NR - 128), F32)],
        [DMA((8,))],
    )
    far_left = lax.ppermute(far_right, "az", higher_az)
    near_up, near_down = call(
        pack_near_planes,
        [*near_tiles, near_left],
        [VMEM((NEAR_BELOW_ROWS, 128), F32), VMEM((NEAR_ABOVE_ROWS, 128), F32)],
    )
    tables = filter_tables()
    crossing, volume, *held_tables = call(
        crossing_kernel,
        [plane_code, strip_width, tile_reader.T, landing_column.T]
        + [(jnp.asarray(t), HBM) for t in tables]
        + [(near_up, pl.ANY)],
        [VMEM((2 * R_AX, 128), F32), VMEM((XR, ROWS), F32)] + [VMEM(t.shape, t.dtype) for t in tables],
        [DMA((len(tables),))],
    )
    near_below = lax.ppermute(near_up, "ax", higher_ax)
    near_above = lax.ppermute(near_down, "ax", lower_ax)
    far_up, far_down = call(
        pack_far_planes,
        [*fields, far_left],
        [VMEM((FAR_BELOW_ROWS, 128), F32), VMEM((FAR_ABOVE_ROWS, 128), F32)],
        [VMEM(((TILES - 1) * ROWS, 128), F32)] * 4 + [DMA((4 * (TILES - 1),))],
    )
    (send,) = call(
        near_kernel,
        [*near_tiles, near_below, near_above, near_left, crossing],
        [free(4 * R_AX, 128)],
        [VMEM((1, 36 * 8, 128), F32)] * 4 + [VMEM((ROWS, 128), F32)],
    )
    got = lax.all_to_all(send.reshape(R_AX, 4, 128), "az", 0, 0, tiled=True).reshape(4 * R_AX, 128)

    far_below = lax.ppermute(far_up, "ax", higher_ax)
    far_above = lax.ppermute(far_down, "ax", lower_ax)
    far_inputs = [*fields, near_below, near_above, far_below, far_above, near_left, far_left]
    far_halos = [VMEM((TILES, 36 * 8, 128), F32)] * 4
    (first_columns,) = call(
        far_first_kernel, far_inputs, [VMEM((16, NR), F32)], far_halos + [VMEM((16, NR), F32)] * 4 + [DMA((4,))]
    )
    last_columns = lax.ppermute(first_columns, "az", lower_az)
    swept, first_tile = call(
        far_kernel,
        far_inputs,
        [HBM((ROWS, NR), F32), VMEM((KEPT, 128), F32)],
        far_halos + [VMEM((ROWS, NR), F32)] * 4 + [VMEM((KEPT, NR), F32), DMA((20,))],
        cost=4.0,
    )

    (back,) = call(filter_kernel, [got, *held_tables], [free(2 * R_AX, 128)])
    returned = lax.all_to_all(back.reshape(R_AX, 2, 128), "az", 0, 0, tiled=True).reshape(2 * R_AX, 128)
    (delta,) = call(arrival_kernel, [got, volume], [VMEM((XR, ROWS), F32)])
    (out,) = call(
        final_kernel,
        [returned, delta, first_tile, last_columns, (swept, HBM)],
        [HBM((ROWS, NR), F32)],
        [VMEM((ROWS, 128), F32), DMA((2,))],
        aliases={4: 0},
    )
    return out.reshape(COLS, PLANES, NR)


def solution(mesh):
    return jax.shard_map(
        local,
        mesh=mesh,
        in_specs=(
            P("az", "ax", None),
            P("az", "ax", None),
            P("az", "ax", None),
            P("az", "ax", None),
            P("az", "ax"),
            P("az", "ax"),
            P("az", "ax"),
            P("az", "ax"),
        ),
        out_specs=P("az", "ax", None),
        check_vma=False,
    )
```
